32 devices in a mesh: lon: 16 (over z, y, core), lat: 2 (over x).
Axes of the slice: x: 2, y: 2, z: 4, core: 2. Of those that a mesh axis runs over, the one named last changes fastest.
Arguments:
- state: bfloat16 [90, 384, 128], P('lat', 'lon'), may hold values from -6 to 6
- land_sea: int32 [90, 384], P('lat', 'lon'), may hold values 0 or 1
- cotangent: bfloat16 [90, 384, 128], P('lat', 'lon'), may hold values from -6 to 6
- dw_kernel: bfloat16 [2, 7, 7, 128], replicated, may hold values from -0.875 to 0.875
- conv_bias: float32 [2, 128], replicated, may hold values from -3 to 3
- norm_gain: float32 [2, 128], replicated, may hold values from 0.1 to 1.9
- norm_bias: float32 [2, 128], replicated, may hold values from -3 to 3
- weight_in: bfloat16 [2, 128, 512], replicated, may hold values from -0.5 to 0.5
- bias_in: float32 [2, 512], replicated, may hold values from -3 to 3
- weight_out: bfloat16 [2, 512, 128], replicated, may hold values from -0.25 to 0.25
- bias_out: float32 [2, 128], replicated, may hold values from -3 to 3
- layer_scale: float32 [2, 128], replicated, may hold values from 0.3 to 1
Outputs:
- output: bfloat16 [90, 384, 128], P('lat', 'lon')
- grad_state: bfloat16 [90, 384, 128], P('lat', 'lon')
- grad_dw_kernel: float32 [2, 7, 7, 128], replicated
- grad_conv_bias: float32 [2, 128], replicated
- grad_norm_gain: float32 [2, 128], replicated
- grad_norm_bias: float32 [2, 128], replicated
- grad_weight_in: float32 [2, 128, 512], replicated
- grad_bias_in: float32 [2, 512], replicated
- grad_weight_out: float32 [2, 512, 128], replicated
- grad_bias_out: float32 [2, 128], replicated
- grad_layer_scale: float32 [2, 128], replicated
The draws below stay inside these ranges and needn't reach their ends.
All inputs are finite; a program needn't handle non-finite values. No bound on the sum of `land_sea` on one device may be relied on, other than what follows from the above.
Results may differ from the reference program's by a relative error of at most 0.02.
Values may be sent and summed in bfloat16 or wider, within the bound.
No kernel may reach another device: no remote copies, remote signals or barrier semaphores. Data moves between devices by JAX's collectives and lax.ppermute only.
A program may use at most 64 MiB of HBM per device.

```python
import math
import jax
import jax.numpy as jnp
from jax import lax

C = 128
F = 512
KSIZE = 7
BLOCKS = 2
LAT_DEV = 45
NLAT = 90
NLON = 384


def plant(entries, own_key, smallest, top_value):
    longest = entries.shape.index(max(entries.shape))
    spots = []
    for shift in (0, 1):
        where = [jax.random.randint(jax.random.fold_in(own_key, axis), (), 0, length) for axis, length in enumerate(entries.shape)]
        where[longest] = (where[longest] + shift) % entries.shape[longest]
        spots.append(tuple(where))
    return entries.at[spots[0]].set(smallest).at[spots[1]].set(top_value)


def block_scale(rng, extent, cuts, smallest, largest):
    def one(dim, shards_of):
        steps = jax.random.uniform(jax.random.fold_in(jax.random.fold_in(rng, 6), dim), (shards_of,), jnp.float32, smallest / len(cuts), largest / len(cuts))
        return jnp.repeat(jnp.exp(steps), extent[dim] // shards_of).reshape((-1,) + (1,) * (len(extent) - dim - 1))

    level = one(*cuts[0])
    for cut in cuts[1:]:
        level = level * one(*cut)
    return level


def noise(stream_key, shape, deviation, most, split=(), held_as=jnp.bfloat16):
    array = deviation * jax.random.normal(stream_key, shape, jnp.float32)
    if split:
        array = array * block_scale(stream_key, shape, split, -0.22, 0.18)
    return jnp.clip(array, -most, most).astype(held_as)


def setup_inputs(seed: int = 0) -> dict:
    key_of = jax.random.split(jax.random.key(seed), 13)
    return {
        "state": noise(key_of[0], (NLAT, NLON, C), 1.0, 6.0, ((0, 2), (1, 16))),
        "land_sea": plant((jax.random.randint(key_of[1], (NLAT, NLON), 0, 10) < 7).astype(jnp.int32), jax.random.fold_in(key_of[1], 1), 0, 1),
        "cotangent": noise(key_of[2], (NLAT, NLON, C), 1.0, 6.0, ((0, 2), (1, 16))),
        "dw_kernel": noise(key_of[3], (BLOCKS, KSIZE, KSIZE, C), (KSIZE * KSIZE) ** -0.5, 0.875),
        "conv_bias": noise(key_of[4], (BLOCKS, C), 0.5, 3.0, (), jnp.float32),
        "norm_gain": jnp.clip(1.0 + 0.18 * jax.random.normal(key_of[5], (BLOCKS, C), jnp.float32), 0.1, 1.9),
        "norm_bias": noise(key_of[6], (BLOCKS, C), 0.5, 3.0, (), jnp.float32),
        "weight_in": noise(key_of[7], (BLOCKS, C, F), C ** -0.5, 0.5),
        "bias_in": noise(key_of[8], (BLOCKS, F), 0.5, 3.0, (), jnp.float32),
        "weight_out": noise(key_of[9], (BLOCKS, F, C), F ** -0.5, 0.25),
        "bias_out": noise(key_of[10], (BLOCKS, C), 0.5, 3.0, (), jnp.float32),
        "layer_scale": jnp.clip(jnp.exp(jax.random.uniform(key_of[11], (BLOCKS, C), jnp.float32, math.log(0.3), math.log(1.0))), 0.3, 1.0),
    }


EPS_NORM = 1e-06
INV_ROOT_TWO = 0.7071067811865476
INV_ROOT_TWO_PI = 0.3989422804014327

def depthwise(window, kernel, height, breadth):
    summed = jnp.zeros((height, breadth, window.shape[2]), jnp.float32)
    for tap_row in range(KSIZE):
        for tap_col in range(KSIZE):
            piece = window[tap_row:tap_row + height, tap_col:tap_col + breadth].astype(jnp.float32)
            summed = summed + piece * kernel[tap_row, tap_col].astype(jnp.float32)
    return summed

def block_forward(window, land_rows, params):
    kernel, conv_bias, norm_gain, norm_bias, weight_in, bias_in, weight_out, bias_out, layer_scale = params
    margin = KSIZE // 2
    height = window.shape[0] - 2 * margin
    breadth = window.shape[1] - 2 * margin
    channels = window.shape[2]
    cell_count = height * breadth
    mixed_sum = depthwise(window, kernel, height, breadth) + conv_bias
    center = mixed_sum - lax.optimization_barrier(jnp.mean(mixed_sum, axis=-1, keepdims=True))
    inverse = lax.rsqrt(lax.optimization_barrier(jnp.mean(center * center, axis=-1, keepdims=True)) + EPS_NORM)
    normed = (center * inverse).reshape(cell_count, channels)
    lifted = (normed * norm_gain + norm_bias).astype(jnp.bfloat16)
    hidden = jnp.dot(lifted, weight_in, preferred_element_type=jnp.float32) + bias_in
    active = jax.nn.gelu(hidden, approximate=False).astype(jnp.bfloat16)
    branch = jnp.dot(active, weight_out, preferred_element_type=jnp.float32) + bias_out
    interior = window[margin:margin + height, margin:margin + breadth].astype(jnp.float32).reshape(cell_count, channels)
    ocean_mask = land_rows.reshape(cell_count, 1).astype(jnp.float32)
    result = ((interior + layer_scale * branch) * ocean_mask).astype(jnp.bfloat16).reshape(height, breadth, channels)
    return (result, (normed, inverse.reshape(cell_count, 1), lifted, hidden, active, branch))

def block_backward(window, land_rows, incoming, params, stored):
    kernel, conv_bias, norm_gain, norm_bias, weight_in, bias_in, weight_out, bias_out, layer_scale = params
    normed, inverse, lifted, hidden, active, branch = stored
    margin = KSIZE // 2
    height = window.shape[0] - 2 * margin
    breadth = window.shape[1] - 2 * margin
    channels = window.shape[2]
    cell_count = height * breadth
    ocean_mask = land_rows.reshape(cell_count, 1).astype(jnp.float32)
    masked = incoming.reshape(cell_count, channels).astype(jnp.float32) * ocean_mask
    grad_branch = (masked * layer_scale).astype(jnp.bfloat16)
    contract_rows = (((0,), (0,)), ((), ()))
    contract_cols = (((1,), (1,)), ((), ()))
    grad_scale = lax.optimization_barrier(jnp.sum(masked * branch, axis=0))
    grad_bias_out = lax.optimization_barrier(jnp.sum(grad_branch.astype(jnp.float32), axis=0))
    grad_weight_out = lax.dot_general(active, grad_branch, contract_rows, preferred_element_type=jnp.float32)
    grad_active = lax.dot_general(grad_branch, weight_out, contract_cols, preferred_element_type=jnp.float32)
    cumulative = 0.5 * (1.0 + lax.erf(hidden * INV_ROOT_TWO))
    density = jnp.exp(-0.5 * hidden * hidden) * INV_ROOT_TWO_PI
    grad_hidden = (grad_active * (cumulative + hidden * density)).astype(jnp.bfloat16)
    grad_bias_in = lax.optimization_barrier(jnp.sum(grad_hidden.astype(jnp.float32), axis=0))
    grad_weight_in = lax.dot_general(lifted, grad_hidden, contract_rows, preferred_element_type=jnp.float32)
    grad_lifted = lax.dot_general(grad_hidden, weight_in, contract_cols, preferred_element_type=jnp.float32)
    grad_gain = lax.optimization_barrier(jnp.sum(grad_lifted * normed, axis=0))
    grad_shift = lax.optimization_barrier(jnp.sum(grad_lifted, axis=0))
    scaled = grad_lifted * norm_gain
    grad_mixed = inverse * (scaled - lax.optimization_barrier(jnp.mean(scaled, axis=-1, keepdims=True)) - normed * lax.optimization_barrier(jnp.mean(scaled * normed, axis=-1, keepdims=True)))
    grad_mixed = grad_mixed.astype(jnp.bfloat16).reshape(height, breadth, channels)
    spread = grad_mixed.astype(jnp.float32)
    grad_conv_bias = lax.optimization_barrier(jnp.sum(spread, axis=(0, 1)))
    tap_sums = []
    for tap_row in range(KSIZE):
        for tap_col in range(KSIZE):
            piece = window[tap_row:tap_row + height, tap_col:tap_col + breadth].astype(jnp.float32)
            tap_sums.append(lax.optimization_barrier(jnp.sum(spread * piece, axis=(0, 1))))
    grad_kernel = jnp.stack(tap_sums).reshape(KSIZE, KSIZE, channels)
    gradients = (grad_kernel, grad_conv_bias, grad_gain, grad_shift, grad_weight_in, grad_bias_in, grad_weight_out, grad_bias_out, grad_scale)
    return (grad_mixed, masked.reshape(height, breadth, channels), gradients)

def adjoint(padded, masked, kernel):
    margin = KSIZE // 2
    height = masked.shape[0]
    breadth = masked.shape[1]
    summed = masked
    for tap_row in range(KSIZE):
        for tap_col in range(KSIZE):
            first_row = 2 * margin - tap_row
            first_col = 2 * margin - tap_col
            piece = padded[first_row:first_row + height, first_col:first_col + breadth].astype(jnp.float32)
            summed = summed + piece * kernel[tap_row, tap_col].astype(jnp.float32)
    return summed.astype(jnp.bfloat16)

def pad_grid(grid_field):
    margin = KSIZE // 2
    columns = grid_field.shape[1]
    wrapped = jnp.concatenate([grid_field[:, columns - margin:], grid_field, grid_field[:, :margin]], axis=1)
    return jnp.pad(wrapped, ((margin, margin), (0, 0), (0, 0)))

def rows_forward(padded, land_sea, params):
    row_blocks = land_sea.shape[0] // LAT_DEV
    row_span = LAT_DEV + KSIZE - 1

    def one_block(position):
        row_start = position * LAT_DEV
        window = lax.dynamic_slice_in_dim(padded, row_start, row_span, 0)
        land_rows = lax.dynamic_slice_in_dim(land_sea, row_start, LAT_DEV, 0)
        return block_forward(window, land_rows, params)[0]
    pieces = lax.map(one_block, jnp.arange(row_blocks, dtype=jnp.int32))
    return pieces.reshape(land_sea.shape[0], land_sea.shape[1], pieces.shape[3])

def rows_backward(padded, land_sea, incoming, params):
    row_blocks = land_sea.shape[0] // LAT_DEV
    row_span = LAT_DEV + KSIZE - 1
    empty_sums = tuple((jnp.zeros(member.shape, jnp.float32) for member in params))

    def advance(running, position):
        row_start = position * LAT_DEV
        window = lax.dynamic_slice_in_dim(padded, row_start, row_span, 0)
        land_rows = lax.dynamic_slice_in_dim(land_sea, row_start, LAT_DEV, 0)
        grad_rows = lax.dynamic_slice_in_dim(incoming, row_start, LAT_DEV, 0)
        stored = block_forward(window, land_rows, params)[1]
        grad_mixed, masked, gradients = block_backward(window, land_rows, grad_rows, params, stored)
        return (tuple((left + right for left, right in zip(running, gradients))), (grad_mixed, masked))
    totals, (mixed_rows, masked_rows) = lax.scan(advance, empty_sums, jnp.arange(row_blocks, dtype=jnp.int32))
    shape_out = (land_sea.shape[0], land_sea.shape[1], incoming.shape[2])
    return (mixed_rows.reshape(shape_out), masked_rows.reshape(shape_out), totals)

def reference(state, land_sea, cotangent, dw_kernel, conv_bias, norm_gain, norm_bias, weight_in, bias_in, weight_out, bias_out, layer_scale):
    stacked = (dw_kernel, conv_bias, norm_gain, norm_bias, weight_in, bias_in, weight_out, bias_out, layer_scale)
    current = state
    padded_inputs = []
    for layer_index in range(BLOCKS):
        params = tuple((member[layer_index] for member in stacked))
        padded = pad_grid(current)
        padded_inputs.append(padded)
        current = rows_forward(padded, land_sea, params)
    incoming = cotangent
    per_layer = [None] * BLOCKS
    for layer_index in reversed(range(BLOCKS)):
        params = tuple((member[layer_index] for member in stacked))
        grad_mixed, masked, gradients = rows_backward(padded_inputs[layer_index], land_sea, incoming, params)
        incoming = adjoint(pad_grid(grad_mixed), masked, params[0])
        per_layer[layer_index] = gradients
    grad_norm = 1.0 / math.sqrt(NLAT * NLON)
    summed = [jnp.stack([per_layer[layer_index][member] for layer_index in range(BLOCKS)]) * grad_norm for member in range(9)]
    return (current, incoming, summed[0], summed[1], summed[2], summed[3], summed[4], summed[5], summed[6], summed[7], summed[8])
```

```python
import functools
import math

import jax
import jax.numpy as jnp
from jax import lax
from jax.experimental import pallas as pl
from jax.experimental.pallas import tpu as pltpu
from jax.sharding import PartitionSpec as P

KSIZE = 7
MARGIN = KSIZE // 2
TAPS = KSIZE * KSIZE
BLOCKS = 2
EPS_NORM = 1e-06
INV_ROOT_TWO = 0.7071067811865476
INV_ROOT_TWO_PI = 0.3989422804014327
LAND = 1024.0
LAND_BOUND = 512.0
F32 = jnp.float32
BF16 = jnp.bfloat16
STEP = 3
STATE_AT = 11
FIELD_AT = 8
INNER_AT = 3
WIDE = 3 * MARGIN
NARROW = 2 * MARGIN


def round_up(size, unit):
    return (size + unit - 1) // unit * unit


def conv_rows(source, base, first, count, width, kernel_ref, flip):
    sums = [None] * count
    for tap_col in range(KSIZE):
        taps = []
        for tap_row in range(KSIZE):
            index = tap_row * KSIZE + tap_col
            taps.append(kernel_ref[pl.ds(TAPS - 1 - index if flip else index, 1), :])
        for row in range(count + KSIZE - 1):
            piece = source[base + row, pl.ds(first + tap_col, width), :]
            for tap_row in range(KSIZE):
                out = row - tap_row
                if 0 <= out < count:
                    term = piece * taps[tap_row]
                    sums[out] = term if sums[out] is None else sums[out] + term
    return jnp.concatenate(sums, axis=0)


def normal_parts(hidden):
    cumulative = 0.5 + 0.5 * lax.erf(hidden * INV_ROOT_TWO)
    return cumulative, jnp.exp(-0.5 * hidden * hidden)


def fold(values):
    return jnp.sum(values.reshape(values.shape[0] // 8, 8, values.shape[1]), axis=0)


def normalise(mixed):
    center = mixed - jnp.mean(mixed, axis=-1, keepdims=True)
    inverse = lax.rsqrt(jnp.mean(center * center, axis=-1, keepdims=True) + EPS_NORM)
    return center * inverse, inverse


def normalise_back(grad, normed, inverse):
    return inverse * (
        grad
        - jnp.mean(grad, axis=-1, keepdims=True)
        - normed * jnp.mean(grad * normed, axis=-1, keepdims=True)
    )


def rows_of(ref, base, first, count, width):
    return jnp.concatenate(
        [ref[base + row, pl.ds(first, width), :] for row in range(count)], axis=0
    )


CONTRACT_COLS = (((1,), (1,)), ((), ()))
CONTRACT_ROWS = (((0,), (0,)), ((), ()))


def dot(left, right):
    return jnp.dot(left, right, preferred_element_type=F32)


def dot_cols(left, right):
    return lax.dot_general(left, right, CONTRACT_COLS, preferred_element_type=F32)


def dot_rows(left, right):
    return lax.dot_general(left, right, CONTRACT_ROWS, preferred_element_type=F32)


def tap_sums(grad_ref, grad_row, grad_col, field_ref, field_row, field_col, height, width, out):
    for cols in ((0, 1), (2, 3), (4, 5), (6,)):

        def advance(row, sums):
            sums = list(sums)
            grad = grad_ref[grad_row + row, pl.ds(grad_col, width), :]
            for tap_row in range(KSIZE):
                for place, tap_col in enumerate(cols):
                    piece = field_ref[
                        field_row + row + tap_row, pl.ds(field_col + tap_col, width), :
                    ]
                    index = place * KSIZE + tap_row
                    sums[index] = sums[index] + fold(grad * piece)
            return tuple(sums)

        zeros = tuple(jnp.zeros((8, grad_ref.shape[2]), F32) for _ in range(KSIZE * len(cols)))
        sums = lax.fori_loop(0, height, advance, zeros)
        for place, tap_col in enumerate(cols):
            for tap_row in range(KSIZE):
                total = jnp.sum(sums[place * KSIZE + tap_row], axis=0, keepdims=True)
                out[pl.ds(tap_row * KSIZE + tap_col, 1), :] = total


def tile_kernel(
    sizes,
    starts,
    state_in,
    coded_in,
    dw_in,
    conv_bias,
    norm_gain,
    norm_bias,
    weight_in,
    bias_in,
    weight_out,
    bias_out,
    layer_scale,
    output,
    mixed_out,
    masked_out,
    grads_out,
    state,
    coded,
    kernels,
    field,
    inner,
    result,
    normed_own,
    inverse_own,
    branch_own,
    slope_own,
    active_own,
    hidden_own,
    lifted_own,
    branch_grad_own,
    mixed_own,
    active_all,
    hidden_all,
    lifted_all,
    branch_grad_all,
    sums,
    hidden_sums,
    taps,
):
    height, breadth, first_rows, second_rows, window_rows = sizes
    channels = state.shape[2]
    own_start = starts[0]
    second_start = starts[1]
    first_start = starts[2]
    first_width = field.shape[1]
    second_width = inner.shape[1]
    pad = MARGIN

    for ref in (state, coded, field, inner):
        edge = jnp.zeros((pad,) + ref.shape[1:], F32)
        ref[pl.ds(0, pad)] = edge
        ref[pl.ds(pad + window_rows, pad)] = edge
    state[pl.ds(pad, window_rows)] = state_in[...].astype(F32)
    coded[pl.ds(pad, window_rows)] = coded_in[...].astype(F32)
    kernels[...] = dw_in[...].astype(F32)
    sums[...] = jnp.zeros_like(sums)
    hidden_sums[...] = jnp.zeros_like(hidden_sums)

    def param(ref, layer):
        return ref[pl.ds(layer, 1), :]

    def forward_first(step, carry):
        row = first_start + step * STEP
        cells = STEP * first_width
        mixed = conv_rows(state, row, 0, STEP, first_width, kernels.at[0], False)
        normed, inverse = normalise(mixed + param(conv_bias, 0))
        lifted = (normed * param(norm_gain, 0) + param(norm_bias, 0)).astype(BF16)
        hidden = dot(lifted, weight_in[0]) + param(bias_in, 0)
        cumulative, bell = normal_parts(hidden)
        active = hidden * cumulative
        branch = dot(active.astype(BF16), weight_out[0]) + param(bias_out, 0)
        center = rows_of(state, row + pad, MARGIN, STEP, first_width)
        mark = rows_of(coded, row + pad, 0, STEP, first_width)
        value = jnp.where(mark < LAND_BOUND, center + param(layer_scale, 0) * branch, 0.0)
        value = value.reshape(STEP, first_width, channels)

        for index in range(STEP):
            field[row + pad + index] = value[index]

        def own(values):
            shape = (STEP, first_width, values.shape[1])
            return values.reshape(shape)[:, FIELD_AT : FIELD_AT + breadth]

        slope = own(cumulative) + own(hidden) * (own(bell) * INV_ROOT_TWO_PI)
        spots = pl.ds(row, STEP)
        slope_own[spots] = slope
        active_own[spots] = own(active).astype(BF16)
        normed_own[spots] = own(normed)
        inverse_own[spots] = own(jnp.broadcast_to(inverse, normed.shape))
        branch_own[spots] = own(branch)
        lifted_own[spots] = own(normed * param(norm_gain, 0) + param(norm_bias, 0)).astype(BF16)
        return carry

    lax.fori_loop(0, first_rows // STEP, forward_first, 0)

    def both_second(step, carry):
        row = second_start + step * STEP
        cells = STEP * second_width
        shift = FIELD_AT - INNER_AT
        mixed = conv_rows(
            field, row, shift - MARGIN, STEP, second_width, kernels.at[1], False
        )
        normed, inverse = normalise(mixed + param(conv_bias, 1))
        lifted = normed * param(norm_gain, 1) + param(norm_bias, 1)
        hidden = dot(lifted.astype(BF16), weight_in[1]) + param(bias_in, 1)
        cumulative, bell = normal_parts(hidden)
        active = (hidden * cumulative).astype(BF16)
        branch = dot(active, weight_out[1]) + param(bias_out, 1)
        center = rows_of(field, row + pad, shift, STEP, second_width)
        mark = rows_of(coded, row + pad, shift, STEP, second_width)
        ocean = mark < LAND_BOUND
        value = jnp.where(ocean, center + param(layer_scale, 1) * branch, 0.0)
        value = value.reshape(STEP, second_width, channels)
        masked = jnp.where(ocean, mark, 0.0)
        grad_branch = (masked * param(layer_scale, 1)).astype(BF16)
        grad_active = dot_cols(grad_branch, weight_out[1])
        slope = cumulative + hidden * (bell * INV_ROOT_TWO_PI)
        grad_hidden = (grad_active * slope).astype(BF16)
        grad_lifted = dot_cols(grad_hidden, weight_in[1])
        grad_mixed = normalise_back(grad_lifted * param(norm_gain, 1), normed, inverse)
        grad_mixed = grad_mixed.reshape(STEP, second_width, channels)
        for index in range(STEP):
            result[row + index] = value[index]
            inner[row + pad + index] = grad_mixed[index]

        shape = (STEP, second_width, channels)
        row_of = lax.broadcasted_iota(jnp.int32, shape, 0) + (row - own_start)
        col_of = lax.broadcasted_iota(jnp.int32, shape, 1) - INNER_AT
        inside = (row_of >= 0) & (row_of < height) & (col_of >= 0) & (col_of < breadth)
        inside = jnp.where(inside, 1.0, 0.0).astype(F32).reshape(cells, channels)
        own_lifted = grad_lifted * inside
        own_branch = grad_branch.astype(F32) * inside
        sums[1, 0] += fold(masked * branch * inside)
        sums[1, 1] += fold(own_branch)
        sums[1, 2] += fold(own_lifted * normed)
        sums[1, 3] += fold(own_lifted)
        wide = jnp.concatenate([inside] * (hidden.shape[1] // channels), axis=1)
        hidden_sums[1] += fold(grad_hidden.astype(F32) * wide)
        spots = pl.ds(pl.multiple_of(step * cells, cells), cells)
        active_all[spots] = active
        hidden_all[spots] = grad_hidden
        lifted_all[spots] = (lifted * inside).astype(BF16)
        branch_grad_all[spots] = own_branch.astype(BF16)
        return carry

    lax.fori_loop(0, second_rows // STEP, both_second, 0)

    def backward_first(step, carry):
        row = own_start + step * STEP
        cells = STEP * breadth
        mark = rows_of(coded, row + pad, FIELD_AT, STEP, breadth)
        ocean = mark < LAND_BOUND
        masked_next = jnp.where(ocean, mark, 0.0)
        spread = conv_rows(inner, row, 0, STEP, breadth, kernels.at[1], True)
        masked = jnp.where(ocean, masked_next + spread, 0.0)
        grad_branch = (masked * param(layer_scale, 0)).astype(BF16)
        grad_active = dot_cols(grad_branch, weight_out[0])
        slope = slope_own[pl.ds(row, STEP)].reshape(cells, grad_active.shape[1])
        grad_hidden = (grad_active * slope).astype(BF16)
        grad_lifted = dot_cols(grad_hidden, weight_in[0])
        normed = normed_own[pl.ds(row, STEP)].reshape(cells, channels)
        inverse = inverse_own[pl.ds(row, STEP)].reshape(cells, channels)
        grad_mixed = normalise_back(grad_lifted * param(norm_gain, 0), normed, inverse)
        branch = branch_own[pl.ds(row, STEP)].reshape(cells, channels)
        sums[0, 0] += fold(masked * branch)
        sums[0, 1] += fold(grad_branch.astype(F32))
        sums[0, 2] += fold(grad_lifted * normed)
        sums[0, 3] += fold(grad_lifted)
        sums[0, 4] += fold(grad_mixed)
        hidden_sums[0] += fold(grad_hidden.astype(F32))
        inner_rows = rows_of(inner, row + pad, INNER_AT, STEP, breadth)
        sums[1, 4] += fold(inner_rows)
        tile = pl.ds(step * STEP, STEP)
        shape = (STEP, breadth, channels)
        grad_mixed = grad_mixed.reshape(shape)
        mixed_own[tile] = grad_mixed
        mixed_out[tile] = grad_mixed.astype(BF16)
        masked_out[tile] = masked.reshape(shape).astype(BF16)
        hidden_own[tile] = grad_hidden.reshape(STEP, breadth, grad_hidden.shape[1])
        branch_grad_own[tile] = grad_branch.reshape(shape)
        value = rows_of(result, row, INNER_AT, STEP, breadth)
        output[tile] = value.reshape(shape).astype(BF16)
        return carry

    lax.fori_loop(0, height // STEP, backward_first, 0)

    hidden_units = weight_in.shape[2]
    groups = hidden_units // channels
    tile = pl.ds(own_start, height)
    cells = height * breadth

    def flat(ref, spots):
        return ref[spots].reshape(cells, ref.shape[2])

    operands = (
        (
            flat(lifted_own, tile),
            flat(hidden_own, pl.ds(0, height)),
            flat(active_own, tile),
            flat(branch_grad_own, pl.ds(0, height)),
        ),
        (lifted_all[...], hidden_all[...], active_all[...], branch_grad_all[...]),
    )
    for layer, (lifted, grad_hidden, active, grad_branch) in enumerate(operands):
        at = layer * 2 * hidden_units
        grad_in = dot_rows(lifted, grad_hidden)
        for group in range(groups):
            grads_out[pl.ds(at + group * channels, channels), :] = grad_in[
                :, group * channels : (group + 1) * channels
            ].astype(BF16)
        grad_out = dot_rows(grad_branch, active)
        for group in range(groups):
            grads_out[pl.ds(at + hidden_units + group * channels, channels), :] = grad_out[
                :, group * channels : (group + 1) * channels
            ].T.astype(BF16)

    at = BLOCKS * 2 * hidden_units
    tail = grads_out.shape[0] - at
    taps[...] = jnp.zeros_like(taps)
    for layer in range(BLOCKS):
        base = layer * (TAPS + 5 + groups)
        if layer:
            tap_sums(
                inner,
                own_start + pad,
                INNER_AT,
                field,
                own_start,
                FIELD_AT - MARGIN,
                height,
                breadth,
                taps.at[pl.ds(base, TAPS)],
            )
        else:
            tap_sums(
                mixed_own,
                0,
                0,
                state,
                own_start,
                STATE_AT - MARGIN,
                height,
                breadth,
                taps.at[pl.ds(base, TAPS)],
            )
        for member in range(5):
            taps[pl.ds(base + TAPS + member, 1), :] = jnp.sum(
                sums[layer, member], axis=0, keepdims=True
            )
        hidden_total = jnp.sum(hidden_sums[layer], axis=0, keepdims=True)
        for group in range(groups):
            taps[pl.ds(base + TAPS + 5 + group, 1), :] = hidden_total[
                :, group * channels : (group + 1) * channels
            ]
    grads_out[pl.ds(at, tail), :] = taps[...].astype(BF16)


def state_kernel(window, masked, dw_in, out, wide, kernels):
    height, breadth, channels = masked.shape
    wide[...] = window[...].astype(F32)
    kernels[...] = dw_in[...].astype(F32)

    def advance(step, carry):
        row = step * STEP
        spread = conv_rows(wide, row, 0, STEP, breadth, kernels, True)
        tile = pl.ds(row, STEP)
        shape = (STEP, breadth, channels)
        out[tile] = (masked[tile].astype(F32) + spread.reshape(shape)).astype(BF16)
        return carry

    lax.fori_loop(0, height // STEP, advance, 0)


class Links:
    def __init__(self, mesh):
        self.lon = mesh.shape["lon"]
        self.lat = mesh.shape["lat"]
        self.axes = ("lon", "lat")

    def shift_lon(self, values, by):
        pairs = [(place, (place + by) % self.lon) for place in range(self.lon)]
        return lax.ppermute(values, "lon", pairs)

    def shift_lat(self, values, by):
        pairs = [
            (place, place + by) for place in range(self.lat) if 0 <= place + by < self.lat
        ]
        return lax.ppermute(values, "lat", pairs)

    def swap(self, values, lon_bits, lat_bits):
        pairs = []
        for lon in range(self.lon):
            for lat in range(self.lat):
                there = (lon ^ lon_bits) * self.lat + (lat ^ lat_bits)
                pairs.append((lon * self.lat + lat, there))
        return lax.ppermute(values, self.axes, pairs)

    def extend_lat(self, field, width, outside):
        place = lax.axis_index("lat")
        if self.lat == 2:
            mine = jnp.where(place == 0, field[-width:], field[:width])
            other = lax.ppermute(mine, "lat", [(0, 1), (1, 0)])
            below = jnp.concatenate([field, other], axis=0)
            above = jnp.concatenate([other, field], axis=0)
            return jnp.where(place == 0, below, above)
        before = self.shift_lat(field[-width:], 1)
        after = self.shift_lat(field[:width], -1)
        before = jnp.where(place == 0, outside, before)
        after = jnp.where(place == self.lat - 1, outside, after)
        return jnp.concatenate([before, field, after], axis=0)

    def sum_all(self, rows):
        lon = lax.axis_index("lon")
        lat = lax.axis_index("lat")
        bits = [(1 << bit, 0) for bit in range(self.lon.bit_length() - 1)]
        bits = bits[:1] + [(0, 1 << bit) for bit in range(self.lat.bit_length() - 1)] + bits[1:]

        def code(group):
            total = jnp.int32(0)
            for index, (lon_bit, lat_bit) in enumerate(group):
                held = (lon // lon_bit) % 2 if lon_bit else (lat // lat_bit) % 2
                total = total + held * (1 << index)
            return total

        def merged(group, choice):
            lon_bits = sum(bit[0] for index, bit in enumerate(group) if choice >> index & 1)
            lat_bits = sum(bit[1] for index, bit in enumerate(group) if choice >> index & 1)
            return lon_bits, lat_bits

        def scatter(values, group):
            count = 1 << len(group)
            pieces = values.reshape(count, -1, values.shape[1])
            here = code(group)
            total = lax.dynamic_index_in_dim(pieces, here, 0, False).astype(F32)
            for choice in range(1, count):
                sent = lax.dynamic_index_in_dim(pieces, here ^ choice, 0, False)
                total = total + self.swap(sent, *merged(group, choice)).astype(F32)
            return total.astype(BF16)

        def exchange(values, group):
            total = values.astype(F32)
            for choice in range(1, 1 << len(group)):
                total = total + self.swap(values, *merged(group, choice)).astype(F32)
            return total.astype(BF16)

        def gather(values, group):
            count = 1 << len(group)
            pieces = [values]
            for choice in range(1, count):
                pieces.append(self.swap(values, *merged(group, choice)))
            stack = jnp.stack(pieces)
            here = code(group)
            ordered = [
                lax.dynamic_index_in_dim(stack, here ^ place, 0, False) for place in range(count)
            ]
            return jnp.concatenate(ordered, axis=0)

        pair, quad, rest = bits[:1], bits[1:3], bits[3:]
        values = scatter(scatter(rows, pair), quad)
        while rest:
            values = exchange(values, rest[:2])
            rest = rest[2:]
        return gather(gather(values, quad), pair)


def on_device(links, state, land_sea, cotangent, *params):
    dw_kernel, weight_in = params[0], params[4]
    height, breadth, channels = state.shape
    hidden_units = weight_in.shape[2]
    groups = hidden_units // channels
    grad_norm = 1.0 / math.sqrt(links.lat * height * links.lon * breadth)
    lat = lax.axis_index("lat")
    sides = 1 if links.lat == 2 else 2
    window_rows = height + sides * WIDE
    first_rows = height + sides * NARROW
    second_rows = height + sides * MARGIN

    def start(margin):
        skipped = WIDE - margin
        return lat * skipped if sides == 1 else jnp.int32(skipped)

    starts = jnp.stack([start(0), start(MARGIN), start(NARROW)]).astype(jnp.int32)

    ocean = (land_sea != 0)[:, :, None]
    coded = jnp.where(ocean, cotangent, jnp.asarray(LAND, BF16))
    packed = jnp.concatenate([state, coded], axis=1)
    outside = jnp.concatenate(
        [
            jnp.zeros((1, breadth, 1), BF16),
            jnp.full((1, breadth, 1), LAND, BF16),
        ],
        axis=1,
    )
    packed = links.extend_lat(packed, WIDE, outside)
    state_rows = packed[:, :breadth]
    coded_rows = packed[:, breadth:]
    east_edge = jnp.concatenate([state_rows[:, -WIDE:], coded_rows[:, -NARROW:]], axis=1)
    west_edge = jnp.concatenate([state_rows[:, :WIDE], coded_rows[:, :NARROW]], axis=1)
    west = links.shift_lon(east_edge, 1)
    east = links.shift_lon(west_edge, -1)

    def window(parts, at, pitch):
        used = at + sum(part.shape[1] for part in parts)
        lead = jnp.zeros((window_rows, at, channels), BF16)
        rest = jnp.zeros((window_rows, pitch - used, channels), BF16)
        return jnp.concatenate([lead, *parts, rest], axis=1)

    state_pitch, field_pitch, inner_pitch = (
        round_up(breadth + size, 8) for size in (STATE_AT + WIDE, FIELD_AT + NARROW, NARROW)
    )
    state_window = window(
        [west[:, :WIDE], state_rows, east[:, :WIDE]], STATE_AT - WIDE, state_pitch
    )
    coded_window = window(
        [west[:, WIDE:], coded_rows, east[:, WIDE:]], FIELD_AT - NARROW, field_pitch
    )

    padded_rows = window_rows + 2 * MARGIN
    all_cells = second_rows * inner_pitch
    small_rows = round_up(BLOCKS * (TAPS + 5 + groups), 16)
    grad_rows = BLOCKS * 2 * hidden_units + small_rows
    unit = 16 * 8
    small_rows += round_up(grad_rows, unit) - grad_rows
    grad_rows = round_up(grad_rows, unit)
    tile = (height, breadth, channels)
    vmem = pl.BlockSpec(memory_space=pltpu.VMEM)
    own_rows = (window_rows, breadth)
    scratch = [
        pltpu.VMEM((padded_rows, state_pitch, channels), F32),
        pltpu.VMEM((padded_rows, field_pitch, channels), F32),
        pltpu.VMEM((BLOCKS, TAPS, channels), F32),
        pltpu.VMEM((padded_rows, field_pitch, channels), F32),
        pltpu.VMEM((padded_rows, inner_pitch, channels), F32),
        pltpu.VMEM((window_rows, inner_pitch, channels), F32),
        pltpu.VMEM(own_rows + (channels,), F32),
        pltpu.VMEM(own_rows + (channels,), F32),
        pltpu.VMEM(own_rows + (channels,), F32),
        pltpu.VMEM(own_rows + (hidden_units,), F32),
        pltpu.VMEM(own_rows + (hidden_units,), BF16),
        pltpu.VMEM((height, breadth, hidden_units), BF16),
        pltpu.VMEM(own_rows + (channels,), BF16),
        pltpu.VMEM(tile, BF16),
        pltpu.VMEM(tile, F32),
        pltpu.VMEM((all_cells, hidden_units), BF16),
        pltpu.VMEM((all_cells, hidden_units), BF16),
        pltpu.VMEM((all_cells, channels), BF16),
        pltpu.VMEM((all_cells, channels), BF16),
        pltpu.VMEM((BLOCKS, 5, 8, channels), F32),
        pltpu.VMEM((BLOCKS, 8, hidden_units), F32),
        pltpu.VMEM((small_rows, channels), F32),
    ]
    sizes = (height, breadth, first_rows, second_rows, window_rows)
    taps_in = dw_kernel.reshape(BLOCKS, TAPS, channels)
    output, grad_mixed, masked, grads = pl.pallas_call(
        functools.partial(tile_kernel, sizes),
        out_shape=(
            jax.ShapeDtypeStruct(tile, BF16),
            jax.ShapeDtypeStruct(tile, BF16),
            jax.ShapeDtypeStruct(tile, BF16),
            jax.ShapeDtypeStruct((grad_rows, channels), BF16),
        ),
        in_specs=[pl.BlockSpec(memory_space=pltpu.SMEM)] + [vmem] * 11,
        out_specs=(vmem,) * 4,
        scratch_shapes=scratch,
        compiler_params=pltpu.CompilerParams(vmem_limit_bytes=48 * 1024 * 1024),
        cost_estimate=pl.CostEstimate(
            flops=20 * all_cells * channels * hidden_units,
            bytes_accessed=4 * height * breadth * channels * 4,
            transcendentals=0,
        ),
    )(starts, state_window, coded_window, taps_in, *params[1:])

    before = links.shift_lon(grad_mixed[:, -MARGIN:], 1)
    after = links.shift_lon(grad_mixed[:, :MARGIN], -1)
    beside = jnp.concatenate([before, grad_mixed, after], axis=1)
    spread = links.extend_lat(beside, MARGIN, jnp.zeros((1, 1, 1), BF16))
    if sides == 1:
        empty = jnp.zeros((MARGIN,) + spread.shape[1:], BF16)
        first = jnp.concatenate([empty, spread], axis=0)
        last = jnp.concatenate([spread, empty], axis=0)
        spread = jnp.where(lat == 0, first, last)
    pitch = round_up(spread.shape[1], 8)
    spread = jnp.pad(spread, ((0, 0), (0, pitch - spread.shape[1]), (0, 0)))
    grad_state = pl.pallas_call(
        state_kernel,
        out_shape=jax.ShapeDtypeStruct(tile, BF16),
        in_specs=[vmem] * 3,
        out_specs=vmem,
        scratch_shapes=[pltpu.VMEM(spread.shape, F32), pltpu.VMEM((TAPS, channels), F32)],
        compiler_params=pltpu.CompilerParams(vmem_limit_bytes=16 * 1024 * 1024),
    )(spread, masked, taps_in[0])

    total = links.sum_all(grads).astype(F32) * grad_norm
    size = 2 * hidden_units
    at = BLOCKS * size
    weights = total[:at].reshape(BLOCKS, 2, groups, channels, channels)
    grad_in = weights[:, 0].transpose(0, 2, 1, 3).reshape(BLOCKS, channels, hidden_units)
    grad_out = weights[:, 1].reshape(BLOCKS, hidden_units, channels)
    small = total[at : at + BLOCKS * (TAPS + 5 + groups)].reshape(BLOCKS, -1, channels)
    grad_kernel = small[:, :TAPS].reshape(BLOCKS, KSIZE, KSIZE, channels)
    grad_bias_in = small[:, TAPS + 5 :].reshape(BLOCKS, hidden_units)
    return (
        output,
        grad_state,
        grad_kernel,
        small[:, TAPS + 4],
        small[:, TAPS + 2],
        small[:, TAPS + 3],
        grad_in,
        grad_bias_in,
        grad_out,
        small[:, TAPS + 1],
        small[:, TAPS],
    )


def solution(mesh):
    tile = P("lat", "lon", None)
    placed = (tile, P("lat", "lon"), tile) + (P(),) * 9
    return jax.shard_map(
        functools.partial(on_device, Links(mesh)),
        mesh=mesh,
        in_specs=placed,
        out_specs=(tile, tile) + (P(),) * 9,
        check_vma=False,
    )
```

```python
import functools
import math

import jax
import jax.numpy as jnp
from jax import lax
from jax.experimental import pallas as pl
from jax.experimental.pallas import tpu as pltpu
from jax.sharding import PartitionSpec as P

KSIZE = 7
MARGIN = KSIZE // 2
TAPS = KSIZE * KSIZE
BLOCKS = 2
EPS_NORM = 1e-06
INV_ROOT_TWO = 0.7071067811865476
INV_ROOT_TWO_PI = 0.3989422804014327
LAND = 1024.0
LAND_BOUND = 512.0
F32 = jnp.float32
BF16 = jnp.bfloat16
FIRST_STEP = 19
SECOND_STEP = 8
BACK_STEP = 9
TAP_STEP = 5
STATE_AT = 11
FIELD_AT = 8
INNER_AT = 3
WIDE = 3 * MARGIN
NARROW = 2 * MARGIN


def divisor(size, most):
    return max(step for step in range(1, most + 1) if size % step == 0)


def round_up(size, unit):
    return (size + unit - 1) // unit * unit


def conv_rows(source, base, first, count, width, kernel_ref, flip):
    sums = [None] * count
    for tap_col in range(KSIZE):
        taps = []
        for tap_row in range(KSIZE):
            index = tap_row * KSIZE + tap_col
            taps.append(kernel_ref[pl.ds(TAPS - 1 - index if flip else index, 1), :])
        for row in range(count + KSIZE - 1):
            piece = source[base + row, pl.ds(first + tap_col, width), :]
            for tap_row in range(KSIZE):
                out = row - tap_row
                if 0 <= out < count:
                    term = piece * taps[tap_row]
                    sums[out] = term if sums[out] is None else sums[out] + term
    return jnp.concatenate(sums, axis=0)


def normal_parts(hidden):
    cumulative = 0.5 + 0.5 * lax.erf(hidden * INV_ROOT_TWO)
    return cumulative, jnp.exp(-0.5 * hidden * hidden)


def fold(values):
    return jnp.sum(values.reshape(values.shape[0] // 8, 8, values.shape[1]), axis=0)


def normalise(mixed):
    center = mixed - jnp.mean(mixed, axis=-1, keepdims=True)
    inverse = lax.rsqrt(jnp.mean(center * center, axis=-1, keepdims=True) + EPS_NORM)
    return center * inverse, inverse


def normalise_back(grad, normed, inverse):
    return inverse * (
        grad
        - jnp.mean(grad, axis=-1, keepdims=True)
        - normed * jnp.mean(grad * normed, axis=-1, keepdims=True)
    )


def rows_of(ref, base, first, count, width):
    return jnp.concatenate(
        [ref[base + row, pl.ds(first, width), :] for row in range(count)], axis=0
    )


CONTRACT_COLS = (((1,), (1,)), ((), ()))
CONTRACT_ROWS = (((0,), (0,)), ((), ()))


def dot(left, right):
    return jnp.dot(left, right, preferred_element_type=F32)


def dot_cols(left, right):
    return lax.dot_general(left, right, CONTRACT_COLS, preferred_element_type=F32)


def dot_rows(left, right):
    return lax.dot_general(left, right, CONTRACT_ROWS, preferred_element_type=F32)


def tap_sums(grad_ref, grad_row, grad_col, field_ref, field_row, field_col, height, width, out):
    rows = divisor(height, TAP_STEP)
    for cols in ((0, 1, 2, 3), (4, 5, 6)):

        def advance(step, sums):
            sums = list(sums)
            at = step * rows
            grads = [grad_ref[grad_row + at + row, pl.ds(grad_col, width), :] for row in range(rows)]
            for place, tap_col in enumerate(cols):
                for row in range(rows + KSIZE - 1):
                    piece = field_ref[field_row + at + row, pl.ds(field_col + tap_col, width), :]
                    for tap_row in range(KSIZE):
                        if 0 <= row - tap_row < rows:
                            index = place * KSIZE + tap_row
                            sums[index] = sums[index] + fold(grads[row - tap_row] * piece)
            return tuple(sums)

        zeros = tuple(jnp.zeros((8, grad_ref.shape[2]), F32) for _ in range(KSIZE * len(cols)))
        sums = lax.fori_loop(0, height // rows, advance, zeros)
        for place, tap_col in enumerate(cols):
            for tap_row in range(KSIZE):
                total = jnp.sum(sums[place * KSIZE + tap_row], axis=0, keepdims=True)
                out[pl.ds(tap_row * KSIZE + tap_col, 1), :] = total


def tile_kernel(
    sizes,
    starts,
    state_tile,
    coded_tile,
    lat_pieces,
    west,
    east,
    dw_in,
    conv_bias,
    norm_gain,
    norm_bias,
    weight_in,
    bias_in,
    weight_out,
    bias_out,
    layer_scale,
    output,
    mixed_out,
    masked_out,
    grads_out,
    state,
    coded,
    kernels,
    field,
    inner,
    result,
    normed_own,
    inverse_own,
    branch_own,
    slope_own,
    active_own,
    hidden_own,
    lifted_own,
    branch_grad_own,
    mixed_own,
    active_all,
    hidden_all,
    lifted_all,
    branch_grad_all,
    sums,
    hidden_sums,
    taps,
):
    height, breadth, first_rows, second_rows, window_rows = sizes
    channels = state.shape[2]
    own_start = starts[0]
    second_start = starts[1]
    first_start = starts[2]
    first_width = field.shape[1]
    second_width = inner.shape[1]
    pad = MARGIN

    for ref in (state, coded, field, inner):
        edge = jnp.zeros((pad,) + ref.shape[1:], F32)
        ref[pl.ds(0, pad)] = edge
        ref[pl.ds(pad + window_rows, pad)] = edge
    state[pl.ds(pad, window_rows)] = jnp.zeros((window_rows,) + state.shape[1:], F32)
    coded[pl.ds(pad, window_rows)] = jnp.zeros((window_rows,) + coded.shape[1:], F32)

    def place(window, at, values):
        window[at[0], pl.ds(at[1], values.shape[1]), :] = values.astype(F32)

    place(state, (pl.ds(pad + own_start, height), STATE_AT), state_tile[...])
    place(coded, (pl.ds(pad + own_start, height), FIELD_AT), coded_tile[...])
    for index in range(lat_pieces.shape[0]):
        spots = pl.ds(pad + starts[3 + index], WIDE)
        place(state, (spots, STATE_AT), lat_pieces[index, :, :breadth])
        place(coded, (spots, FIELD_AT), lat_pieces[index, :, breadth:])
    spots = pl.ds(pad, window_rows)
    place(state, (spots, STATE_AT - WIDE), west[:, :WIDE])
    place(state, (spots, STATE_AT + breadth), east[:, :WIDE])
    place(coded, (spots, FIELD_AT - NARROW), west[:, WIDE:])
    place(coded, (spots, FIELD_AT + breadth), east[:, WIDE:])
    kernels[...] = dw_in[...].astype(F32)
    sums[...] = jnp.zeros_like(sums)
    hidden_sums[...] = jnp.zeros_like(hidden_sums)

    def param(ref, layer):
        return ref[pl.ds(layer, 1), :]

    first_step = divisor(first_rows, FIRST_STEP)

    def forward_first(step, carry):
        row = first_start + step * first_step
        cells = first_step * first_width
        mixed = conv_rows(state, row, 0, first_step, first_width, kernels.at[0], False)
        normed, inverse = normalise(mixed + param(conv_bias, 0))
        lifted = (normed * param(norm_gain, 0) + param(norm_bias, 0)).astype(BF16)
        hidden = dot(lifted, weight_in[0]) + param(bias_in, 0)
        cumulative, bell = normal_parts(hidden)
        active = hidden * cumulative
        branch = dot(active.astype(BF16), weight_out[0]) + param(bias_out, 0)
        center = rows_of(state, row + pad, MARGIN, first_step, first_width)
        mark = rows_of(coded, row + pad, 0, first_step, first_width)
        value = jnp.where(mark < LAND_BOUND, center + param(layer_scale, 0) * branch, 0.0)
        value = value.reshape(first_step, first_width, channels)

        for index in range(first_step):
            field[row + pad + index] = value[index]

        def own(values):
            shape = (first_step, first_width, values.shape[1])
            return values.reshape(shape)[:, FIELD_AT : FIELD_AT + breadth]

        slope = own(cumulative) + own(hidden) * (own(bell) * INV_ROOT_TWO_PI)
        spots = pl.ds(row, first_step)
        slope_own[spots] = slope
        active_own[spots] = own(active).astype(BF16)
        normed_own[spots] = own(normed)
        inverse_own[spots] = own(jnp.broadcast_to(inverse, normed.shape))
        branch_own[spots] = own(branch)
        lifted_own[spots] = own(normed * param(norm_gain, 0) + param(norm_bias, 0)).astype(BF16)
        return carry

    lax.fori_loop(0, first_rows // first_step, forward_first, 0)

    second_step = divisor(second_rows, SECOND_STEP)

    def both_second(step, carry):
        row = second_start + step * second_step
        cells = second_step * second_width
        shift = FIELD_AT - INNER_AT
        mixed = conv_rows(
            field, row, shift - MARGIN, second_step, second_width, kernels.at[1], False
        )
        normed, inverse = normalise(mixed + param(conv_bias, 1))
        lifted = normed * param(norm_gain, 1) + param(norm_bias, 1)
        hidden = dot(lifted.astype(BF16), weight_in[1]) + param(bias_in, 1)
        cumulative, bell = normal_parts(hidden)
        active = (hidden * cumulative).astype(BF16)
        branch = dot(active, weight_out[1]) + param(bias_out, 1)
        center = rows_of(field, row + pad, shift, second_step, second_width)
        mark = rows_of(coded, row + pad, shift, second_step, second_width)
        ocean = mark < LAND_BOUND
        value = jnp.where(ocean, center + param(layer_scale, 1) * branch, 0.0)
        value = value.reshape(second_step, second_width, channels)
        masked = jnp.where(ocean, mark, 0.0)
        grad_branch = (masked * param(layer_scale, 1)).astype(BF16)
        grad_active = dot_cols(grad_branch, weight_out[1])
        slope = cumulative + hidden * (bell * INV_ROOT_TWO_PI)
        grad_hidden = (grad_active * slope).astype(BF16)
        grad_lifted = dot_cols(grad_hidden, weight_in[1])
        grad_mixed = normalise_back(grad_lifted * param(norm_gain, 1), normed, inverse)
        grad_mixed = grad_mixed.reshape(second_step, second_width, channels)
        for index in range(second_step):
            result[row + index] = value[index]
            inner[row + pad + index] = grad_mixed[index]

        shape = (second_step, second_width, channels)
        row_of = lax.broadcasted_iota(jnp.int32, shape, 0) + (row - own_start)
        col_of = lax.broadcasted_iota(jnp.int32, shape, 1) - INNER_AT
        inside = (row_of >= 0) & (row_of < height) & (col_of >= 0) & (col_of < breadth)
        inside = jnp.where(inside, 1.0, 0.0).astype(F32).reshape(cells, channels)
        own_lifted = grad_lifted * inside
        own_branch = grad_branch.astype(F32) * inside
        sums[1, 0] += fold(masked * branch * inside)
        sums[1, 1] += fold(own_branch)
        sums[1, 2] += fold(own_lifted * normed)
        sums[1, 3] += fold(own_lifted)
        wide = jnp.concatenate([inside] * (hidden.shape[1] // channels), axis=1)
        hidden_sums[1] += fold(grad_hidden.astype(F32) * wide)
        spots = pl.ds(pl.multiple_of(step * cells, cells), cells)
        active_all[spots] = active
        hidden_all[spots] = grad_hidden
        lifted_all[spots] = (lifted * inside).astype(BF16)
        branch_grad_all[spots] = own_branch.astype(BF16)
        return carry

    lax.fori_loop(0, second_rows // second_step, both_second, 0)

    back_step = divisor(height, BACK_STEP)

    def backward_first(step, carry):
        row = own_start + step * back_step
        cells = back_step * breadth
        mark = rows_of(coded, row + pad, FIELD_AT, back_step, breadth)
        ocean = mark < LAND_BOUND
        masked_next = jnp.where(ocean, mark, 0.0)
        spread = conv_rows(inner, row, 0, back_step, breadth, kernels.at[1], True)
        masked = jnp.where(ocean, masked_next + spread, 0.0)
        grad_branch = (masked * param(layer_scale, 0)).astype(BF16)
        grad_active = dot_cols(grad_branch, weight_out[0])
        slope = slope_own[pl.ds(row, back_step)].reshape(cells, grad_active.shape[1])
        grad_hidden = (grad_active * slope).astype(BF16)
        grad_lifted = dot_cols(grad_hidden, weight_in[0])
        normed = normed_own[pl.ds(row, back_step)].reshape(cells, channels)
        inverse = inverse_own[pl.ds(row, back_step)].reshape(cells, channels)
        grad_mixed = normalise_back(grad_lifted * param(norm_gain, 0), normed, inverse)
        branch = branch_own[pl.ds(row, back_step)].reshape(cells, channels)
        sums[0, 0] += fold(masked * branch)
        sums[0, 1] += fold(grad_branch.astype(F32))
        sums[0, 2] += fold(grad_lifted * normed)
        sums[0, 3] += fold(grad_lifted)
        sums[0, 4] += fold(grad_mixed)
        hidden_sums[0] += fold(grad_hidden.astype(F32))
        inner_rows = rows_of(inner, row + pad, INNER_AT, back_step, breadth)
        sums[1, 4] += fold(inner_rows)
        tile = pl.ds(step * back_step, back_step)
        shape = (back_step, breadth, channels)
        grad_mixed = grad_mixed.reshape(shape)
        mixed_own[tile] = grad_mixed
        mixed_out[tile] = grad_mixed.astype(BF16)
        masked_out[tile] = masked.reshape(shape).astype(BF16)
        hidden_own[tile] = grad_hidden.reshape(back_step, breadth, grad_hidden.shape[1])
        branch_grad_own[tile] = grad_branch.reshape(shape)
        value = rows_of(result, row, INNER_AT, back_step, breadth)
        output[tile] = value.reshape(shape).astype(BF16)
        return carry

    lax.fori_loop(0, height // back_step, backward_first, 0)

    hidden_units = weight_in.shape[2]
    groups = hidden_units // channels
    tile = pl.ds(own_start, height)
    cells = height * breadth

    def flat(ref, spots):
        return ref[spots].reshape(cells, ref.shape[2])

    operands = (
        (
            flat(lifted_own, tile),
            flat(hidden_own, pl.ds(0, height)),
            flat(active_own, tile),
            flat(branch_grad_own, pl.ds(0, height)),
        ),
        (lifted_all[...], hidden_all[...], active_all[...], branch_grad_all[...]),
    )
    for layer, (lifted, grad_hidden, active, grad_branch) in enumerate(operands):
        at = layer * 2 * hidden_units
        grad_in = dot_rows(lifted, grad_hidden)
        for group in range(groups):
            grads_out[pl.ds(at + group * channels, channels), :] = grad_in[
                :, group * channels : (group + 1) * channels
            ].astype(BF16)
        grad_out = dot_rows(grad_branch, active)
        for group in range(groups):
            grads_out[pl.ds(at + hidden_units + group * channels, channels), :] = grad_out[
                :, group * channels : (group + 1) * channels
            ].T.astype(BF16)

    at = BLOCKS * 2 * hidden_units
    tail = grads_out.shape[0] - at
    taps[...] = jnp.zeros_like(taps)
    for layer in range(BLOCKS):
        base = layer * (TAPS + 5 + groups)
        if layer:
            tap_sums(
                inner,
                own_start + pad,
                INNER_AT,
                field,
                own_start,
                FIELD_AT - MARGIN,
                height,
                breadth,
                taps.at[pl.ds(base, TAPS)],
            )
        else:
            tap_sums(
                mixed_own,
                0,
                0,
                state,
                own_start,
                STATE_AT - MARGIN,
                height,
                breadth,
                taps.at[pl.ds(base, TAPS)],
            )
        for member in range(5):
            taps[pl.ds(base + TAPS + member, 1), :] = jnp.sum(
                sums[layer, member], axis=0, keepdims=True
            )
        hidden_total = jnp.sum(hidden_sums[layer], axis=0, keepdims=True)
        for group in range(groups):
            taps[pl.ds(base + TAPS + 5 + group, 1), :] = hidden_total[
                :, group * channels : (group + 1) * channels
            ]
    grads_out[pl.ds(at, tail), :] = taps[...].astype(BF16)


def state_kernel(window, masked, dw_in, out, wide, kernels):
    height, breadth, channels = masked.shape
    wide[...] = window[...].astype(F32)
    kernels[...] = dw_in[...].astype(F32)

    rows = divisor(height, BACK_STEP)

    def advance(step, carry):
        row = step * rows
        spread = conv_rows(wide, row, 0, rows, breadth, kernels, True)
        tile = pl.ds(row, rows)
        shape = (rows, breadth, channels)
        out[tile] = (masked[tile].astype(F32) + spread.reshape(shape)).astype(BF16)
        return carry

    lax.fori_loop(0, height // rows, advance, 0)


def code_kernel(lat, state, land_sea, cotangent, coded, edge):
    height, breadth, channels = state.shape
    ocean = jnp.where(land_sea[...] != 0, 1.0, 0.0).astype(F32)
    shape = (height, breadth, breadth)
    row_of = lax.broadcasted_iota(jnp.int32, shape, 1)
    col_of = lax.broadcasted_iota(jnp.int32, shape, 2)
    chosen = jnp.where(row_of == col_of, ocean[:, None, :], 0.0)
    chosen = chosen.reshape(height * breadth, breadth).astype(BF16)
    wide = dot(chosen, jnp.ones((breadth, channels), BF16)).reshape(height, breadth, channels)
    coded[...] = jnp.where(wide > 0.5, cotangent[...].astype(F32), LAND).astype(BF16)
    for side in range(edge.shape[0]):
        first = (1 - lat[0]) * (height - WIDE) if edge.shape[0] == 1 else (1 - side) * (height - WIDE)
        edge[side, :, :breadth] = state[pl.ds(first, WIDE)]
        edge[side, :, breadth:] = coded[pl.ds(first, WIDE)]


def gradient_kernel(grad_norm, held, own, other, *outs_and_scratch):
    *outs, total = outs_and_scratch
    kernel, conv_bias, gain, shift, first, first_bias, second, second_bias, scale = outs
    half = own.shape[0]
    channels = own.shape[1]
    total[pl.ds(held[0] * half, half)] = own[...].astype(F32) * grad_norm
    total[pl.ds((1 - held[0]) * half, half)] = other[...].astype(F32) * grad_norm
    units = second.shape[1]
    groups = units // channels
    for layer in range(BLOCKS):
        at = layer * 2 * units
        for group in range(groups):
            first[layer, :, group * channels : (group + 1) * channels] = total[
                at + group * channels : at + (group + 1) * channels
            ]
        second[layer] = total[at + units : at + 2 * units]
        at = BLOCKS * 2 * units + layer * (TAPS + 5 + groups)
        for tap_row in range(KSIZE):
            kernel[layer, tap_row] = total[at + tap_row * KSIZE : at + (tap_row + 1) * KSIZE]
        for member, out in enumerate((scale, second_bias, gain, shift, conv_bias)):
            out[layer : layer + 1] = total[at + TAPS + member : at + TAPS + member + 1]
        for group in range(groups):
            row = at + TAPS + 5 + group
            first_bias[layer : layer + 1, group * channels : (group + 1) * channels] = total[
                row : row + 1
            ]


class Links:
    def __init__(self, mesh):
        self.lon = mesh.shape["lon"]
        self.lat = mesh.shape["lat"]
        self.axes = ("lon", "lat")

    def shift_lon(self, values, by):
        pairs = [(place, (place + by) % self.lon) for place in range(self.lon)]
        return lax.ppermute(values, "lon", pairs)

    def shift_lat(self, values, by):
        pairs = [
            (place, place + by) for place in range(self.lat) if 0 <= place + by < self.lat
        ]
        return lax.ppermute(values, "lat", pairs)

    def swap(self, values, lon_bits, lat_bits):
        pairs = []
        for lon in range(self.lon):
            for lat in range(self.lat):
                there = (lon ^ lon_bits) * self.lat + (lat ^ lat_bits)
                pairs.append((lon * self.lat + lat, there))
        return lax.ppermute(values, self.axes, pairs)

    def extend_lat(self, field, width, outside):
        place = lax.axis_index("lat")
        if self.lat == 2:
            mine = jnp.where(place == 0, field[-width:], field[:width])
            other = lax.ppermute(mine, "lat", [(0, 1), (1, 0)])
            below = jnp.concatenate([field, other], axis=0)
            above = jnp.concatenate([other, field], axis=0)
            return jnp.where(place == 0, below, above)
        before = self.shift_lat(field[-width:], 1)
        after = self.shift_lat(field[:width], -1)
        before = jnp.where(place == 0, outside, before)
        after = jnp.where(place == self.lat - 1, outside, after)
        return jnp.concatenate([before, field, after], axis=0)

    def sum_all(self, rows):
        lon = lax.axis_index("lon")
        lat = lax.axis_index("lat")
        bits = [(1 << bit, 0) for bit in range(self.lon.bit_length() - 1)]
        bits = bits[:1] + [(0, 1 << bit) for bit in range(self.lat.bit_length() - 1)] + bits[1:]

        def code(group):
            total = jnp.int32(0)
            for index, (lon_bit, lat_bit) in enumerate(group):
                held = (lon // lon_bit) % 2 if lon_bit else (lat // lat_bit) % 2
                total = total + held * (1 << index)
            return total

        def merged(group, choice):
            lon_bits = sum(bit[0] for index, bit in enumerate(group) if choice >> index & 1)
            lat_bits = sum(bit[1] for index, bit in enumerate(group) if choice >> index & 1)
            return lon_bits, lat_bits

        def scatter(values, group):
            count = 1 << len(group)
            pieces = values.reshape(count, -1, values.shape[1])
            here = code(group)
            total = lax.dynamic_index_in_dim(pieces, here, 0, False).astype(F32)
            for choice in range(1, count):
                sent = lax.dynamic_index_in_dim(pieces, here ^ choice, 0, False)
                total = total + self.swap(sent, *merged(group, choice)).astype(F32)
            return total.astype(BF16)

        def exchange(values, group):
            total = values.astype(F32)
            for choice in range(1, 1 << len(group)):
                total = total + self.swap(values, *merged(group, choice)).astype(F32)
            return total.astype(BF16)

        def gather(values, group):
            count = 1 << len(group)
            pieces = [values]
            for choice in range(1, count):
                pieces.append(self.swap(values, *merged(group, choice)))
            stack = jnp.stack(pieces)
            here = code(group)
            ordered = [
                lax.dynamic_index_in_dim(stack, here ^ place, 0, False) for place in range(count)
            ]
            return jnp.concatenate(ordered, axis=0)

        pair, quad, rest = bits[:1], bits[1:3], bits[3:]
        values = scatter(scatter(rows, pair), quad)
        while rest:
            values = exchange(values, rest[:2])
            rest = rest[2:]
        values = gather(values, quad)
        return code(pair), values, self.swap(values, *pair[0])


def on_device(links, state, land_sea, cotangent, *params):
    dw_kernel, weight_in = params[0], params[4]
    height, breadth, channels = state.shape
    hidden_units = weight_in.shape[2]
    groups = hidden_units // channels
    grad_norm = 1.0 / math.sqrt(links.lat * height * links.lon * breadth)
    lat = lax.axis_index("lat")
    sides = 1 if links.lat == 2 else 2
    window_rows = height + sides * WIDE
    first_rows = height + sides * NARROW
    second_rows = height + sides * MARGIN

    def start(margin):
        skipped = WIDE - margin
        return lat * skipped if sides == 1 else jnp.int32(skipped)

    vmem = pl.BlockSpec(memory_space=pltpu.VMEM)
    smem = pl.BlockSpec(memory_space=pltpu.SMEM)
    tile = (height, breadth, channels)
    coded, edges = pl.pallas_call(
        code_kernel,
        out_shape=(
            jax.ShapeDtypeStruct(tile, BF16),
            jax.ShapeDtypeStruct((sides, WIDE, 2 * breadth, channels), BF16),
        ),
        in_specs=[smem, vmem, vmem, vmem],
        out_specs=(vmem, vmem),
    )(lat.reshape(1), state, land_sea, cotangent)
    if sides == 1:
        pieces = links.swap(edges, 0, 1)
        places = [(1 - lat) * height]
    else:
        outside = jnp.concatenate(
            [jnp.zeros((1, breadth, 1), BF16), jnp.full((1, breadth, 1), LAND, BF16)], axis=1
        )
        above = jnp.where(lat == 0, outside, links.shift_lat(edges[0], 1))
        below = jnp.where(lat == links.lat - 1, outside, links.shift_lat(edges[1], -1))
        pieces = jnp.stack([above, below])
        places = [jnp.int32(0), jnp.int32(WIDE + height)]

    def edge(tile_cols):
        own = jnp.concatenate([state[:, tile_cols[0]], coded[:, tile_cols[1]]], axis=1)
        ends = [
            jnp.concatenate(
                [piece[:, :breadth][:, tile_cols[0]], piece[:, breadth:][:, tile_cols[1]]], axis=1
            )
            for piece in pieces
        ]
        if sides == 2:
            return jnp.concatenate([ends[0], own, ends[1]], axis=0)
        after = jnp.concatenate([own, ends[0]], axis=0)
        before = jnp.concatenate([ends[0], own], axis=0)
        return jnp.where(lat == 0, after, before)

    west = links.shift_lon(edge((slice(-WIDE, None), slice(-NARROW, None))), 1)
    east = links.shift_lon(edge((slice(WIDE), slice(NARROW))), -1)
    starts = jnp.stack([start(0), start(MARGIN), start(NARROW), *places]).astype(jnp.int32)
    state_pitch, field_pitch, inner_pitch = (
        round_up(breadth + size, 8) for size in (STATE_AT + WIDE, FIELD_AT + NARROW, NARROW)
    )

    padded_rows = window_rows + 2 * MARGIN
    all_cells = second_rows * inner_pitch
    small_rows = round_up(BLOCKS * (TAPS + 5 + groups), 16)
    grad_rows = BLOCKS * 2 * hidden_units + small_rows
    unit = 16 * 8
    small_rows += round_up(grad_rows, unit) - grad_rows
    grad_rows = round_up(grad_rows, unit)
    own_rows = (window_rows, breadth)
    scratch = [
        pltpu.VMEM((padded_rows, state_pitch, channels), F32),
        pltpu.VMEM((padded_rows, field_pitch, channels), F32),
        pltpu.VMEM((BLOCKS, TAPS, channels), F32),
        pltpu.VMEM((padded_rows, field_pitch, channels), F32),
        pltpu.VMEM((padded_rows, inner_pitch, channels), F32),
        pltpu.VMEM((window_rows, inner_pitch, channels), F32),
        pltpu.VMEM(own_rows + (channels,), F32),
        pltpu.VMEM(own_rows + (channels,), F32),
        pltpu.VMEM(own_rows + (channels,), F32),
        pltpu.VMEM(own_rows + (hidden_units,), F32),
        pltpu.VMEM(own_rows + (hidden_units,), BF16),
        pltpu.VMEM((height, breadth, hidden_units), BF16),
        pltpu.VMEM(own_rows + (channels,), BF16),
        pltpu.VMEM(tile, BF16),
        pltpu.VMEM(tile, F32),
        pltpu.VMEM((all_cells, hidden_units), BF16),
        pltpu.VMEM((all_cells, hidden_units), BF16),
        pltpu.VMEM((all_cells, channels), BF16),
        pltpu.VMEM((all_cells, channels), BF16),
        pltpu.VMEM((BLOCKS, 5, 8, channels), F32),
        pltpu.VMEM((BLOCKS, 8, hidden_units), F32),
        pltpu.VMEM((small_rows, channels), F32),
    ]
    sizes = (height, breadth, first_rows, second_rows, window_rows)
    taps_in = dw_kernel.reshape(BLOCKS, TAPS, channels)
    output, grad_mixed, masked, grads = pl.pallas_call(
        functools.partial(tile_kernel, sizes),
        out_shape=(
            jax.ShapeDtypeStruct(tile, BF16),
            jax.ShapeDtypeStruct(tile, BF16),
            jax.ShapeDtypeStruct(tile, BF16),
            jax.ShapeDtypeStruct((grad_rows, channels), BF16),
        ),
        in_specs=[smem] + [vmem] * 14,
        out_specs=(vmem,) * 4,
        scratch_shapes=scratch,
        compiler_params=pltpu.CompilerParams(vmem_limit_bytes=48 * 1024 * 1024),
        cost_estimate=pl.CostEstimate(
            flops=20 * all_cells * channels * hidden_units,
            bytes_accessed=4 * height * breadth * channels * 4,
            transcendentals=0,
        ),
    )(starts, state, coded, pieces, west, east, taps_in, *params[1:])

    before = links.shift_lon(grad_mixed[:, -MARGIN:], 1)
    after = links.shift_lon(grad_mixed[:, :MARGIN], -1)
    beside = jnp.concatenate([before, grad_mixed, after], axis=1)
    spread = links.extend_lat(beside, MARGIN, jnp.zeros((1, 1, 1), BF16))
    if sides == 1:
        empty = jnp.zeros((MARGIN,) + spread.shape[1:], BF16)
        first = jnp.concatenate([empty, spread], axis=0)
        last = jnp.concatenate([spread, empty], axis=0)
        spread = jnp.where(lat == 0, first, last)
    pitch = round_up(spread.shape[1], 8)
    spread = jnp.pad(spread, ((0, 0), (0, pitch - spread.shape[1]), (0, 0)))
    grad_state = pl.pallas_call(
        state_kernel,
        out_shape=jax.ShapeDtypeStruct(tile, BF16),
        in_specs=[vmem] * 3,
        out_specs=vmem,
        scratch_shapes=[pltpu.VMEM(spread.shape, F32), pltpu.VMEM((TAPS, channels), F32)],
        compiler_params=pltpu.CompilerParams(vmem_limit_bytes=16 * 1024 * 1024),
        cost_estimate=pl.CostEstimate(
            flops=4_000_000_000, bytes_accessed=8_000_000, transcendentals=0
        ),
    )(spread, masked, taps_in[0])

    held, own, other = links.sum_all(grads)
    shapes = [(BLOCKS, KSIZE, KSIZE, channels)] + [member.shape for member in params[1:]]
    gradients = pl.pallas_call(
        functools.partial(gradient_kernel, grad_norm),
        out_shape=tuple(jax.ShapeDtypeStruct(shape, F32) for shape in shapes),
        in_specs=[smem, vmem, vmem],
        out_specs=(vmem,) * 9,
        scratch_shapes=[pltpu.VMEM((grad_rows, channels), F32)],
    )(held.reshape(1), own, other)
    return (output, grad_state, *gradients)


def solution(mesh):
    tile = P("lat", "lon", None)
    placed = (tile, P("lat", "lon"), tile) + (P(),) * 9
    return jax.shard_map(
        functools.partial(on_device, Links(mesh)),
        mesh=mesh,
        in_specs=placed,
        out_specs=(tile, tile) + (P(),) * 9,
        check_vma=False,
    )
```

```python
import functools
import math

import jax
import jax.numpy as jnp
from jax import lax
from jax.experimental import pallas as pl
from jax.experimental.pallas import tpu as pltpu
from jax.sharding import PartitionSpec as P

KSIZE = 7
MARGIN = KSIZE // 2
TAPS = KSIZE * KSIZE
BLOCKS = 2
EPS_NORM = 1e-06
INV_ROOT_TWO = 0.7071067811865476
INV_ROOT_TWO_PI = 0.3989422804014327
LAND = 1024.0
LAND_BOUND = 512.0
F32 = jnp.float32
BF16 = jnp.bfloat16
FIRST_STEP = 19
SECOND_STEP = 8
BACK_STEP = 9
TAP_STEP = 5
STATE_AT = 11
FIELD_AT = 8
INNER_AT = 3
WIDE = 3 * MARGIN
NARROW = 2 * MARGIN


def divisor(size, most):
    return max(step for step in range(1, most + 1) if size % step == 0)


def round_up(size, unit):
    return (size + unit - 1) // unit * unit


def conv_rows(source, base, first, count, width, kernel_ref, flip):
    sums = [None] * count
    for tap_col in range(KSIZE):
        taps = []
        for tap_row in range(KSIZE):
            index = tap_row * KSIZE + tap_col
            taps.append(kernel_ref[pl.ds(TAPS - 1 - index if flip else index, 1), :])
        for row in range(count + KSIZE - 1):
            piece = source[base + row, pl.ds(first + tap_col, width), :]
            for tap_row in range(KSIZE):
                out = row - tap_row
                if 0 <= out < count:
                    term = piece * taps[tap_row]
                    sums[out] = term if sums[out] is None else sums[out] + term
    return jnp.concatenate(sums, axis=0)


def normal_parts(hidden):
    cumulative = 0.5 + 0.5 * lax.erf(hidden * INV_ROOT_TWO)
    return cumulative, jnp.exp(-0.5 * hidden * hidden)


def fold(values):
    return jnp.sum(values.reshape(values.shape[0] // 8, 8, values.shape[1]), axis=0)


def normalise(mixed):
    center = mixed - jnp.mean(mixed, axis=-1, keepdims=True)
    inverse = lax.rsqrt(jnp.mean(center * center, axis=-1, keepdims=True) + EPS_NORM)
    return center * inverse, inverse


def normalise_back(grad, normed, inverse):
    return inverse * (
        grad
        - jnp.mean(grad, axis=-1, keepdims=True)
        - normed * jnp.mean(grad * normed, axis=-1, keepdims=True)
    )


def rows_of(ref, base, first, count, width):
    return jnp.concatenate(
        [ref[base + row, pl.ds(first, width), :] for row in range(count)], axis=0
    )


CONTRACT_COLS = (((1,), (1,)), ((), ()))
CONTRACT_ROWS = (((0,), (0,)), ((), ()))


def dot(left, right):
    return jnp.dot(left, right, preferred_element_type=F32)


def dot_cols(left, right):
    return lax.dot_general(left, right, CONTRACT_COLS, preferred_element_type=F32)


def dot_rows(left, right):
    return lax.dot_general(left, right, CONTRACT_ROWS, preferred_element_type=F32)


def tap_sums(grad_ref, grad_row, grad_col, field_ref, field_row, field_col, height, width, out):
    rows = divisor(height, TAP_STEP)
    for cols in ((0, 1, 2, 3), (4, 5, 6)):

        def advance(step, sums):
            sums = list(sums)
            at = step * rows
            grads = [grad_ref[grad_row + at + row, pl.ds(grad_col, width), :] for row in range(rows)]
            for place, tap_col in enumerate(cols):
                for row in range(rows + KSIZE - 1):
                    piece = field_ref[field_row + at + row, pl.ds(field_col + tap_col, width), :]
                    for tap_row in range(KSIZE):
                        if 0 <= row - tap_row < rows:
                            index = place * KSIZE + tap_row
                            sums[index] = sums[index] + fold(grads[row - tap_row] * piece)
            return tuple(sums)

        zeros = tuple(jnp.zeros((8, grad_ref.shape[2]), F32) for _ in range(KSIZE * len(cols)))
        sums = lax.fori_loop(0, height // rows, advance, zeros)
        for place, tap_col in enumerate(cols):
            for tap_row in range(KSIZE):
                total = jnp.sum(sums[place * KSIZE + tap_row], axis=0, keepdims=True)
                out[pl.ds(tap_row * KSIZE + tap_col, 1), :] = total


def tile_kernel(
    sizes,
    starts,
    state_tile,
    coded_tile,
    lat_pieces,
    west,
    east,
    dw_in,
    conv_bias,
    norm_gain,
    norm_bias,
    weight_in,
    bias_in,
    weight_out,
    bias_out,
    layer_scale,
    output,
    mixed_out,
    masked_out,
    grads_out,
    state,
    coded,
    kernels,
    field,
    inner,
    result,
    normed_own,
    inverse_own,
    branch_own,
    slope_own,
    active_own,
    hidden_own,
    lifted_own,
    branch_grad_own,
    mixed_own,
    active_all,
    hidden_all,
    lifted_all,
    branch_grad_all,
    sums,
    hidden_sums,
    taps,
):
    height, breadth, first_rows, second_rows, window_rows = sizes
    channels = state.shape[2]
    own_start = starts[0]
    second_start = starts[1]
    first_start = starts[2]
    first_width = field.shape[1]
    second_width = inner.shape[1]
    pad = MARGIN

    for ref in (state, coded, field, inner):
        edge = jnp.zeros((pad,) + ref.shape[1:], F32)
        ref[pl.ds(0, pad)] = edge
        ref[pl.ds(pad + window_rows, pad)] = edge
    state[pl.ds(pad, window_rows)] = jnp.zeros((window_rows,) + state.shape[1:], F32)
    coded[pl.ds(pad, window_rows)] = jnp.zeros((window_rows,) + coded.shape[1:], F32)

    def place(window, at, values):
        window[at[0], pl.ds(at[1], values.shape[1]), :] = values.astype(F32)

    place(state, (pl.ds(pad + own_start, height), STATE_AT), state_tile[...])
    place(coded, (pl.ds(pad + own_start, height), FIELD_AT), coded_tile[...])
    for index in range(lat_pieces.shape[0]):
        spots = pl.ds(pad + starts[3 + index], WIDE)
        place(state, (spots, STATE_AT), lat_pieces[index, :, :breadth])
        place(coded, (spots, FIELD_AT), lat_pieces[index, :, breadth:])
    spots = pl.ds(pad, window_rows)
    place(state, (spots, STATE_AT - WIDE), west[:, :WIDE])
    place(state, (spots, STATE_AT + breadth), east[:, :WIDE])
    place(coded, (spots, FIELD_AT - NARROW), west[:, WIDE:])
    place(coded, (spots, FIELD_AT + breadth), east[:, WIDE:])
    kernels[...] = dw_in[...].astype(F32)
    sums[...] = jnp.zeros_like(sums)
    hidden_sums[...] = jnp.zeros_like(hidden_sums)

    def param(ref, layer):
        return ref[pl.ds(layer, 1), :]

    first_step = divisor(first_rows, FIRST_STEP)

    def forward_first(step, carry):
        row = first_start + step * first_step
        cells = first_step * first_width
        mixed = conv_rows(state, row, 0, first_step, first_width, kernels.at[0], False)
        normed, inverse = normalise(mixed + param(conv_bias, 0))
        lifted = (normed * param(norm_gain, 0) + param(norm_bias, 0)).astype(BF16)
        hidden = dot(lifted, weight_in[0]) + param(bias_in, 0)
        cumulative, bell = normal_parts(hidden)
        active = hidden * cumulative
        branch = dot(active.astype(BF16), weight_out[0]) + param(bias_out, 0)
        center = rows_of(state, row + pad, MARGIN, first_step, first_width)
        mark = rows_of(coded, row + pad, 0, first_step, first_width)
        value = jnp.where(mark < LAND_BOUND, center + param(layer_scale, 0) * branch, 0.0)
        value = value.reshape(first_step, first_width, channels)

        for index in range(first_step):
            field[row + pad + index] = value[index]

        def own(values):
            shape = (first_step, first_width, values.shape[1])
            return values.reshape(shape)[:, FIELD_AT : FIELD_AT + breadth]

        slope = own(cumulative) + own(hidden) * (own(bell) * INV_ROOT_TWO_PI)
        spots = pl.ds(row, first_step)
        slope_own[spots] = slope
        active_own[spots] = own(active).astype(BF16)
        normed_own[spots] = own(normed)
        inverse_own[spots] = own(jnp.broadcast_to(inverse, normed.shape))
        branch_own[spots] = own(branch)
        lifted_own[spots] = own(normed * param(norm_gain, 0) + param(norm_bias, 0)).astype(BF16)
        return carry

    lax.fori_loop(0, first_rows // first_step, forward_first, 0)

    second_step = divisor(second_rows, SECOND_STEP)

    def both_second(step, carry):
        row = second_start + step * second_step
        cells = second_step * second_width
        shift = FIELD_AT - INNER_AT
        mixed = conv_rows(
            field, row, shift - MARGIN, second_step, second_width, kernels.at[1], False
        )
        normed, inverse = normalise(mixed + param(conv_bias, 1))
        lifted = normed * param(norm_gain, 1) + param(norm_bias, 1)
        hidden = dot(lifted.astype(BF16), weight_in[1]) + param(bias_in, 1)
        cumulative, bell = normal_parts(hidden)
        active = (hidden * cumulative).astype(BF16)
        branch = dot(active, weight_out[1]) + param(bias_out, 1)
        center = rows_of(field, row + pad, shift, second_step, second_width)
        mark = rows_of(coded, row + pad, shift, second_step, second_width)
        ocean = mark < LAND_BOUND
        value = jnp.where(ocean, center + param(layer_scale, 1) * branch, 0.0)
        value = value.reshape(second_step, second_width, channels)
        masked = jnp.where(ocean, mark, 0.0)
        grad_branch = (masked * param(layer_scale, 1)).astype(BF16)
        grad_active = dot_cols(grad_branch, weight_out[1])
        slope = cumulative + hidden * (bell * INV_ROOT_TWO_PI)
        grad_hidden = (grad_active * slope).astype(BF16)
        grad_lifted = dot_cols(grad_hidden, weight_in[1])
        grad_mixed = normalise_back(grad_lifted * param(norm_gain, 1), normed, inverse)
        grad_mixed = grad_mixed.reshape(second_step, second_width, channels)
        for index in range(second_step):
            result[row + index] = value[index]
            inner[row + pad + index] = grad_mixed[index]

        shape = (second_step, second_width, channels)
        row_of = lax.broadcasted_iota(jnp.int32, shape, 0) + (row - own_start)
        col_of = lax.broadcasted_iota(jnp.int32, shape, 1) - INNER_AT
        inside = (row_of >= 0) & (row_of < height) & (col_of >= 0) & (col_of < breadth)
        inside = jnp.where(inside, 1.0, 0.0).astype(F32).reshape(cells, channels)
        own_lifted = grad_lifted * inside
        own_branch = grad_branch.astype(F32) * inside
        sums[1, 0] += fold(masked * branch * inside)
        sums[1, 1] += fold(own_branch)
        sums[1, 2] += fold(own_lifted * normed)
        sums[1, 3] += fold(own_lifted)
        wide = jnp.concatenate([inside] * (hidden.shape[1] // channels), axis=1)
        hidden_sums[1] += fold(grad_hidden.astype(F32) * wide)
        spots = pl.ds(pl.multiple_of(step * cells, cells), cells)
        active_all[spots] = active
        hidden_all[spots] = grad_hidden
        lifted_all[spots] = (lifted * inside).astype(BF16)
        branch_grad_all[spots] = own_branch.astype(BF16)
        return carry

    lax.fori_loop(0, second_rows // second_step, both_second, 0)

    back_step = divisor(height, BACK_STEP)

    def backward_first(step, carry):
        row = own_start + step * back_step
        cells = back_step * breadth
        mark = rows_of(coded, row + pad, FIELD_AT, back_step, breadth)
        ocean = mark < LAND_BOUND
        masked_next = jnp.where(ocean, mark, 0.0)
        spread = conv_rows(inner, row, 0, back_step, breadth, kernels.at[1], True)
        masked = jnp.where(ocean, masked_next + spread, 0.0)
        grad_branch = (masked * param(layer_scale, 0)).astype(BF16)
        grad_active = dot_cols(grad_branch, weight_out[0])
        slope = slope_own[pl.ds(row, back_step)].reshape(cells, grad_active.shape[1])
        grad_hidden = (grad_active * slope).astype(BF16)
        grad_lifted = dot_cols(grad_hidden, weight_in[0])
        normed = normed_own[pl.ds(row, back_step)].reshape(cells, channels)
        inverse = inverse_own[pl.ds(row, back_step)].reshape(cells, channels)
        grad_mixed = normalise_back(grad_lifted * param(norm_gain, 0), normed, inverse)
        branch = branch_own[pl.ds(row, back_step)].reshape(cells, channels)
        sums[0, 0] += fold(masked * branch)
        sums[0, 1] += fold(grad_branch.astype(F32))
        sums[0, 2] += fold(grad_lifted * normed)
        sums[0, 3] += fold(grad_lifted)
        sums[0, 4] += fold(grad_mixed)
        hidden_sums[0] += fold(grad_hidden.astype(F32))
        inner_rows = rows_of(inner, row + pad, INNER_AT, back_step, breadth)
        sums[1, 4] += fold(inner_rows)
        tile = pl.ds(step * back_step, back_step)
        shape = (back_step, breadth, channels)
        grad_mixed = grad_mixed.reshape(shape)
        mixed_own[tile] = grad_mixed
        mixed_out[tile] = grad_mixed.astype(BF16)
        masked_out[tile] = masked.reshape(shape).astype(BF16)
        hidden_own[tile] = grad_hidden.reshape(back_step, breadth, grad_hidden.shape[1])
        branch_grad_own[tile] = grad_branch.reshape(shape)
        value = rows_of(result, row, INNER_AT, back_step, breadth)
        output[tile] = value.reshape(shape).astype(BF16)
        return carry

    lax.fori_loop(0, height // back_step, backward_first, 0)

    hidden_units = weight_in.shape[2]
    groups = hidden_units // channels
    tile = pl.ds(own_start, height)
    cells = height * breadth

    def flat(ref, spots):
        return ref[spots].reshape(cells, ref.shape[2])

    operands = (
        (
            flat(lifted_own, tile),
            flat(hidden_own, pl.ds(0, height)),
            flat(active_own, tile),
            flat(branch_grad_own, pl.ds(0, height)),
        ),
        (lifted_all[...], hidden_all[...], active_all[...], branch_grad_all[...]),
    )
    for layer, (lifted, grad_hidden, active, grad_branch) in enumerate(operands):
        at = layer * (grads_out.shape[0] // BLOCKS)
        grad_in = dot_rows(lifted, grad_hidden)
        for group in range(groups):
            grads_out[pl.ds(at + group * channels, channels), :] = grad_in[
                :, group * channels : (group + 1) * channels
            ].astype(BF16)
        grad_out = dot_rows(grad_branch, active)
        for group in range(groups):
            grads_out[pl.ds(at + hidden_units + group * channels, channels), :] = grad_out[
                :, group * channels : (group + 1) * channels
            ].T.astype(BF16)

    taps[...] = jnp.zeros_like(taps)
    for layer in range(BLOCKS):
        base = layer * (taps.shape[0] // BLOCKS)
        if layer:
            tap_sums(
                inner,
                own_start + pad,
                INNER_AT,
                field,
                own_start,
                FIELD_AT - MARGIN,
                height,
                breadth,
                taps.at[pl.ds(base, TAPS)],
            )
        else:
            tap_sums(
                mixed_own,
                0,
                0,
                state,
                own_start,
                STATE_AT - MARGIN,
                height,
                breadth,
                taps.at[pl.ds(base, TAPS)],
            )
        for member in range(5):
            taps[pl.ds(base + TAPS + member, 1), :] = jnp.sum(
                sums[layer, member], axis=0, keepdims=True
            )
        hidden_total = jnp.sum(hidden_sums[layer], axis=0, keepdims=True)
        for group in range(groups):
            taps[pl.ds(base + TAPS + 5 + group, 1), :] = hidden_total[
                :, group * channels : (group + 1) * channels
            ]
    small = taps.shape[0] // BLOCKS
    for layer in range(BLOCKS):
        at = layer * (grads_out.shape[0] // BLOCKS) + 2 * hidden_units
        grads_out[pl.ds(at, small), :] = taps[pl.ds(layer * small, small), :].astype(BF16)


def state_kernel(window, masked, dw_in, out, wide, kernels):
    height, breadth, channels = masked.shape
    wide[...] = window[...].astype(F32)
    kernels[...] = dw_in[...].astype(F32)

    rows = divisor(height, BACK_STEP)

    def advance(step, carry):
        row = step * rows
        spread = conv_rows(wide, row, 0, rows, breadth, kernels, True)
        tile = pl.ds(row, rows)
        shape = (rows, breadth, channels)
        out[tile] = (masked[tile].astype(F32) + spread.reshape(shape)).astype(BF16)
        return carry

    lax.fori_loop(0, height // rows, advance, 0)


def code_kernel(lat, state, land_sea, cotangent, coded, edge):
    height, breadth, channels = state.shape
    ocean = jnp.where(land_sea[...] != 0, 1.0, 0.0).astype(F32)
    for row in range(height):
        wide = jnp.broadcast_to(ocean[:, row : row + 1], (breadth, channels))
        coded[row] = jnp.where(wide > 0.5, cotangent[row].astype(F32), LAND).astype(BF16)
    for side in range(edge.shape[0]):
        first = (1 - lat[0]) * (height - WIDE) if edge.shape[0] == 1 else (1 - side) * (height - WIDE)
        edge[side, :, :breadth] = state[pl.ds(first, WIDE)]
        edge[side, :, breadth:] = coded[pl.ds(first, WIDE)]


def gradient_kernel(grad_norm, held, own, other, *outs):
    kernel, conv_bias, gain, shift, first, first_bias, second, second_bias, scale = outs
    channels = own.shape[1]
    units = second.shape[1]
    groups = units // channels

    def unpack(rows, layer):
        for group in range(groups):
            spots = pl.ds(group * channels, channels)
            first[layer, :, spots] = rows[spots].astype(F32) * grad_norm
        second[layer] = rows[pl.ds(units, units)].astype(F32) * grad_norm
        small = rows[pl.ds(2 * units, rows.shape[0] - 2 * units)].astype(F32) * grad_norm
        for index in range(TAPS):
            kernel[index // KSIZE, index % KSIZE, layer : layer + 1] = small[index : index + 1]
        for member, out in enumerate((scale, second_bias, gain, shift, conv_bias)):
            out[layer : layer + 1] = small[TAPS + member : TAPS + member + 1]
        for group in range(groups):
            row = TAPS + 5 + group
            first_bias[layer : layer + 1, pl.ds(group * channels, channels)] = small[row : row + 1]

    @pl.when(held[0] == 0)
    def _():
        unpack(own, 0)
        unpack(other, 1)

    @pl.when(held[0] != 0)
    def _():
        unpack(own, 1)
        unpack(other, 0)


class Links:
    def __init__(self, mesh):
        self.lon = mesh.shape["lon"]
        self.lat = mesh.shape["lat"]
        self.axes = ("lon", "lat")

    def shift_lon(self, values, by):
        pairs = [(place, (place + by) % self.lon) for place in range(self.lon)]
        return lax.ppermute(values, "lon", pairs)

    def shift_lat(self, values, by):
        pairs = [
            (place, place + by) for place in range(self.lat) if 0 <= place + by < self.lat
        ]
        return lax.ppermute(values, "lat", pairs)

    def swap(self, values, lon_bits, lat_bits):
        pairs = []
        for lon in range(self.lon):
            for lat in range(self.lat):
                there = (lon ^ lon_bits) * self.lat + (lat ^ lat_bits)
                pairs.append((lon * self.lat + lat, there))
        return lax.ppermute(values, self.axes, pairs)

    def extend_lat(self, field, width, outside):
        place = lax.axis_index("lat")
        if self.lat == 2:
            mine = jnp.where(place == 0, field[-width:], field[:width])
            other = lax.ppermute(mine, "lat", [(0, 1), (1, 0)])
            below = jnp.concatenate([field, other], axis=0)
            above = jnp.concatenate([other, field], axis=0)
            return jnp.where(place == 0, below, above)
        before = self.shift_lat(field[-width:], 1)
        after = self.shift_lat(field[:width], -1)
        before = jnp.where(place == 0, outside, before)
        after = jnp.where(place == self.lat - 1, outside, after)
        return jnp.concatenate([before, field, after], axis=0)

    def sum_all(self, rows, beside):
        lon = lax.axis_index("lon")
        lat = lax.axis_index("lat")
        bits = [(1 << bit, 0) for bit in range(self.lon.bit_length() - 1)]
        bits = bits[:1] + [(0, 1 << bit) for bit in range(self.lat.bit_length() - 1)] + bits[1:]

        def code(group):
            total = jnp.int32(0)
            for index, (lon_bit, lat_bit) in enumerate(group):
                held = (lon // lon_bit) % 2 if lon_bit else (lat // lat_bit) % 2
                total = total + held * (1 << index)
            return total

        def merged(group, choice):
            lon_bits = sum(bit[0] for index, bit in enumerate(group) if choice >> index & 1)
            lat_bits = sum(bit[1] for index, bit in enumerate(group) if choice >> index & 1)
            return lon_bits, lat_bits

        def scatter(values, group):
            count = 1 << len(group)
            pieces = values.reshape(count, -1, values.shape[1])
            here = code(group)
            total = lax.dynamic_index_in_dim(pieces, here, 0, False).astype(F32)
            for choice in range(1, count):
                sent = lax.dynamic_index_in_dim(pieces, here ^ choice, 0, False)
                total = total + self.swap(sent, *merged(group, choice)).astype(F32)
            return total.astype(BF16)

        def exchange(values, group):
            total = values.astype(F32)
            for choice in range(1, 1 << len(group)):
                total = total + self.swap(values, *merged(group, choice)).astype(F32)
            return total.astype(BF16)

        def gather(values, group):
            count = 1 << len(group)
            pieces = [values]
            for choice in range(1, count):
                pieces.append(self.swap(values, *merged(group, choice)))
            stack = jnp.stack(pieces)
            here = code(group)
            ordered = [
                lax.dynamic_index_in_dim(stack, here ^ place, 0, False) for place in range(count)
            ]
            return jnp.concatenate(ordered, axis=0)

        pair, quad, rest = bits[:1], bits[1:3], bits[3:]
        values = scatter(scatter(rows, pair), quad)
        while rest:
            values = exchange(values, rest[:2])
            rest = rest[2:]
        values = gather(values, quad)
        values, beside = lax.optimization_barrier((values, beside))
        return code(pair), values, self.swap(values, *pair[0]), beside


def on_device(links, state, land_sea, cotangent, *params):
    dw_kernel, weight_in = params[0], params[4]
    height, breadth, channels = state.shape
    hidden_units = weight_in.shape[2]
    groups = hidden_units // channels
    grad_norm = 1.0 / math.sqrt(links.lat * height * links.lon * breadth)
    lat = lax.axis_index("lat")
    sides = 1 if links.lat == 2 else 2
    window_rows = height + sides * WIDE
    first_rows = height + sides * NARROW
    second_rows = height + sides * MARGIN

    def start(margin):
        skipped = WIDE - margin
        return lat * skipped if sides == 1 else jnp.int32(skipped)

    vmem = pl.BlockSpec(memory_space=pltpu.VMEM)
    smem = pl.BlockSpec(memory_space=pltpu.SMEM)
    tile = (height, breadth, channels)
    coded, edges = pl.pallas_call(
        code_kernel,
        out_shape=(
            jax.ShapeDtypeStruct(tile, BF16),
            jax.ShapeDtypeStruct((sides, WIDE, 2 * breadth, channels), BF16),
        ),
        in_specs=[smem, vmem, vmem, vmem],
        out_specs=(vmem, vmem),
    )(lat.reshape(1), state, land_sea.T, cotangent)
    if sides == 1:
        pieces = links.swap(edges, 0, 1)
        places = [(1 - lat) * height]
    else:
        outside = jnp.concatenate(
            [jnp.zeros((1, breadth, 1), BF16), jnp.full((1, breadth, 1), LAND, BF16)], axis=1
        )
        above = jnp.where(lat == 0, outside, links.shift_lat(edges[0], 1))
        below = jnp.where(lat == links.lat - 1, outside, links.shift_lat(edges[1], -1))
        pieces = jnp.stack([above, below])
        places = [jnp.int32(0), jnp.int32(WIDE + height)]

    def edge(tile_cols):
        own = jnp.concatenate([state[:, tile_cols[0]], coded[:, tile_cols[1]]], axis=1)
        ends = [
            jnp.concatenate(
                [piece[:, :breadth][:, tile_cols[0]], piece[:, breadth:][:, tile_cols[1]]], axis=1
            )
            for piece in pieces
        ]
        if sides == 2:
            return jnp.concatenate([ends[0], own, ends[1]], axis=0)
        after = jnp.concatenate([own, ends[0]], axis=0)
        before = jnp.concatenate([ends[0], own], axis=0)
        return jnp.where(lat == 0, after, before)

    west = links.shift_lon(edge((slice(-WIDE, None), slice(-NARROW, None))), 1)
    east = links.shift_lon(edge((slice(WIDE), slice(NARROW))), -1)
    starts = jnp.stack([start(0), start(MARGIN), start(NARROW), *places]).astype(jnp.int32)
    state_pitch, field_pitch, inner_pitch = (
        round_up(breadth + size, 8) for size in (STATE_AT + WIDE, FIELD_AT + NARROW, NARROW)
    )

    padded_rows = window_rows + 2 * MARGIN
    all_cells = second_rows * inner_pitch
    layer_rows = round_up(2 * hidden_units + TAPS + 5 + groups, 4 * 16)
    small_rows = BLOCKS * (layer_rows - 2 * hidden_units)
    grad_rows = BLOCKS * layer_rows
    own_rows = (window_rows, breadth)
    scratch = [
        pltpu.VMEM((padded_rows, state_pitch, channels), F32),
        pltpu.VMEM((padded_rows, field_pitch, channels), F32),
        pltpu.VMEM((BLOCKS, TAPS, channels), F32),
        pltpu.VMEM((padded_rows, field_pitch, channels), F32),
        pltpu.VMEM((padded_rows, inner_pitch, channels), F32),
        pltpu.VMEM((window_rows, inner_pitch, channels), F32),
        pltpu.VMEM(own_rows + (channels,), F32),
        pltpu.VMEM(own_rows + (channels,), F32),
        pltpu.VMEM(own_rows + (channels,), F32),
        pltpu.VMEM(own_rows + (hidden_units,), F32),
        pltpu.VMEM(own_rows + (hidden_units,), BF16),
        pltpu.VMEM((height, breadth, hidden_units), BF16),
        pltpu.VMEM(own_rows + (channels,), BF16),
        pltpu.VMEM(tile, BF16),
        pltpu.VMEM(tile, F32),
        pltpu.VMEM((all_cells, hidden_units), BF16),
        pltpu.VMEM((all_cells, hidden_units), BF16),
        pltpu.VMEM((all_cells, channels), BF16),
        pltpu.VMEM((all_cells, channels), BF16),
        pltpu.VMEM((BLOCKS, 5, 8, channels), F32),
        pltpu.VMEM((BLOCKS, 8, hidden_units), F32),
        pltpu.VMEM((small_rows, channels), F32),
    ]
    sizes = (height, breadth, first_rows, second_rows, window_rows)
    taps_in = dw_kernel.reshape(BLOCKS, TAPS, channels)
    output, grad_mixed, masked, grads = pl.pallas_call(
        functools.partial(tile_kernel, sizes),
        out_shape=(
            jax.ShapeDtypeStruct(tile, BF16),
            jax.ShapeDtypeStruct(tile, BF16),
            jax.ShapeDtypeStruct(tile, BF16),
            jax.ShapeDtypeStruct((grad_rows, channels), BF16),
        ),
        in_specs=[smem] + [vmem] * 14,
        out_specs=(vmem,) * 4,
        scratch_shapes=scratch,
        compiler_params=pltpu.CompilerParams(vmem_limit_bytes=48 * 1024 * 1024),
        cost_estimate=pl.CostEstimate(
            flops=20 * all_cells * channels * hidden_units,
            bytes_accessed=4 * height * breadth * channels * 4,
            transcendentals=0,
        ),
    )(starts, state, coded, pieces, west, east, taps_in, *params[1:])

    before = links.shift_lon(grad_mixed[:, -MARGIN:], 1)
    after = links.shift_lon(grad_mixed[:, :MARGIN], -1)
    beside = jnp.concatenate([before, grad_mixed, after], axis=1)
    spread = links.extend_lat(beside, MARGIN, jnp.zeros((1, 1, 1), BF16))
    if sides == 1:
        empty = jnp.zeros((MARGIN,) + spread.shape[1:], BF16)
        first = jnp.concatenate([empty, spread], axis=0)
        last = jnp.concatenate([spread, empty], axis=0)
        spread = jnp.where(lat == 0, first, last)
    pitch = round_up(spread.shape[1], 8)
    spread = jnp.pad(spread, ((0, 0), (0, pitch - spread.shape[1]), (0, 0)))
    grad_state = pl.pallas_call(
        state_kernel,
        out_shape=jax.ShapeDtypeStruct(tile, BF16),
        in_specs=[vmem] * 3,
        out_specs=vmem,
        scratch_shapes=[pltpu.VMEM(spread.shape, F32), pltpu.VMEM((TAPS, channels), F32)],
        compiler_params=pltpu.CompilerParams(vmem_limit_bytes=16 * 1024 * 1024),
        cost_estimate=pl.CostEstimate(
            flops=4_000_000_000, bytes_accessed=8_000_000, transcendentals=0
        ),
    )(spread, masked, taps_in[0])

    held, own, other, grad_state = links.sum_all(grads, grad_state)
    shapes = [(KSIZE, KSIZE, BLOCKS, channels)] + [member.shape for member in params[1:]]
    grad_kernel, *gradients = pl.pallas_call(
        functools.partial(gradient_kernel, grad_norm),
        out_shape=tuple(jax.ShapeDtypeStruct(shape, F32) for shape in shapes),
        in_specs=[smem, vmem, vmem],
        out_specs=(vmem,) * 9,
        compiler_params=pltpu.CompilerParams(vmem_limit_bytes=8 * 1024 * 1024),
    )(held.reshape(1), own, other)
    return (output, grad_state, grad_kernel.transpose(2, 0, 1, 3), *gradients)


def solution(mesh):
    tile = P("lat", "lon", None)
    placed = (tile, P("lat", "lon"), tile) + (P(),) * 9
    return jax.shard_map(
        functools.partial(on_device, Links(mesh)),
        mesh=mesh,
        in_specs=placed,
        out_specs=(tile, tile) + (P(),) * 9,
        check_vma=False,
    )
```

```python
import functools
import math

import jax
import jax.numpy as jnp
from jax import lax
from jax.experimental import pallas as pl
from jax.experimental.pallas import tpu as pltpu
from jax.sharding import PartitionSpec as P

KSIZE = 7
MARGIN = KSIZE // 2
TAPS = KSIZE * KSIZE
BLOCKS = 2
EPS_NORM = 1e-06
INV_ROOT_TWO = 0.7071067811865476
INV_ROOT_TWO_PI = 0.3989422804014327
LAND = 1024.0
LAND_BOUND = 512.0
F32 = jnp.float32
BF16 = jnp.bfloat16
FIRST_STEP = 19
SECOND_STEP = 17
BACK_STEP = 45
TAP_STEP = 9
STATE_AT = 11
FIELD_AT = 8
INNER_AT = 3
WIDE = 3 * MARGIN
NARROW = 2 * MARGIN


def divisor(size, most):
    return max(step for step in range(1, most + 1) if size % step == 0)


def round_up(size, unit):
    return (size + unit - 1) // unit * unit


def pack_rows(above, below):
    shape = (above.shape[0] // 8, 8, above.shape[1])
    return jnp.concatenate([above.reshape(shape), below.reshape(shape)], axis=1).astype(BF16)


def conv_rows(source, base, first, count, width, kernel_ref, flip):
    pairs = (count + 1) // 2
    sums = [[None, None] for _ in range(pairs)]
    channels = source.shape[2]
    for tap_col in range(KSIZE):
        parts = [None] * pairs
        taps = []
        for tap_row in range(KSIZE):
            index = tap_row * KSIZE + tap_col
            tap = kernel_ref[pl.ds(TAPS - 1 - index if flip else index, 1), :]
            taps.append(jnp.broadcast_to(tap, (16, channels)).astype(BF16)[None])
        above = source[base, pl.ds(first + tap_col, width), :]
        for row in range(2 * pairs + KSIZE - 2):
            below = source[base + row + 1, pl.ds(first + tap_col, width), :]
            both = pack_rows(above, below)
            above = below
            for tap_row in range(row % 2, KSIZE, 2):
                out = (row - tap_row) // 2
                if 0 <= out < pairs:
                    term = both * taps[tap_row]
                    parts[out] = term if parts[out] is None else parts[out] + term
        for out in range(pairs):
            for side in range(2):
                value = parts[out].astype(F32)[:, 8 * side : 8 * side + 8]
                old = sums[out][side]
                sums[out][side] = value if old is None else old + value
    rows = [sums[row // 2][row % 2].reshape(width, channels) for row in range(count)]
    return jnp.concatenate(rows, axis=0)


def normal_parts(hidden):
    cumulative = 0.5 + 0.5 * lax.erf(hidden * INV_ROOT_TWO)
    return cumulative, jnp.exp(-0.5 * hidden * hidden)


def fold(values):
    return jnp.sum(values.reshape(values.shape[0] // 8, 8, values.shape[1]), axis=0)


def normalise(mixed):
    center = mixed - jnp.mean(mixed, axis=-1, keepdims=True)
    inverse = lax.rsqrt(jnp.mean(center * center, axis=-1, keepdims=True) + EPS_NORM)
    return center * inverse, inverse


def normalise_back(grad, normed, inverse):
    return inverse * (
        grad
        - jnp.mean(grad, axis=-1, keepdims=True)
        - normed * jnp.mean(grad * normed, axis=-1, keepdims=True)
    )


def rows_of(ref, base, first, count, width):
    return jnp.concatenate(
        [ref[base + row, pl.ds(first, width), :] for row in range(count)], axis=0
    )


CONTRACT_COLS = (((1,), (1,)), ((), ()))
CONTRACT_ROWS = (((0,), (0,)), ((), ()))


def dot(left, right):
    return jnp.dot(left, right, preferred_element_type=F32)


def dot_cols(left, right):
    return lax.dot_general(left, right, CONTRACT_COLS, preferred_element_type=F32)


def dot_rows(left, right):
    return lax.dot_general(left, right, CONTRACT_ROWS, preferred_element_type=F32)


def tap_sums(grad_ref, grad_row, grad_col, field_ref, field_row, field_col, height, width, out):
    rows = divisor(height, TAP_STEP)
    pairs = (rows + 1) // 2
    for cols in ((0, 1, 2, 3), (4, 5, 6)):

        def advance(step, sums):
            sums = list(sums)
            at = step * rows
            grads = [grad_ref[grad_row + at + row, pl.ds(grad_col, width), :] for row in range(rows)]
            grads += [jnp.zeros_like(grads[0])] * (2 * pairs - rows)
            grads = [pack_rows(grads[2 * pair], grads[2 * pair + 1]) for pair in range(pairs)]
            for place, tap_col in enumerate(cols):
                spots = pl.ds(field_col + tap_col, width)
                parts = [None] * KSIZE
                above = field_ref[field_row + at, spots, :]
                for row in range(2 * pairs + KSIZE - 2):
                    below = field_ref[field_row + at + row + 1, spots, :]
                    both = pack_rows(above, below)
                    above = below
                    for tap_row in range(row % 2, KSIZE, 2):
                        pair = (row - tap_row) // 2
                        if 0 <= pair < pairs:
                            term = grads[pair] * both
                            old = parts[tap_row]
                            parts[tap_row] = term if old is None else old + term
                for tap_row in range(KSIZE):
                    part = parts[tap_row]
                    total = part[0]
                    for group in range(1, part.shape[0]):
                        total = total + part[group]
                    index = place * KSIZE + tap_row
                    sums[index] = sums[index] + fold(total.astype(F32))
            return tuple(sums)

        zeros = tuple(jnp.zeros((8, grad_ref.shape[2]), F32) for _ in range(KSIZE * len(cols)))
        sums = lax.fori_loop(0, height // rows, advance, zeros)
        for place, tap_col in enumerate(cols):
            for tap_row in range(KSIZE):
                total = jnp.sum(sums[place * KSIZE + tap_row], axis=0, keepdims=True)
                out[pl.ds(tap_row * KSIZE + tap_col, 1), :] = total


def tile_kernel(
    sizes,
    starts,
    state_tile,
    coded_tile,
    lat_pieces,
    west,
    east,
    dw_in,
    conv_bias,
    norm_gain,
    norm_bias,
    weight_in,
    bias_in,
    weight_out,
    bias_out,
    layer_scale,
    output,
    mixed_out,
    masked_out,
    grads_out,
    state,
    coded,
    kernels,
    field,
    inner,
    result,
    normed_own,
    inverse_own,
    branch_own,
    slope_own,
    active_own,
    hidden_own,
    lifted_own,
    branch_grad_own,
    mixed_own,
    active_all,
    hidden_all,
    lifted_all,
    branch_grad_all,
    sums,
    hidden_sums,
    taps,
):
    height, breadth, first_rows, second_rows, window_rows = sizes
    channels = state.shape[2]
    own_start = starts[0]
    second_start = starts[1]
    first_start = starts[2]
    first_width = field.shape[1]
    second_width = inner.shape[1]
    pad = MARGIN

    for ref in (state, coded, field, inner):
        ref[pl.ds(0, pad)] = jnp.zeros((pad,) + ref.shape[1:], F32)
        below = ref.shape[0] - pad - window_rows
        ref[pl.ds(pad + window_rows, below)] = jnp.zeros((below,) + ref.shape[1:], F32)
    state[pl.ds(pad, window_rows)] = jnp.zeros((window_rows,) + state.shape[1:], F32)
    coded[pl.ds(pad, window_rows)] = jnp.zeros((window_rows,) + coded.shape[1:], F32)

    def place(window, at, values):
        window[at[0], pl.ds(at[1], values.shape[1]), :] = values.astype(F32)

    place(state, (pl.ds(pad + own_start, height), STATE_AT), state_tile[...])
    place(coded, (pl.ds(pad + own_start, height), FIELD_AT), coded_tile[...])
    for index in range(lat_pieces.shape[0]):
        spots = pl.ds(pad + starts[3 + index], WIDE)
        place(state, (spots, STATE_AT), lat_pieces[index, :, :breadth])
        place(coded, (spots, FIELD_AT), lat_pieces[index, :, breadth:])
    spots = pl.ds(pad, window_rows)
    place(state, (spots, STATE_AT - WIDE), west[:, :WIDE])
    place(state, (spots, STATE_AT + breadth), east[:, :WIDE])
    place(coded, (spots, FIELD_AT - NARROW), west[:, WIDE:])
    place(coded, (spots, FIELD_AT + breadth), east[:, WIDE:])
    kernels[...] = dw_in[...].astype(F32)
    sums[...] = jnp.zeros_like(sums)
    hidden_sums[...] = jnp.zeros_like(hidden_sums)

    def param(ref, layer):
        return ref[pl.ds(layer, 1), :]

    first_step = divisor(first_rows, FIRST_STEP)

    def forward_first(step, carry):
        row = first_start + step * first_step
        cells = first_step * first_width
        mixed = conv_rows(state, row, 0, first_step, first_width, kernels.at[0], False)
        normed, inverse = normalise(mixed + param(conv_bias, 0))
        lifted = (normed * param(norm_gain, 0) + param(norm_bias, 0)).astype(BF16)
        hidden = dot(lifted, weight_in[0]) + param(bias_in, 0)
        cumulative, bell = normal_parts(hidden)
        active = hidden * cumulative
        branch = dot(active.astype(BF16), weight_out[0]) + param(bias_out, 0)
        center = rows_of(state, row + pad, MARGIN, first_step, first_width)
        mark = rows_of(coded, row + pad, 0, first_step, first_width)
        value = jnp.where(mark < LAND_BOUND, center + param(layer_scale, 0) * branch, 0.0)
        value = value.reshape(first_step, first_width, channels)

        for index in range(first_step):
            field[row + pad + index] = value[index]

        def own(values):
            shape = (first_step, first_width, values.shape[1])
            return values.reshape(shape)[:, FIELD_AT : FIELD_AT + breadth]

        slope = own(cumulative) + own(hidden) * (own(bell) * INV_ROOT_TWO_PI)
        spots = pl.ds(row, first_step)
        slope_own[spots] = slope
        active_own[spots] = own(active).astype(BF16)
        normed_own[spots] = own(normed)
        inverse_own[spots] = own(jnp.broadcast_to(inverse, normed.shape))
        branch_own[spots] = own(branch)
        lifted_own[spots] = own(normed * param(norm_gain, 0) + param(norm_bias, 0)).astype(BF16)
        return carry

    lax.fori_loop(0, first_rows // first_step, forward_first, 0)

    second_step = divisor(second_rows, SECOND_STEP)

    def both_second(step, carry):
        row = second_start + step * second_step
        cells = second_step * second_width
        shift = FIELD_AT - INNER_AT
        mixed = conv_rows(
            field, row, shift - MARGIN, second_step, second_width, kernels.at[1], False
        )
        normed, inverse = normalise(mixed + param(conv_bias, 1))
        lifted = normed * param(norm_gain, 1) + param(norm_bias, 1)
        hidden = dot(lifted.astype(BF16), weight_in[1]) + param(bias_in, 1)
        cumulative, bell = normal_parts(hidden)
        active = (hidden * cumulative).astype(BF16)
        branch = dot(active, weight_out[1]) + param(bias_out, 1)
        center = rows_of(field, row + pad, shift, second_step, second_width)
        mark = rows_of(coded, row + pad, shift, second_step, second_width)
        ocean = mark < LAND_BOUND
        value = jnp.where(ocean, center + param(layer_scale, 1) * branch, 0.0)
        value = value.reshape(second_step, second_width, channels)
        masked = jnp.where(ocean, mark, 0.0)
        grad_branch = (masked * param(layer_scale, 1)).astype(BF16)
        grad_active = dot_cols(grad_branch, weight_out[1])
        slope = cumulative + hidden * (bell * INV_ROOT_TWO_PI)
        grad_hidden = (grad_active * slope).astype(BF16)
        grad_lifted = dot_cols(grad_hidden, weight_in[1])
        grad_mixed = normalise_back(grad_lifted * param(norm_gain, 1), normed, inverse)
        grad_mixed = grad_mixed.reshape(second_step, second_width, channels)
        for index in range(second_step):
            result[row + index] = value[index]
            inner[row + pad + index] = grad_mixed[index]

        shape = (second_step, second_width, channels)
        row_of = lax.broadcasted_iota(jnp.int32, shape, 0) + (row - own_start)
        col_of = lax.broadcasted_iota(jnp.int32, shape, 1) - INNER_AT
        inside = (row_of >= 0) & (row_of < height) & (col_of >= 0) & (col_of < breadth)
        inside = jnp.where(inside, 1.0, 0.0).astype(F32).reshape(cells, channels)
        own_lifted = grad_lifted * inside
        own_branch = grad_branch.astype(F32) * inside
        sums[1, 0] += fold(masked * branch * inside)
        sums[1, 1] += fold(own_branch)
        sums[1, 2] += fold(own_lifted * normed)
        sums[1, 3] += fold(own_lifted)
        wide = jnp.concatenate([inside] * (hidden.shape[1] // channels), axis=1)
        hidden_sums[1] += fold(grad_hidden.astype(F32) * wide)
        spots = pl.ds(pl.multiple_of(step * cells, cells), cells)
        active_all[spots] = active
        hidden_all[spots] = grad_hidden
        lifted_all[spots] = (lifted * inside).astype(BF16)
        branch_grad_all[spots] = own_branch.astype(BF16)
        return carry

    lax.fori_loop(0, second_rows // second_step, both_second, 0)

    back_step = divisor(height, BACK_STEP)

    def backward_first(step, carry):
        row = own_start + step * back_step
        cells = back_step * breadth
        mark = rows_of(coded, row + pad, FIELD_AT, back_step, breadth)
        ocean = mark < LAND_BOUND
        masked_next = jnp.where(ocean, mark, 0.0)
        spread = conv_rows(inner, row, 0, back_step, breadth, kernels.at[1], True)
        masked = jnp.where(ocean, masked_next + spread, 0.0)
        grad_branch = (masked * param(layer_scale, 0)).astype(BF16)
        grad_active = dot_cols(grad_branch, weight_out[0])
        slope = slope_own[pl.ds(row, back_step)].reshape(cells, grad_active.shape[1])
        grad_hidden = (grad_active * slope).astype(BF16)
        grad_lifted = dot_cols(grad_hidden, weight_in[0])
        normed = normed_own[pl.ds(row, back_step)].reshape(cells, channels)
        inverse = inverse_own[pl.ds(row, back_step)].reshape(cells, channels)
        grad_mixed = normalise_back(grad_lifted * param(norm_gain, 0), normed, inverse)
        branch = branch_own[pl.ds(row, back_step)].reshape(cells, channels)
        sums[0, 0] += fold(masked * branch)
        sums[0, 1] += fold(grad_branch.astype(F32))
        sums[0, 2] += fold(grad_lifted * normed)
        sums[0, 3] += fold(grad_lifted)
        sums[0, 4] += fold(grad_mixed)
        hidden_sums[0] += fold(grad_hidden.astype(F32))
        inner_rows = rows_of(inner, row + pad, INNER_AT, back_step, breadth)
        sums[1, 4] += fold(inner_rows)
        tile = pl.ds(step * back_step, back_step)
        shape = (back_step, breadth, channels)
        grad_mixed = grad_mixed.reshape(shape)
        mixed_own[tile] = grad_mixed
        mixed_out[tile] = grad_mixed.astype(BF16)
        masked_out[tile] = masked.reshape(shape).astype(BF16)
        hidden_own[tile] = grad_hidden.reshape(back_step, breadth, grad_hidden.shape[1])
        branch_grad_own[tile] = grad_branch.reshape(shape)
        value = rows_of(result, row, INNER_AT, back_step, breadth)
        output[tile] = value.reshape(shape).astype(BF16)
        return carry

    lax.fori_loop(0, height // back_step, backward_first, 0)

    hidden_units = weight_in.shape[2]
    groups = hidden_units // channels
    tile = pl.ds(own_start, height)
    cells = height * breadth

    def flat(ref, spots):
        return ref[spots].reshape(cells, ref.shape[2])

    operands = (
        (
            flat(lifted_own, tile),
            flat(hidden_own, pl.ds(0, height)),
            flat(active_own, tile),
            flat(branch_grad_own, pl.ds(0, height)),
        ),
        (lifted_all[...], hidden_all[...], active_all[...], branch_grad_all[...]),
    )
    for layer, (lifted, grad_hidden, active, grad_branch) in enumerate(operands):
        at = layer * (grads_out.shape[0] // BLOCKS)
        grad_in = dot_rows(lifted, grad_hidden)
        for group in range(groups):
            grads_out[pl.ds(at + group * channels, channels), :] = grad_in[
                :, group * channels : (group + 1) * channels
            ].astype(BF16)
        grad_out = dot_rows(grad_branch, active)
        for group in range(groups):
            grads_out[pl.ds(at + hidden_units + group * channels, channels), :] = grad_out[
                :, group * channels : (group + 1) * channels
            ].T.astype(BF16)

    taps[...] = jnp.zeros_like(taps)
    for layer in range(BLOCKS):
        base = layer * (taps.shape[0] // BLOCKS)
        if layer:
            tap_sums(
                inner,
                own_start + pad,
                INNER_AT,
                field,
                own_start,
                FIELD_AT - MARGIN,
                height,
                breadth,
                taps.at[pl.ds(base, TAPS)],
            )
        else:
            tap_sums(
                mixed_own,
                0,
                0,
                state,
                own_start,
                STATE_AT - MARGIN,
                height,
                breadth,
                taps.at[pl.ds(base, TAPS)],
            )
        for member in range(5):
            taps[pl.ds(base + TAPS + member, 1), :] = jnp.sum(
                sums[layer, member], axis=0, keepdims=True
            )
        hidden_total = jnp.sum(hidden_sums[layer], axis=0, keepdims=True)
        for group in range(groups):
            taps[pl.ds(base + TAPS + 5 + group, 1), :] = hidden_total[
                :, group * channels : (group + 1) * channels
            ]
    small = taps.shape[0] // BLOCKS
    for layer in range(BLOCKS):
        at = layer * (grads_out.shape[0] // BLOCKS) + 2 * hidden_units
        grads_out[pl.ds(at, small), :] = taps[pl.ds(layer * small, small), :].astype(BF16)


def state_kernel(window, masked, dw_in, out, wide, kernels):
    height, breadth, channels = masked.shape
    wide[...] = window[...].astype(F32)
    kernels[...] = dw_in[...].astype(F32)

    rows = divisor(height, BACK_STEP)

    def advance(step, carry):
        row = step * rows
        spread = conv_rows(wide, row, 0, rows, breadth, kernels, True)
        tile = pl.ds(row, rows)
        shape = (rows, breadth, channels)
        out[tile] = (masked[tile].astype(F32) + spread.reshape(shape)).astype(BF16)
        return carry

    lax.fori_loop(0, height // rows, advance, 0)


def code_kernel(lat, state, land_sea, cotangent, coded, edge):
    height, breadth, channels = state.shape
    ocean = jnp.where(land_sea[...] != 0, 1.0, 0.0).astype(F32)
    for row in range(height):
        wide = jnp.broadcast_to(ocean[:, row : row + 1], (breadth, channels))
        coded[row] = jnp.where(wide > 0.5, cotangent[row].astype(F32), LAND).astype(BF16)
    for side in range(edge.shape[0]):
        first = (1 - lat[0]) * (height - WIDE) if edge.shape[0] == 1 else (1 - side) * (height - WIDE)
        edge[side, :, :breadth] = state[pl.ds(first, WIDE)]
        edge[side, :, breadth:] = coded[pl.ds(first, WIDE)]


def gradient_kernel(grad_norm, held, own, other, *outs):
    kernel, conv_bias, gain, shift, first, first_bias, second, second_bias, scale = outs
    channels = own.shape[1]
    units = second.shape[1]
    groups = units // channels

    def unpack(rows, layer):
        for group in range(groups):
            spots = pl.ds(group * channels, channels)
            first[layer, :, spots] = rows[spots].astype(F32) * grad_norm
        second[layer] = rows[pl.ds(units, units)].astype(F32) * grad_norm
        small = rows[pl.ds(2 * units, rows.shape[0] - 2 * units)].astype(F32) * grad_norm
        for index in range(TAPS):
            kernel[index // KSIZE, index % KSIZE, layer : layer + 1] = small[index : index + 1]
        for member, out in enumerate((scale, second_bias, gain, shift, conv_bias)):
            out[layer : layer + 1] = small[TAPS + member : TAPS + member + 1]
        for group in range(groups):
            row = TAPS + 5 + group
            first_bias[layer : layer + 1, pl.ds(group * channels, channels)] = small[row : row + 1]

    @pl.when(held[0] == 0)
    def _():
        unpack(own, 0)
        unpack(other, 1)

    @pl.when(held[0] != 0)
    def _():
        unpack(own, 1)
        unpack(other, 0)


class Links:
    def __init__(self, mesh):
        self.lon = mesh.shape["lon"]
        self.lat = mesh.shape["lat"]
        self.axes = ("lon", "lat")

    def shift_lon(self, values, by):
        pairs = [(place, (place + by) % self.lon) for place in range(self.lon)]
        return lax.ppermute(values, "lon", pairs)

    def shift_lat(self, values, by):
        pairs = [
            (place, place + by) for place in range(self.lat) if 0 <= place + by < self.lat
        ]
        return lax.ppermute(values, "lat", pairs)

    def swap(self, values, lon_bits, lat_bits):
        pairs = []
        for lon in range(self.lon):
            for lat in range(self.lat):
                there = (lon ^ lon_bits) * self.lat + (lat ^ lat_bits)
                pairs.append((lon * self.lat + lat, there))
        return lax.ppermute(values, self.axes, pairs)

    def extend_lat(self, field, width, outside):
        place = lax.axis_index("lat")
        if self.lat == 2:
            mine = jnp.where(place == 0, field[-width:], field[:width])
            other = lax.ppermute(mine, "lat", [(0, 1), (1, 0)])
            below = jnp.concatenate([field, other], axis=0)
            above = jnp.concatenate([other, field], axis=0)
            return jnp.where(place == 0, below, above)
        before = self.shift_lat(field[-width:], 1)
        after = self.shift_lat(field[:width], -1)
        before = jnp.where(place == 0, outside, before)
        after = jnp.where(place == self.lat - 1, outside, after)
        return jnp.concatenate([before, field, after], axis=0)

    def sum_all(self, rows, beside):
        lon = lax.axis_index("lon")
        lat = lax.axis_index("lat")
        bits = [(1 << bit, 0) for bit in range(self.lon.bit_length() - 1)]
        bits = bits[:1] + [(0, 1 << bit) for bit in range(self.lat.bit_length() - 1)] + bits[1:]

        def code(group):
            total = jnp.int32(0)
            for index, (lon_bit, lat_bit) in enumerate(group):
                held = (lon // lon_bit) % 2 if lon_bit else (lat // lat_bit) % 2
                total = total + held * (1 << index)
            return total

        def merged(group, choice):
            lon_bits = sum(bit[0] for index, bit in enumerate(group) if choice >> index & 1)
            lat_bits = sum(bit[1] for index, bit in enumerate(group) if choice >> index & 1)
            return lon_bits, lat_bits

        def scatter(values, group):
            count = 1 << len(group)
            pieces = values.reshape(count, -1, values.shape[1])
            here = code(group)
            total = lax.dynamic_index_in_dim(pieces, here, 0, False).astype(F32)
            for choice in range(1, count):
                sent = lax.dynamic_index_in_dim(pieces, here ^ choice, 0, False)
                total = total + self.swap(sent, *merged(group, choice)).astype(F32)
            return total.astype(BF16)

        def exchange(values, group):
            total = values.astype(F32)
            for choice in range(1, 1 << len(group)):
                total = total + self.swap(values, *merged(group, choice)).astype(F32)
            return total.astype(BF16)

        def gather(values, group):
            count = 1 << len(group)
            pieces = [values]
            for choice in range(1, count):
                pieces.append(self.swap(values, *merged(group, choice)))
            stack = jnp.stack(pieces)
            here = code(group)
            ordered = [
                lax.dynamic_index_in_dim(stack, here ^ place, 0, False) for place in range(count)
            ]
            return jnp.concatenate(ordered, axis=0)

        pair, quad, rest = bits[:1], bits[1:3], bits[3:]
        values = scatter(scatter(rows, pair), quad)
        while rest:
            values = exchange(values, rest[:2])
            rest = rest[2:]
        values = gather(values, quad)
        values, beside = lax.optimization_barrier((values, beside))
        return code(pair), values, self.swap(values, *pair[0]), beside


def on_device(links, state, land_sea, cotangent, *params):
    dw_kernel, weight_in = params[0], params[4]
    height, breadth, channels = state.shape
    hidden_units = weight_in.shape[2]
    groups = hidden_units // channels
    grad_norm = 1.0 / math.sqrt(links.lat * height * links.lon * breadth)
    lat = lax.axis_index("lat")
    sides = 1 if links.lat == 2 else 2
    window_rows = height + sides * WIDE
    first_rows = height + sides * NARROW
    second_rows = height + sides * MARGIN

    def start(margin):
        skipped = WIDE - margin
        return lat * skipped if sides == 1 else jnp.int32(skipped)

    vmem = pl.BlockSpec(memory_space=pltpu.VMEM)
    smem = pl.BlockSpec(memory_space=pltpu.SMEM)
    tile = (height, breadth, channels)
    coded, edges = pl.pallas_call(
        code_kernel,
        out_shape=(
            jax.ShapeDtypeStruct(tile, BF16),
            jax.ShapeDtypeStruct((sides, WIDE, 2 * breadth, channels), BF16),
        ),
        in_specs=[smem, vmem, vmem, vmem],
        out_specs=(vmem, vmem),
    )(lat.reshape(1), state, land_sea.T, cotangent)
    if sides == 1:
        pieces = links.swap(edges, 0, 1)
        places = [(1 - lat) * height]
    else:
        outside = jnp.concatenate(
            [jnp.zeros((1, breadth, 1), BF16), jnp.full((1, breadth, 1), LAND, BF16)], axis=1
        )
        above = jnp.where(lat == 0, outside, links.shift_lat(edges[0], 1))
        below = jnp.where(lat == links.lat - 1, outside, links.shift_lat(edges[1], -1))
        pieces = jnp.stack([above, below])
        places = [jnp.int32(0), jnp.int32(WIDE + height)]

    def edge(tile_cols):
        own = jnp.concatenate([state[:, tile_cols[0]], coded[:, tile_cols[1]]], axis=1)
        ends = [
            jnp.concatenate(
                [piece[:, :breadth][:, tile_cols[0]], piece[:, breadth:][:, tile_cols[1]]], axis=1
            )
            for piece in pieces
        ]
        if sides == 2:
            return jnp.concatenate([ends[0], own, ends[1]], axis=0)
        after = jnp.concatenate([own, ends[0]], axis=0)
        before = jnp.concatenate([ends[0], own], axis=0)
        return jnp.where(lat == 0, after, before)

    west = links.shift_lon(edge((slice(-WIDE, None), slice(-NARROW, None))), 1)
    east = links.shift_lon(edge((slice(WIDE), slice(NARROW))), -1)
    starts = jnp.stack([start(0), start(MARGIN), start(NARROW), *places]).astype(jnp.int32)
    state_pitch, field_pitch, inner_pitch = (
        round_up(breadth + size, 8) for size in (STATE_AT + WIDE, FIELD_AT + NARROW, NARROW)
    )

    padded_rows = window_rows + 2 * MARGIN + 1
    all_cells = second_rows * inner_pitch
    layer_rows = round_up(2 * hidden_units + TAPS + 5 + groups, 4 * 16)
    small_rows = BLOCKS * (layer_rows - 2 * hidden_units)
    grad_rows = BLOCKS * layer_rows
    own_rows = (window_rows, breadth)
    scratch = [
        pltpu.VMEM((padded_rows, state_pitch, channels), F32),
        pltpu.VMEM((padded_rows, field_pitch, channels), F32),
        pltpu.VMEM((BLOCKS, TAPS, channels), F32),
        pltpu.VMEM((padded_rows, field_pitch, channels), F32),
        pltpu.VMEM((padded_rows, inner_pitch, channels), F32),
        pltpu.VMEM((window_rows, inner_pitch, channels), F32),
        pltpu.VMEM(own_rows + (channels,), F32),
        pltpu.VMEM(own_rows + (channels,), F32),
        pltpu.VMEM(own_rows + (channels,), F32),
        pltpu.VMEM(own_rows + (hidden_units,), F32),
        pltpu.VMEM(own_rows + (hidden_units,), BF16),
        pltpu.VMEM((height, breadth, hidden_units), BF16),
        pltpu.VMEM(own_rows + (channels,), BF16),
        pltpu.VMEM(tile, BF16),
        pltpu.VMEM(tile, F32),
        pltpu.VMEM((all_cells, hidden_units), BF16),
        pltpu.VMEM((all_cells, hidden_units), BF16),
        pltpu.VMEM((all_cells, channels), BF16),
        pltpu.VMEM((all_cells, channels), BF16),
        pltpu.VMEM((BLOCKS, 5, 8, channels), F32),
        pltpu.VMEM((BLOCKS, 8, hidden_units), F32),
        pltpu.VMEM((small_rows, channels), F32),
    ]
    sizes = (height, breadth, first_rows, second_rows, window_rows)
    taps_in = dw_kernel.reshape(BLOCKS, TAPS, channels)
    output, grad_mixed, masked, grads = pl.pallas_call(
        functools.partial(tile_kernel, sizes),
        out_shape=(
            jax.ShapeDtypeStruct(tile, BF16),
            jax.ShapeDtypeStruct(tile, BF16),
            jax.ShapeDtypeStruct(tile, BF16),
            jax.ShapeDtypeStruct((grad_rows, channels), BF16),
        ),
        in_specs=[smem] + [vmem] * 14,
        out_specs=(vmem,) * 4,
        scratch_shapes=scratch,
        compiler_params=pltpu.CompilerParams(vmem_limit_bytes=48 * 1024 * 1024),
        cost_estimate=pl.CostEstimate(
            flops=20 * all_cells * channels * hidden_units,
            bytes_accessed=4 * height * breadth * channels * 4,
            transcendentals=0,
        ),
    )(starts, state, coded, pieces, west, east, taps_in, *params[1:])

    before = links.shift_lon(grad_mixed[:, -MARGIN:], 1)
    after = links.shift_lon(grad_mixed[:, :MARGIN], -1)
    beside = jnp.concatenate([before, grad_mixed, after], axis=1)
    spread = links.extend_lat(beside, MARGIN, jnp.zeros((1, 1, 1), BF16))
    if sides == 1:
        empty = jnp.zeros((MARGIN,) + spread.shape[1:], BF16)
        first = jnp.concatenate([empty, spread], axis=0)
        last = jnp.concatenate([spread, empty], axis=0)
        spread = jnp.where(lat == 0, first, last)
    pitch = round_up(spread.shape[1], 8)
    spread = jnp.pad(spread, ((0, 1), (0, pitch - spread.shape[1]), (0, 0)))
    grad_state = pl.pallas_call(
        state_kernel,
        out_shape=jax.ShapeDtypeStruct(tile, BF16),
        in_specs=[vmem] * 3,
        out_specs=vmem,
        scratch_shapes=[pltpu.VMEM(spread.shape, F32), pltpu.VMEM((TAPS, channels), F32)],
        compiler_params=pltpu.CompilerParams(vmem_limit_bytes=16 * 1024 * 1024),
        cost_estimate=pl.CostEstimate(
            flops=4_000_000_000, bytes_accessed=8_000_000, transcendentals=0
        ),
    )(spread, masked, taps_in[0])

    held, own, other, grad_state = links.sum_all(grads, grad_state)
    shapes = [(KSIZE, KSIZE, BLOCKS, channels)] + [member.shape for member in params[1:]]
    grad_kernel, *gradients = pl.pallas_call(
        functools.partial(gradient_kernel, grad_norm),
        out_shape=tuple(jax.ShapeDtypeStruct(shape, F32) for shape in shapes),
        in_specs=[smem, vmem, vmem],
        out_specs=(vmem,) * 9,
        compiler_params=pltpu.CompilerParams(vmem_limit_bytes=8 * 1024 * 1024),
    )(held.reshape(1), own, other)
    return (output, grad_state, grad_kernel.transpose(2, 0, 1, 3), *gradients)


def solution(mesh):
    tile = P("lat", "lon", None)
    placed = (tile, P("lat", "lon"), tile) + (P(),) * 9
    return jax.shard_map(
        functools.partial(on_device, Links(mesh)),
        mesh=mesh,
        in_specs=placed,
        out_specs=(tile, tile) + (P(),) * 9,
        check_vma=False,
    )
```

```python
import functools
import math

import jax
import jax.numpy as jnp
from jax import lax
from jax.experimental import pallas as pl
from jax.experimental.pallas import tpu as pltpu
from jax.sharding import PartitionSpec as P

KSIZE = 7
MARGIN = KSIZE // 2
TAPS = KSIZE * KSIZE
BLOCKS = 2
EPS_NORM = 1e-06
INV_ROOT_TWO = 0.7071067811865476
INV_ROOT_TWO_PI = 0.3989422804014327
LAND = 1024.0
LAND_BOUND = 512.0
F32 = jnp.float32
BF16 = jnp.bfloat16
FIRST_STEP = 19
SECOND_STEP = 17
BACK_STEP = 45
TAP_STEP = 9
STATE_AT = 11
FIELD_AT = 8
INNER_AT = 3
WIDE = 3 * MARGIN
NARROW = 2 * MARGIN


def divisor(size, most):
    return max(step for step in range(1, most + 1) if size % step == 0)


def round_up(size, unit):
    return (size + unit - 1) // unit * unit


def pack_rows(above, below):
    shape = (above.shape[0] // 8, 8, above.shape[1])
    return jnp.concatenate([above.reshape(shape), below.reshape(shape)], axis=1).astype(BF16)


def conv_rows(source, base, first, count, width, kernel_ref, flip):
    pairs = (count + 1) // 2
    sums = [[None, None] for _ in range(pairs)]
    channels = source.shape[2]
    for tap_col in range(KSIZE):
        parts = [None] * pairs
        taps = []
        for tap_row in range(KSIZE):
            index = tap_row * KSIZE + tap_col
            tap = kernel_ref[pl.ds(TAPS - 1 - index if flip else index, 1), :]
            taps.append(jnp.broadcast_to(tap, (16, channels)).astype(BF16)[None])
        above = source[base, pl.ds(first + tap_col, width), :]
        for row in range(2 * pairs + KSIZE - 2):
            below = source[base + row + 1, pl.ds(first + tap_col, width), :]
            both = pack_rows(above, below)
            above = below
            for tap_row in range(row % 2, KSIZE, 2):
                out = (row - tap_row) // 2
                if 0 <= out < pairs:
                    term = both * taps[tap_row]
                    parts[out] = term if parts[out] is None else parts[out] + term
        for out in range(pairs):
            for side in range(2):
                value = parts[out].astype(F32)[:, 8 * side : 8 * side + 8]
                old = sums[out][side]
                sums[out][side] = value if old is None else old + value
    rows = [sums[row // 2][row % 2].reshape(width, channels) for row in range(count)]
    return jnp.concatenate(rows, axis=0)


def normal_parts(hidden):
    cumulative = 0.5 + 0.5 * lax.erf(hidden * INV_ROOT_TWO)
    return cumulative, jnp.exp(-0.5 * hidden * hidden)


def fold(values):
    return jnp.sum(values.reshape(values.shape[0] // 8, 8, values.shape[1]), axis=0)


def normalise(mixed):
    center = mixed - jnp.mean(mixed, axis=-1, keepdims=True)
    inverse = lax.rsqrt(jnp.mean(center * center, axis=-1, keepdims=True) + EPS_NORM)
    return center * inverse, inverse


def normalise_back(grad, normed, inverse):
    return inverse * (
        grad
        - jnp.mean(grad, axis=-1, keepdims=True)
        - normed * jnp.mean(grad * normed, axis=-1, keepdims=True)
    )


def rows_of(ref, base, first, count, width):
    return jnp.concatenate(
        [ref[base + row, pl.ds(first, width), :] for row in range(count)], axis=0
    )


CONTRACT_COLS = (((1,), (1,)), ((), ()))
CONTRACT_ROWS = (((0,), (0,)), ((), ()))


def dot(left, right):
    return jnp.dot(left, right, preferred_element_type=F32)


def dot_cols(left, right):
    return lax.dot_general(left, right, CONTRACT_COLS, preferred_element_type=F32)


def dot_rows(left, right):
    return lax.dot_general(left, right, CONTRACT_ROWS, preferred_element_type=F32)


def tap_sums(grad_ref, grad_row, grad_col, field_ref, field_row, field_col, height, width, out):
    rows = divisor(height, TAP_STEP)
    pairs = (rows + 1) // 2
    for cols in ((0, 1, 2, 3), (4, 5, 6)):

        def advance(step, sums):
            sums = list(sums)
            at = step * rows
            grads = [grad_ref[grad_row + at + row, pl.ds(grad_col, width), :] for row in range(rows)]
            grads += [jnp.zeros_like(grads[0])] * (2 * pairs - rows)
            grads = [pack_rows(grads[2 * pair], grads[2 * pair + 1]) for pair in range(pairs)]
            for place, tap_col in enumerate(cols):
                spots = pl.ds(field_col + tap_col, width)
                parts = [None] * KSIZE
                above = field_ref[field_row + at, spots, :]
                for row in range(2 * pairs + KSIZE - 2):
                    below = field_ref[field_row + at + row + 1, spots, :]
                    both = pack_rows(above, below)
                    above = below
                    for tap_row in range(row % 2, KSIZE, 2):
                        pair = (row - tap_row) // 2
                        if 0 <= pair < pairs:
                            term = grads[pair] * both
                            old = parts[tap_row]
                            parts[tap_row] = term if old is None else old + term
                for tap_row in range(KSIZE):
                    part = parts[tap_row]
                    total = part[0]
                    for group in range(1, part.shape[0]):
                        total = total + part[group]
                    index = place * KSIZE + tap_row
                    sums[index] = sums[index] + fold(total.astype(F32))
            return tuple(sums)

        zeros = tuple(jnp.zeros((8, grad_ref.shape[2]), F32) for _ in range(KSIZE * len(cols)))
        sums = lax.fori_loop(0, height // rows, advance, zeros)
        for place, tap_col in enumerate(cols):
            for tap_row in range(KSIZE):
                total = jnp.sum(sums[place * KSIZE + tap_row], axis=0, keepdims=True)
                out[pl.ds(tap_row * KSIZE + tap_col, 1), :] = total


def fill_windows(sizes, starts, sources, state, coded, edges):
    height, breadth, window_rows = sizes
    state_tile, cotangent, land_sea, lat_pieces, within, across = sources
    channels = state.shape[2]
    pad = MARGIN
    own = pad + starts[0]
    lower = starts[3] == 0
    state[pl.ds(pad, window_rows)] = jnp.zeros((window_rows,) + state.shape[1:], F32)
    coded[pl.ds(pad, window_rows)] = jnp.zeros((window_rows,) + coded.shape[1:], F32)

    def spread(marks, column):
        return jnp.broadcast_to(marks[:, column : column + 1], (marks.shape[0], channels))

    state[pl.ds(own, height), pl.ds(STATE_AT, breadth), :] = state_tile[...].astype(F32)
    ocean = jnp.where(land_sea[...] != 0, 1.0, 0.0).astype(F32)
    for row in range(height):
        value = jnp.where(spread(ocean, row) > 0.5, cotangent[row].astype(F32), LAND)
        coded[own + row, pl.ds(FIELD_AT, breadth), :] = value

    sides = lat_pieces.shape[0]
    far, near = WIDE * breadth, MARGIN * breadth
    for side in range(sides):
        first = pad + starts[4 + side]
        closest = pad + starts[4 + sides + side]
        piece = lat_pieces[side].astype(F32)
        marks = piece[far + near : far + near + breadth]
        for row in range(WIDE):
            spots = pl.ds(row * breadth, breadth)
            state[first + row, pl.ds(STATE_AT, breadth), :] = lat_pieces[side, spots].astype(F32)
            value = jnp.where(spread(marks, row) > 0.5, 0.0, LAND)
            coded[first + row, pl.ds(FIELD_AT, breadth), :] = value
        for row in range(MARGIN):
            value = piece[far + row * breadth : far + (row + 1) * breadth]
            old = coded[closest + row, pl.ds(FIELD_AT, breadth), :]
            value = jnp.where(old > LAND_BOUND, LAND, value)
            coded[closest + row, pl.ds(FIELD_AT, breadth), :] = value

    group = WIDE + MARGIN

    def fill_columns(source, west):
        edges[...] = source[...].astype(F32)
        state_at = STATE_AT - WIDE if west else STATE_AT + breadth
        mark_at = FIELD_AT - NARROW if west else FIELD_AT + breadth
        value_at = FIELD_AT - MARGIN if west else FIELD_AT + breadth
        shown = slice(NARROW - MARGIN, NARROW) if west else slice(0, MARGIN)
        spans = [(own - pad, height, 0)] + [(starts[4 + side], WIDE, side + 1) for side in range(sides)]
        for first, count, place in spans:
            marks = edges[pl.ds(window_rows * group + place * 8, 8), :]
            for row in range(count):
                at = pad + first + row
                lines = (first + row) * group
                state[at, pl.ds(state_at, WIDE), :] = edges[pl.ds(lines, WIDE), :]
                mark = spread(marks, row)[:NARROW]
                coded[at, pl.ds(mark_at, NARROW), :] = jnp.where(mark > 0.5, 0.0, LAND)
                value = jnp.where(mark[shown] > 0.5, edges[pl.ds(lines + WIDE, MARGIN), :], LAND)
                coded[at, pl.ds(value_at, MARGIN), :] = value

    @pl.when(lower)
    def _():
        fill_columns(across, True)
        fill_columns(within, False)

    @pl.when(jnp.logical_not(lower))
    def _():
        fill_columns(within, True)
        fill_columns(across, False)


def tile_kernel(
    sizes,
    starts,
    state_tile,
    cotangent,
    land_sea,
    lat_pieces,
    within,
    across,
    dw_in,
    conv_bias,
    norm_gain,
    norm_bias,
    weight_in,
    bias_in,
    weight_out,
    bias_out,
    layer_scale,
    output,
    mixed_out,
    masked_out,
    edges_out,
    grads_out,
    state,
    coded,
    kernels,
    field,
    inner,
    result,
    normed_own,
    inverse_own,
    branch_own,
    slope_own,
    active_own,
    hidden_own,
    lifted_own,
    branch_grad_own,
    mixed_own,
    active_all,
    hidden_all,
    lifted_all,
    branch_grad_all,
    sums,
    hidden_sums,
    taps,
    edges,
    mixed_edges,
):
    height, breadth, first_rows, second_rows, window_rows = sizes
    channels = state.shape[2]
    own_start = starts[0]
    second_start = starts[1]
    first_start = starts[2]
    first_width = field.shape[1]
    second_width = inner.shape[1]
    pad = MARGIN

    for ref in (state, coded, field, inner):
        ref[pl.ds(0, pad)] = jnp.zeros((pad,) + ref.shape[1:], F32)
        below = ref.shape[0] - pad - window_rows
        ref[pl.ds(pad + window_rows, below)] = jnp.zeros((below,) + ref.shape[1:], F32)
    state[pl.ds(pad, window_rows)] = jnp.zeros((window_rows,) + state.shape[1:], F32)
    coded[pl.ds(pad, window_rows)] = jnp.zeros((window_rows,) + coded.shape[1:], F32)

    fill_windows(
        (height, breadth, window_rows),
        starts,
        (state_tile, cotangent, land_sea, lat_pieces, within, across),
        state,
        coded,
        edges,
    )
    kernels[...] = dw_in[...].astype(F32)
    sums[...] = jnp.zeros_like(sums)
    hidden_sums[...] = jnp.zeros_like(hidden_sums)

    def param(ref, layer):
        return ref[pl.ds(layer, 1), :]

    first_step = divisor(first_rows, FIRST_STEP)

    def forward_first(step, carry):
        row = first_start + step * first_step
        cells = first_step * first_width
        mixed = conv_rows(state, row, 0, first_step, first_width, kernels.at[0], False)
        normed, inverse = normalise(mixed + param(conv_bias, 0))
        lifted = (normed * param(norm_gain, 0) + param(norm_bias, 0)).astype(BF16)
        hidden = dot(lifted, weight_in[0]) + param(bias_in, 0)
        cumulative, bell = normal_parts(hidden)
        active = hidden * cumulative
        branch = dot(active.astype(BF16), weight_out[0]) + param(bias_out, 0)
        center = rows_of(state, row + pad, MARGIN, first_step, first_width)
        mark = rows_of(coded, row + pad, 0, first_step, first_width)
        value = jnp.where(mark < LAND_BOUND, center + param(layer_scale, 0) * branch, 0.0)
        value = value.reshape(first_step, first_width, channels)

        for index in range(first_step):
            field[row + pad + index] = value[index]

        def own(values):
            shape = (first_step, first_width, values.shape[1])
            return values.reshape(shape)[:, FIELD_AT : FIELD_AT + breadth]

        slope = own(cumulative) + own(hidden) * (own(bell) * INV_ROOT_TWO_PI)
        spots = pl.ds(row, first_step)
        slope_own[spots] = slope
        active_own[spots] = own(active).astype(BF16)
        normed_own[spots] = own(normed)
        inverse_own[spots] = own(jnp.broadcast_to(inverse, normed.shape))
        branch_own[spots] = own(branch)
        lifted_own[spots] = own(normed * param(norm_gain, 0) + param(norm_bias, 0)).astype(BF16)
        return carry

    lax.fori_loop(0, first_rows // first_step, forward_first, 0)

    second_step = divisor(second_rows, SECOND_STEP)

    def both_second(step, carry):
        row = second_start + step * second_step
        cells = second_step * second_width
        shift = FIELD_AT - INNER_AT
        mixed = conv_rows(
            field, row, shift - MARGIN, second_step, second_width, kernels.at[1], False
        )
        normed, inverse = normalise(mixed + param(conv_bias, 1))
        lifted = normed * param(norm_gain, 1) + param(norm_bias, 1)
        hidden = dot(lifted.astype(BF16), weight_in[1]) + param(bias_in, 1)
        cumulative, bell = normal_parts(hidden)
        active = (hidden * cumulative).astype(BF16)
        branch = dot(active, weight_out[1]) + param(bias_out, 1)
        center = rows_of(field, row + pad, shift, second_step, second_width)
        mark = rows_of(coded, row + pad, shift, second_step, second_width)
        ocean = mark < LAND_BOUND
        value = jnp.where(ocean, center + param(layer_scale, 1) * branch, 0.0)
        value = value.reshape(second_step, second_width, channels)
        masked = jnp.where(ocean, mark, 0.0)
        grad_branch = (masked * param(layer_scale, 1)).astype(BF16)
        grad_active = dot_cols(grad_branch, weight_out[1])
        slope = cumulative + hidden * (bell * INV_ROOT_TWO_PI)
        grad_hidden = (grad_active * slope).astype(BF16)
        grad_lifted = dot_cols(grad_hidden, weight_in[1])
        grad_mixed = normalise_back(grad_lifted * param(norm_gain, 1), normed, inverse)
        grad_mixed = grad_mixed.reshape(second_step, second_width, channels)
        for index in range(second_step):
            result[row + index] = value[index]
            inner[row + pad + index] = grad_mixed[index]

        shape = (second_step, second_width, channels)
        row_of = lax.broadcasted_iota(jnp.int32, shape, 0) + (row - own_start)
        col_of = lax.broadcasted_iota(jnp.int32, shape, 1) - INNER_AT
        inside = (row_of >= 0) & (row_of < height) & (col_of >= 0) & (col_of < breadth)
        inside = jnp.where(inside, 1.0, 0.0).astype(F32).reshape(cells, channels)
        own_lifted = grad_lifted * inside
        own_branch = grad_branch.astype(F32) * inside
        sums[1, 0] += fold(masked * branch * inside)
        sums[1, 1] += fold(own_branch)
        sums[1, 2] += fold(own_lifted * normed)
        sums[1, 3] += fold(own_lifted)
        wide = jnp.concatenate([inside] * (hidden.shape[1] // channels), axis=1)
        hidden_sums[1] += fold(grad_hidden.astype(F32) * wide)
        spots = pl.ds(pl.multiple_of(step * cells, cells), cells)
        active_all[spots] = active
        hidden_all[spots] = grad_hidden
        lifted_all[spots] = (lifted * inside).astype(BF16)
        branch_grad_all[spots] = own_branch.astype(BF16)
        return carry

    lax.fori_loop(0, second_rows // second_step, both_second, 0)

    back_step = divisor(height, BACK_STEP)

    def backward_first(step, carry):
        row = own_start + step * back_step
        cells = back_step * breadth
        mark = rows_of(coded, row + pad, FIELD_AT, back_step, breadth)
        ocean = mark < LAND_BOUND
        masked_next = jnp.where(ocean, mark, 0.0)
        spread = conv_rows(inner, row, 0, back_step, breadth, kernels.at[1], True)
        masked = jnp.where(ocean, masked_next + spread, 0.0)
        grad_branch = (masked * param(layer_scale, 0)).astype(BF16)
        grad_active = dot_cols(grad_branch, weight_out[0])
        slope = slope_own[pl.ds(row, back_step)].reshape(cells, grad_active.shape[1])
        grad_hidden = (grad_active * slope).astype(BF16)
        grad_lifted = dot_cols(grad_hidden, weight_in[0])
        normed = normed_own[pl.ds(row, back_step)].reshape(cells, channels)
        inverse = inverse_own[pl.ds(row, back_step)].reshape(cells, channels)
        grad_mixed = normalise_back(grad_lifted * param(norm_gain, 0), normed, inverse)
        branch = branch_own[pl.ds(row, back_step)].reshape(cells, channels)
        sums[0, 0] += fold(masked * branch)
        sums[0, 1] += fold(grad_branch.astype(F32))
        sums[0, 2] += fold(grad_lifted * normed)
        sums[0, 3] += fold(grad_lifted)
        sums[0, 4] += fold(grad_mixed)
        hidden_sums[0] += fold(grad_hidden.astype(F32))
        inner_rows = rows_of(inner, row + pad, INNER_AT, back_step, breadth)
        sums[1, 4] += fold(inner_rows)
        tile = pl.ds(step * back_step, back_step)
        shape = (back_step, breadth, channels)
        grad_mixed = grad_mixed.reshape(shape)
        mixed_own[tile] = grad_mixed
        mixed_out[tile] = grad_mixed.astype(BF16)
        masked_out[tile] = masked.reshape(shape).astype(BF16)
        hidden_own[tile] = grad_hidden.reshape(back_step, breadth, grad_hidden.shape[1])
        branch_grad_own[tile] = grad_branch.reshape(shape)
        value = rows_of(result, row, INNER_AT, back_step, breadth)
        output[tile] = value.reshape(shape).astype(BF16)
        return carry

    lax.fori_loop(0, height // back_step, backward_first, 0)

    mixed_edges[...] = jnp.zeros_like(mixed_edges)
    lower = starts[3] == 0
    for row in range(height):
        first = mixed_own[row, pl.ds(0, MARGIN), :]
        last = mixed_own[row, pl.ds(breadth - MARGIN, MARGIN), :]
        spots = pl.ds(row * MARGIN, MARGIN)
        mixed_edges[0, spots] = jnp.where(lower, last, first)
        mixed_edges[1, spots] = jnp.where(lower, first, last)
    edges_out[...] = mixed_edges[...].astype(BF16)

    hidden_units = weight_in.shape[2]
    groups = hidden_units // channels
    tile = pl.ds(own_start, height)
    cells = height * breadth

    def flat(ref, spots):
        return ref[spots].reshape(cells, ref.shape[2])

    operands = (
        (
            flat(lifted_own, tile),
            flat(hidden_own, pl.ds(0, height)),
            flat(active_own, tile),
            flat(branch_grad_own, pl.ds(0, height)),
        ),
        (lifted_all[...], hidden_all[...], active_all[...], branch_grad_all[...]),
    )
    for layer, (lifted, grad_hidden, active, grad_branch) in enumerate(operands):
        at = layer * (grads_out.shape[0] // BLOCKS)
        grad_in = dot_rows(lifted, grad_hidden)
        for group in range(groups):
            grads_out[pl.ds(at + group * channels, channels), :] = grad_in[
                :, group * channels : (group + 1) * channels
            ].astype(BF16)
        grad_out = dot_rows(grad_branch, active)
        for group in range(groups):
            grads_out[pl.ds(at + hidden_units + group * channels, channels), :] = grad_out[
                :, group * channels : (group + 1) * channels
            ].T.astype(BF16)

    taps[...] = jnp.zeros_like(taps)
    for layer in range(BLOCKS):
        base = layer * (taps.shape[0] // BLOCKS)
        if layer:
            tap_sums(
                inner,
                own_start + pad,
                INNER_AT,
                field,
                own_start,
                FIELD_AT - MARGIN,
                height,
                breadth,
                taps.at[pl.ds(base, TAPS)],
            )
        else:
            tap_sums(
                mixed_own,
                0,
                0,
                state,
                own_start,
                STATE_AT - MARGIN,
                height,
                breadth,
                taps.at[pl.ds(base, TAPS)],
            )
        for member in range(5):
            taps[pl.ds(base + TAPS + member, 1), :] = jnp.sum(
                sums[layer, member], axis=0, keepdims=True
            )
        hidden_total = jnp.sum(hidden_sums[layer], axis=0, keepdims=True)
        for group in range(groups):
            taps[pl.ds(base + TAPS + 5 + group, 1), :] = hidden_total[
                :, group * channels : (group + 1) * channels
            ]
    small = taps.shape[0] // BLOCKS
    for layer in range(BLOCKS):
        at = layer * (grads_out.shape[0] // BLOCKS) + 2 * hidden_units
        grads_out[pl.ds(at, small), :] = taps[pl.ds(layer * small, small), :].astype(BF16)


def state_kernel(starts, mixed, within, across, lat_pieces, masked, dw_in, out, wide, kernels, edges):
    height, breadth, channels = masked.shape
    wide[...] = jnp.zeros_like(wide)
    kernels[...] = dw_in[...].astype(F32)
    wide[pl.ds(MARGIN, height), pl.ds(MARGIN, breadth), :] = mixed[...].astype(F32)
    sides = lat_pieces.shape[0]
    inner = MARGIN * breadth
    beside = MARGIN * MARGIN
    for side in range(sides):
        first = starts[1 + side]
        piece = lat_pieces[side].astype(F32)
        for row in range(MARGIN):
            spots = slice(row * breadth, (row + 1) * breadth)
            wide[first + row, pl.ds(MARGIN, breadth), :] = piece[spots]

    def fill_columns(source, place, west):
        column = 0 if west else MARGIN + breadth
        edges[...] = source[...].astype(F32)
        for row in range(height):
            wide[MARGIN + row, pl.ds(column, MARGIN), :] = edges[pl.ds(row * MARGIN, MARGIN), :]
        for side in range(sides):
            piece = lat_pieces[side].astype(F32)
            for row in range(MARGIN):
                at = inner + place * beside + row * MARGIN
                wide[starts[1 + side] + row, pl.ds(column, MARGIN), :] = piece[at : at + MARGIN]

    @pl.when(starts[0] == 0)
    def _():
        fill_columns(within, 0, False)
        fill_columns(across, 1, True)

    @pl.when(starts[0] != 0)
    def _():
        fill_columns(within, 0, True)
        fill_columns(across, 1, False)

    rows = divisor(height, BACK_STEP)

    def advance(step, carry):
        row = step * rows
        spread = conv_rows(wide, row, 0, rows, breadth, kernels, True)
        tile = pl.ds(row, rows)
        shape = (rows, breadth, channels)
        out[tile] = (masked[tile].astype(F32) + spread.reshape(shape)).astype(BF16)
        return carry

    lax.fori_loop(0, height // rows, advance, 0)


def gradient_kernel(grad_norm, held, own, other, *outs):
    kernel, conv_bias, gain, shift, first, first_bias, second, second_bias, scale = outs
    channels = own.shape[1]
    units = second.shape[1]
    groups = units // channels

    def unpack(rows, layer):
        for group in range(groups):
            spots = pl.ds(group * channels, channels)
            first[layer, :, spots] = rows[spots].astype(F32) * grad_norm
        second[layer] = rows[pl.ds(units, units)].astype(F32) * grad_norm
        small = rows[pl.ds(2 * units, rows.shape[0] - 2 * units)].astype(F32) * grad_norm
        for index in range(TAPS):
            kernel[index // KSIZE, index % KSIZE, layer : layer + 1] = small[index : index + 1]
        for member, out in enumerate((scale, second_bias, gain, shift, conv_bias)):
            out[layer : layer + 1] = small[TAPS + member : TAPS + member + 1]
        for group in range(groups):
            row = TAPS + 5 + group
            first_bias[layer : layer + 1, pl.ds(group * channels, channels)] = small[row : row + 1]

    @pl.when(held[0] == 0)
    def _():
        unpack(own, 0)
        unpack(other, 1)

    @pl.when(held[0] != 0)
    def _():
        unpack(own, 1)
        unpack(other, 0)


class Links:
    def __init__(self, mesh):
        self.lon = mesh.shape["lon"]
        self.lat = mesh.shape["lat"]
        self.axes = ("lon", "lat")

    def lon_neighbours(self, within, across):
        there = [place + 1 if place % 2 else place - 1 for place in range(self.lon)]
        pairs = [(place, other % self.lon) for place, other in enumerate(there)]
        across = lax.ppermute(across, "lon", pairs)
        return self.swap(within, 1, 0), across

    def shift_lat(self, values, by):
        pairs = [
            (place, place + by) for place in range(self.lat) if 0 <= place + by < self.lat
        ]
        return lax.ppermute(values, "lat", pairs)

    def lat_neighbours(self, last, first):
        if self.lat == 2:
            mine = jnp.where(lax.axis_index("lat") == 0, last, first)
            return self.swap(mine, 0, 1)[None]
        return jnp.stack([self.shift_lat(last, 1), self.shift_lat(first, -1)])

    def swap(self, values, lon_bits, lat_bits):
        pairs = []
        for lon in range(self.lon):
            for lat in range(self.lat):
                there = (lon ^ lon_bits) * self.lat + (lat ^ lat_bits)
                pairs.append((lon * self.lat + lat, there))
        return lax.ppermute(values, self.axes, pairs)

    def sum_all(self, rows, beside):
        lon = lax.axis_index("lon")
        lat = lax.axis_index("lat")
        bits = [(1 << bit, 0) for bit in range(self.lon.bit_length() - 1)]
        bits = bits[:1] + [(0, 1 << bit) for bit in range(self.lat.bit_length() - 1)] + bits[1:]

        def code(group):
            total = jnp.int32(0)
            for index, (lon_bit, lat_bit) in enumerate(group):
                held = (lon // lon_bit) % 2 if lon_bit else (lat // lat_bit) % 2
                total = total + held * (1 << index)
            return total

        def merged(group, choice):
            lon_bits = sum(bit[0] for index, bit in enumerate(group) if choice >> index & 1)
            lat_bits = sum(bit[1] for index, bit in enumerate(group) if choice >> index & 1)
            return lon_bits, lat_bits

        def scatter(values, group):
            count = 1 << len(group)
            pieces = values.reshape(count, -1, values.shape[1])
            here = code(group)
            total = lax.dynamic_index_in_dim(pieces, here, 0, False).astype(F32)
            for choice in range(1, count):
                sent = lax.dynamic_index_in_dim(pieces, here ^ choice, 0, False)
                total = total + self.swap(sent, *merged(group, choice)).astype(F32)
            return total.astype(BF16)

        def exchange(values, group):
            total = values.astype(F32)
            for choice in range(1, 1 << len(group)):
                total = total + self.swap(values, *merged(group, choice)).astype(F32)
            return total.astype(BF16)

        def gather(values, group):
            count = 1 << len(group)
            pieces = [values]
            for choice in range(1, count):
                pieces.append(self.swap(values, *merged(group, choice)))
            stack = jnp.stack(pieces)
            here = code(group)
            ordered = [
                lax.dynamic_index_in_dim(stack, here ^ place, 0, False) for place in range(count)
            ]
            return jnp.concatenate(ordered, axis=0)

        pair, quad, rest = bits[:1], bits[1:3], bits[3:]
        values = scatter(scatter(rows, pair), quad)
        while rest:
            values = exchange(values, rest[:2])
            rest = rest[2:]
        values = gather(values, quad)
        values, beside = lax.optimization_barrier((values, beside))
        return code(pair), values, self.swap(values, *pair[0]), beside


def on_device(links, state, land_sea, cotangent, *params):
    dw_kernel, weight_in = params[0], params[4]
    height, breadth, channels = state.shape
    hidden_units = weight_in.shape[2]
    groups = hidden_units // channels
    grad_norm = 1.0 / math.sqrt(links.lat * height * links.lon * breadth)
    lat = lax.axis_index("lat")
    sides = 1 if links.lat == 2 else 2
    window_rows = height + sides * WIDE
    first_rows = height + sides * NARROW
    second_rows = height + sides * MARGIN

    def start(margin):
        skipped = WIDE - margin
        return lat * skipped if sides == 1 else jnp.int32(skipped)

    core = lax.axis_index("lon") % 2
    vmem = pl.BlockSpec(memory_space=pltpu.VMEM)
    smem = pl.BlockSpec(memory_space=pltpu.SMEM)
    tile = (height, breadth, channels)

    def flat(values):
        return values.reshape(-1, channels)

    def whole_rows(values, rows):
        return jnp.pad(values, ((0, rows - values.shape[0]), (0, channels - values.shape[1])))

    land = land_sea.T
    marks = (land != 0).astype(BF16)

    def lat_rows(far, near):
        return jnp.concatenate(
            [flat(state[far]), flat(cotangent[near]), whole_rows(marks[:, far], breadth)]
        )

    pieces = links.lat_neighbours(
        lat_rows(slice(height - WIDE, height), slice(height - MARGIN, height)),
        lat_rows(slice(0, WIDE), slice(0, MARGIN)),
    )
    far, near = WIDE * breadth, MARGIN * breadth
    piece_states = pieces[:, :far].reshape(sides, WIDE, breadth, channels)
    piece_cotangents = pieces[:, far : far + near].reshape(sides, MARGIN, breadth, channels)
    piece_marks = pieces[:, far + near :]

    def lon_columns(wide, narrow, margin):
        own = jnp.concatenate([state[:, wide], cotangent[:, margin]], axis=1)

        def ends(side, above):
            empty = ((NARROW, 0) if above else (0, NARROW), (0, 0), (0, 0))
            near_rows = jnp.pad(piece_cotangents[side][:, margin], empty)
            return jnp.concatenate([piece_states[side][:, wide], near_rows], axis=1)

        if sides == 1:
            rows = jnp.where(
                lat == 0,
                jnp.concatenate([own, ends(0, False)]),
                jnp.concatenate([ends(0, True), own]),
            )
        else:
            rows = jnp.concatenate([ends(0, True), own, ends(1, False)])
        kept = [whole_rows(marks[narrow], 8)]
        kept += [jnp.pad(piece_marks[side][narrow], ((0, 8 - NARROW), (0, 0))) for side in range(sides)]
        return jnp.concatenate([flat(rows), *kept])

    first_columns = lon_columns(slice(0, WIDE), slice(0, NARROW), slice(0, MARGIN))
    last_columns = lon_columns(
        slice(breadth - WIDE, breadth),
        slice(breadth - NARROW, breadth),
        slice(breadth - MARGIN, breadth),
    )
    within, across = links.lon_neighbours(
        jnp.where(core == 0, last_columns, first_columns),
        jnp.where(core == 0, first_columns, last_columns),
    )
    if sides == 1:
        places = [(1 - lat) * height]
        closest = [jnp.where(lat == 0, height, WIDE - MARGIN)]
    else:
        places = [0, WIDE + height]
        closest = [WIDE - MARGIN, WIDE + height]
    starts = [start(0), start(MARGIN), start(NARROW), core, *places, *closest]
    starts = jnp.stack([jnp.asarray(entry, jnp.int32) for entry in starts])
    state_pitch, field_pitch, inner_pitch = (
        round_up(breadth + size, 8) for size in (STATE_AT + WIDE, FIELD_AT + NARROW, NARROW)
    )

    padded_rows = window_rows + 2 * MARGIN + 1
    all_cells = second_rows * inner_pitch
    layer_rows = round_up(2 * hidden_units + TAPS + 5 + groups, 4 * 16)
    small_rows = BLOCKS * (layer_rows - 2 * hidden_units)
    grad_rows = BLOCKS * layer_rows
    own_rows = (window_rows, breadth)
    edge_rows = round_up(height * MARGIN, 8)
    scratch = [
        pltpu.VMEM((padded_rows, state_pitch, channels), F32),
        pltpu.VMEM((padded_rows, field_pitch, channels), F32),
        pltpu.VMEM((BLOCKS, TAPS, channels), F32),
        pltpu.VMEM((padded_rows, field_pitch, channels), F32),
        pltpu.VMEM((padded_rows, inner_pitch, channels), F32),
        pltpu.VMEM((window_rows, inner_pitch, channels), F32),
        pltpu.VMEM(own_rows + (channels,), F32),
        pltpu.VMEM(own_rows + (channels,), F32),
        pltpu.VMEM(own_rows + (channels,), F32),
        pltpu.VMEM(own_rows + (hidden_units,), F32),
        pltpu.VMEM(own_rows + (hidden_units,), BF16),
        pltpu.VMEM((height, breadth, hidden_units), BF16),
        pltpu.VMEM(own_rows + (channels,), BF16),
        pltpu.VMEM(tile, BF16),
        pltpu.VMEM(tile, F32),
        pltpu.VMEM((all_cells, hidden_units), BF16),
        pltpu.VMEM((all_cells, hidden_units), BF16),
        pltpu.VMEM((all_cells, channels), BF16),
        pltpu.VMEM((all_cells, channels), BF16),
        pltpu.VMEM((BLOCKS, 5, 8, channels), F32),
        pltpu.VMEM((BLOCKS, 8, hidden_units), F32),
        pltpu.VMEM((small_rows, channels), F32),
        pltpu.VMEM(within.shape, F32),
        pltpu.VMEM((2, edge_rows, channels), F32),
    ]
    sizes = (height, breadth, first_rows, second_rows, window_rows)
    taps_in = dw_kernel.reshape(BLOCKS, TAPS, channels)
    output, grad_mixed, masked, mixed_edges, grads = pl.pallas_call(
        functools.partial(tile_kernel, sizes),
        out_shape=(
            jax.ShapeDtypeStruct(tile, BF16),
            jax.ShapeDtypeStruct(tile, BF16),
            jax.ShapeDtypeStruct(tile, BF16),
            jax.ShapeDtypeStruct((2, edge_rows, channels), BF16),
            jax.ShapeDtypeStruct((grad_rows, channels), BF16),
        ),
        in_specs=[smem] + [vmem] * 15,
        out_specs=(vmem,) * 5,
        scratch_shapes=scratch,
        compiler_params=pltpu.CompilerParams(vmem_limit_bytes=48 * 1024 * 1024),
        cost_estimate=pl.CostEstimate(
            flops=20 * all_cells * channels * hidden_units,
            bytes_accessed=4 * height * breadth * channels * 4,
            transcendentals=0,
        ),
    )(starts, state, cotangent, land, pieces, within, across, taps_in, *params[1:])

    within, across = links.lon_neighbours(mixed_edges[0], mixed_edges[1])
    corner = MARGIN * MARGIN

    def corner_rows(rows, first):
        beside = slice(first * MARGIN, first * MARGIN + corner)
        parts = jnp.concatenate([flat(grad_mixed[rows]), within[beside], across[beside]])
        return jnp.pad(parts, ((0, -parts.shape[0] % 16), (0, 0)))

    pieces = links.lat_neighbours(
        corner_rows(slice(height - MARGIN, height), height - MARGIN),
        corner_rows(slice(0, MARGIN), 0),
    )
    if sides == 1:
        places = [(1 - lat) * (MARGIN + height)]
    else:
        places = [0, MARGIN + height]
    starts = jnp.stack([jnp.asarray(entry, jnp.int32) for entry in (core, *places)])
    wide = (height + 2 * MARGIN + 1, round_up(breadth + 2 * MARGIN, 8), channels)
    grad_state = pl.pallas_call(
        state_kernel,
        out_shape=jax.ShapeDtypeStruct(tile, BF16),
        in_specs=[smem] + [vmem] * 6,
        out_specs=vmem,
        scratch_shapes=[
            pltpu.VMEM(wide, F32),
            pltpu.VMEM((TAPS, channels), F32),
            pltpu.VMEM((edge_rows, channels), F32),
        ],
        compiler_params=pltpu.CompilerParams(vmem_limit_bytes=16 * 1024 * 1024),
        cost_estimate=pl.CostEstimate(
            flops=4_000_000_000, bytes_accessed=8_000_000, transcendentals=0
        ),
    )(starts, grad_mixed, within, across, pieces, masked, taps_in[0])

    held, own, other, grad_state = links.sum_all(grads, grad_state)
    shapes = [(KSIZE, KSIZE, BLOCKS, channels)] + [member.shape for member in params[1:]]
    grad_kernel, *gradients = pl.pallas_call(
        functools.partial(gradient_kernel, grad_norm),
        out_shape=tuple(jax.ShapeDtypeStruct(shape, F32) for shape in shapes),
        in_specs=[smem, vmem, vmem],
        out_specs=(vmem,) * 9,
        compiler_params=pltpu.CompilerParams(vmem_limit_bytes=8 * 1024 * 1024),
    )(held.reshape(1), own, other)
    return (output, grad_state, grad_kernel.transpose(2, 0, 1, 3), *gradients)


def solution(mesh):
    tile = P("lat", "lon", None)
    placed = (tile, P("lat", "lon"), tile) + (P(),) * 9
    return jax.shard_map(
        functools.partial(on_device, Links(mesh)),
        mesh=mesh,
        in_specs=placed,
        out_specs=(tile, tile) + (P(),) * 9,
        check_vma=False,
    )
```

```python
import functools
import math

import jax
import jax.numpy as jnp
from jax import lax
from jax.experimental import pallas as pl
from jax.experimental.pallas import tpu as pltpu
from jax.sharding import PartitionSpec as P

KSIZE = 7
MARGIN = KSIZE // 2
TAPS = KSIZE * KSIZE
BLOCKS = 2
EPS_NORM = 1e-06
INV_ROOT_TWO = 0.7071067811865476
INV_ROOT_TWO_PI = 0.3989422804014327
LAND = 1024.0
LAND_BOUND = 512.0
F32 = jnp.float32
BF16 = jnp.bfloat16
FIRST_STEP = 19
SECOND_STEP = 17
BACK_STEP = 45
TAP_STEP = 9
STATE_AT = 11
FIELD_AT = 8
INNER_AT = 3
WIDE = 3 * MARGIN
NARROW = 2 * MARGIN


def divisor(size, most):
    return max(step for step in range(1, most + 1) if size % step == 0)


def round_up(size, unit):
    return (size + unit - 1) // unit * unit


def pack_rows(above, below):
    shape = (above.shape[0] // 8, 8, above.shape[1])
    return jnp.concatenate([above.reshape(shape), below.reshape(shape)], axis=1).astype(BF16)


def conv_rows(source, base, first, count, width, kernel_ref, flip):
    pairs = (count + 1) // 2
    sums = [[None, None] for _ in range(pairs)]
    channels = source.shape[2]
    for tap_col in range(KSIZE):
        parts = [None] * pairs
        taps = []
        for tap_row in range(KSIZE):
            index = tap_row * KSIZE + tap_col
            tap = kernel_ref[pl.ds(TAPS - 1 - index if flip else index, 1), :]
            taps.append(jnp.broadcast_to(tap, (16, channels)).astype(BF16)[None])
        above = source[base, pl.ds(first + tap_col, width), :]
        for row in range(2 * pairs + KSIZE - 2):
            below = source[base + row + 1, pl.ds(first + tap_col, width), :]
            both = pack_rows(above, below)
            above = below
            for tap_row in range(row % 2, KSIZE, 2):
                out = (row - tap_row) // 2
                if 0 <= out < pairs:
                    term = both * taps[tap_row]
                    parts[out] = term if parts[out] is None else parts[out] + term
        for out in range(pairs):
            for side in range(2):
                value = parts[out].astype(F32)[:, 8 * side : 8 * side + 8]
                old = sums[out][side]
                sums[out][side] = value if old is None else old + value
    rows = [sums[row // 2][row % 2].reshape(width, channels) for row in range(count)]
    return jnp.concatenate(rows, axis=0)


def normal_parts(hidden):
    cumulative = 0.5 + 0.5 * lax.erf(hidden * INV_ROOT_TWO)
    return cumulative, jnp.exp(-0.5 * hidden * hidden)


def fold(values):
    return jnp.sum(values.reshape(values.shape[0] // 8, 8, values.shape[1]), axis=0)


def normalise(mixed):
    center = mixed - jnp.mean(mixed, axis=-1, keepdims=True)
    inverse = lax.rsqrt(jnp.mean(center * center, axis=-1, keepdims=True) + EPS_NORM)
    return center * inverse, inverse


def normalise_back(grad, normed, inverse):
    return inverse * (
        grad
        - jnp.mean(grad, axis=-1, keepdims=True)
        - normed * jnp.mean(grad * normed, axis=-1, keepdims=True)
    )


def rows_of(ref, base, first, count, width):
    return jnp.concatenate(
        [ref[base + row, pl.ds(first, width), :] for row in range(count)], axis=0
    )


CONTRACT_COLS = (((1,), (1,)), ((), ()))
CONTRACT_ROWS = (((0,), (0,)), ((), ()))


def dot(left, right):
    return jnp.dot(left, right, preferred_element_type=F32)


def dot_cols(left, right):
    return lax.dot_general(left, right, CONTRACT_COLS, preferred_element_type=F32)


def dot_rows(left, right):
    return lax.dot_general(left, right, CONTRACT_ROWS, preferred_element_type=F32)


def tap_sums(grad_ref, grad_row, grad_col, field_ref, field_row, field_col, height, width, out):
    rows = divisor(height, TAP_STEP)
    pairs = (rows + 1) // 2
    for cols in ((0, 1, 2, 3), (4, 5, 6)):

        def advance(step, sums):
            sums = list(sums)
            at = step * rows
            grads = [grad_ref[grad_row + at + row, pl.ds(grad_col, width), :] for row in range(rows)]
            grads += [jnp.zeros_like(grads[0])] * (2 * pairs - rows)
            grads = [pack_rows(grads[2 * pair], grads[2 * pair + 1]) for pair in range(pairs)]
            for place, tap_col in enumerate(cols):
                spots = pl.ds(field_col + tap_col, width)
                parts = [None] * KSIZE
                above = field_ref[field_row + at, spots, :]
                for row in range(2 * pairs + KSIZE - 2):
                    below = field_ref[field_row + at + row + 1, spots, :]
                    both = pack_rows(above, below)
                    above = below
                    for tap_row in range(row % 2, KSIZE, 2):
                        pair = (row - tap_row) // 2
                        if 0 <= pair < pairs:
                            term = grads[pair] * both
                            old = parts[tap_row]
                            parts[tap_row] = term if old is None else old + term
                for tap_row in range(KSIZE):
                    part = parts[tap_row]
                    total = part[0]
                    for group in range(1, part.shape[0]):
                        total = total + part[group]
                    index = place * KSIZE + tap_row
                    sums[index] = sums[index] + fold(total.astype(F32))
            return tuple(sums)

        zeros = tuple(jnp.zeros((8, grad_ref.shape[2]), F32) for _ in range(KSIZE * len(cols)))
        sums = lax.fori_loop(0, height // rows, advance, zeros)
        for place, tap_col in enumerate(cols):
            for tap_row in range(KSIZE):
                total = jnp.sum(sums[place * KSIZE + tap_row], axis=0, keepdims=True)
                out[pl.ds(tap_row * KSIZE + tap_col, 1), :] = total


def pack_kernel(lat, state, cotangent, land_sea, out, rows):
    height, breadth, channels = state.shape
    sides = out.shape[0]
    rows[...] = jnp.zeros_like(rows)
    ocean = jnp.where(land_sea[...] != 0, 1.0, 0.0).astype(F32)
    far, near = WIDE * breadth, MARGIN * breadth
    for side in range(sides):
        last = lat[0] == 0 if sides == 1 else side == 0
        first = jnp.where(last, height - WIDE, 0)
        closest = jnp.where(last, height - MARGIN, 0)
        for row in range(WIDE):
            rows[side, pl.ds(row * breadth, breadth), :] = state[first + row].astype(F32)
        for row in range(MARGIN):
            spots = pl.ds(far + row * breadth, breadth)
            rows[side, spots, :] = cotangent[closest + row].astype(F32)
        marks = jnp.where(last, ocean[:, height - WIDE :], ocean[:, :WIDE])
        rows[side, pl.ds(far + near, breadth), pl.ds(0, WIDE)] = marks
    out[...] = rows[...].astype(BF16)


def fill_windows(sizes, starts, sources, state, coded, edges):
    height, breadth, window_rows = sizes
    state_tile, cotangent, land_sea, lat_pieces, within, across = sources
    channels = state.shape[2]
    pad = MARGIN
    own = pad + starts[0]
    lower = starts[3] == 0
    state[pl.ds(pad, window_rows)] = jnp.zeros((window_rows,) + state.shape[1:], F32)
    coded[pl.ds(pad, window_rows)] = jnp.zeros((window_rows,) + coded.shape[1:], F32)

    def spread(marks, column):
        return jnp.broadcast_to(marks[:, column : column + 1], (marks.shape[0], channels))

    state[pl.ds(own, height), pl.ds(STATE_AT, breadth), :] = state_tile[...].astype(F32)
    ocean = jnp.where(land_sea[...] != 0, 1.0, 0.0).astype(F32)
    for row in range(height):
        value = jnp.where(spread(ocean, row) > 0.5, cotangent[row].astype(F32), LAND)
        coded[own + row, pl.ds(FIELD_AT, breadth), :] = value

    sides = lat_pieces.shape[0]
    far, near = WIDE * breadth, MARGIN * breadth
    for side in range(sides):
        first = pad + starts[4 + side]
        closest = pad + starts[4 + sides + side]
        piece = lat_pieces[side].astype(F32)
        marks = piece[far + near : far + near + breadth]
        for row in range(WIDE):
            spots = pl.ds(row * breadth, breadth)
            state[first + row, pl.ds(STATE_AT, breadth), :] = lat_pieces[side, spots].astype(F32)
            value = jnp.where(spread(marks, row) > 0.5, 0.0, LAND)
            coded[first + row, pl.ds(FIELD_AT, breadth), :] = value
        for row in range(MARGIN):
            value = piece[far + row * breadth : far + (row + 1) * breadth]
            old = coded[closest + row, pl.ds(FIELD_AT, breadth), :]
            value = jnp.where(old > LAND_BOUND, LAND, value)
            coded[closest + row, pl.ds(FIELD_AT, breadth), :] = value

    group = WIDE + MARGIN

    def fill_columns(source, west):
        edges[...] = source[...].astype(F32)
        state_at = STATE_AT - WIDE if west else STATE_AT + breadth
        mark_at = FIELD_AT - NARROW if west else FIELD_AT + breadth
        value_at = FIELD_AT - MARGIN if west else FIELD_AT + breadth
        shown = slice(NARROW - MARGIN, NARROW) if west else slice(0, MARGIN)
        spans = [(own - pad, height, 0)] + [(starts[4 + side], WIDE, side + 1) for side in range(sides)]
        for first, count, place in spans:
            marks = edges[pl.ds(window_rows * group + place * 8, 8), :]
            for row in range(count):
                at = pad + first + row
                lines = (first + row) * group
                state[at, pl.ds(state_at, WIDE), :] = edges[pl.ds(lines, WIDE), :]
                mark = spread(marks, row)[:NARROW]
                coded[at, pl.ds(mark_at, NARROW), :] = jnp.where(mark > 0.5, 0.0, LAND)
                value = jnp.where(mark[shown] > 0.5, edges[pl.ds(lines + WIDE, MARGIN), :], LAND)
                coded[at, pl.ds(value_at, MARGIN), :] = value

    @pl.when(lower)
    def _():
        fill_columns(across, True)
        fill_columns(within, False)

    @pl.when(jnp.logical_not(lower))
    def _():
        fill_columns(within, True)
        fill_columns(across, False)


def tile_kernel(
    sizes,
    starts,
    state_tile,
    cotangent,
    land_sea,
    lat_pieces,
    within,
    across,
    dw_in,
    conv_bias,
    norm_gain,
    norm_bias,
    weight_in,
    bias_in,
    weight_out,
    bias_out,
    layer_scale,
    output,
    mixed_out,
    masked_out,
    edges_out,
    grads_out,
    state,
    coded,
    kernels,
    field,
    inner,
    result,
    normed_own,
    inverse_own,
    branch_own,
    slope_own,
    active_own,
    hidden_own,
    lifted_own,
    branch_grad_own,
    mixed_own,
    active_all,
    hidden_all,
    lifted_all,
    branch_grad_all,
    sums,
    hidden_sums,
    taps,
    edges,
    mixed_edges,
):
    height, breadth, first_rows, second_rows, window_rows = sizes
    channels = state.shape[2]
    own_start = starts[0]
    second_start = starts[1]
    first_start = starts[2]
    first_width = field.shape[1]
    second_width = inner.shape[1]
    pad = MARGIN

    for ref in (state, coded, field, inner):
        ref[pl.ds(0, pad)] = jnp.zeros((pad,) + ref.shape[1:], F32)
        below = ref.shape[0] - pad - window_rows
        ref[pl.ds(pad + window_rows, below)] = jnp.zeros((below,) + ref.shape[1:], F32)
    state[pl.ds(pad, window_rows)] = jnp.zeros((window_rows,) + state.shape[1:], F32)
    coded[pl.ds(pad, window_rows)] = jnp.zeros((window_rows,) + coded.shape[1:], F32)

    fill_windows(
        (height, breadth, window_rows),
        starts,
        (state_tile, cotangent, land_sea, lat_pieces, within, across),
        state,
        coded,
        edges,
    )
    kernels[...] = dw_in[...].astype(F32)
    sums[...] = jnp.zeros_like(sums)
    hidden_sums[...] = jnp.zeros_like(hidden_sums)

    def param(ref, layer):
        return ref[pl.ds(layer, 1), :]

    first_step = divisor(first_rows, FIRST_STEP)

    def forward_first(step, carry):
        row = first_start + step * first_step
        cells = first_step * first_width
        mixed = conv_rows(state, row, 0, first_step, first_width, kernels.at[0], False)
        normed, inverse = normalise(mixed + param(conv_bias, 0))
        lifted = (normed * param(norm_gain, 0) + param(norm_bias, 0)).astype(BF16)
        hidden = dot(lifted, weight_in[0]) + param(bias_in, 0)
        cumulative, bell = normal_parts(hidden)
        active = hidden * cumulative
        branch = dot(active.astype(BF16), weight_out[0]) + param(bias_out, 0)
        center = rows_of(state, row + pad, MARGIN, first_step, first_width)
        mark = rows_of(coded, row + pad, 0, first_step, first_width)
        value = jnp.where(mark < LAND_BOUND, center + param(layer_scale, 0) * branch, 0.0)
        value = value.reshape(first_step, first_width, channels)

        for index in range(first_step):
            field[row + pad + index] = value[index]

        def own(values):
            shape = (first_step, first_width, values.shape[1])
            return values.reshape(shape)[:, FIELD_AT : FIELD_AT + breadth]

        slope = own(cumulative) + own(hidden) * (own(bell) * INV_ROOT_TWO_PI)
        spots = pl.ds(row, first_step)
        slope_own[spots] = slope
        active_own[spots] = own(active).astype(BF16)
        normed_own[spots] = own(normed)
        inverse_own[spots] = own(jnp.broadcast_to(inverse, normed.shape))
        branch_own[spots] = own(branch)
        lifted_own[spots] = own(normed * param(norm_gain, 0) + param(norm_bias, 0)).astype(BF16)
        return carry

    lax.fori_loop(0, first_rows // first_step, forward_first, 0)

    second_step = divisor(second_rows, SECOND_STEP)

    def both_second(step, carry):
        row = second_start + step * second_step
        cells = second_step * second_width
        shift = FIELD_AT - INNER_AT
        mixed = conv_rows(
            field, row, shift - MARGIN, second_step, second_width, kernels.at[1], False
        )
        normed, inverse = normalise(mixed + param(conv_bias, 1))
        lifted = normed * param(norm_gain, 1) + param(norm_bias, 1)
        hidden = dot(lifted.astype(BF16), weight_in[1]) + param(bias_in, 1)
        cumulative, bell = normal_parts(hidden)
        active = (hidden * cumulative).astype(BF16)
        branch = dot(active, weight_out[1]) + param(bias_out, 1)
        center = rows_of(field, row + pad, shift, second_step, second_width)
        mark = rows_of(coded, row + pad, shift, second_step, second_width)
        ocean = mark < LAND_BOUND
        value = jnp.where(ocean, center + param(layer_scale, 1) * branch, 0.0)
        value = value.reshape(second_step, second_width, channels)
        masked = jnp.where(ocean, mark, 0.0)
        grad_branch = (masked * param(layer_scale, 1)).astype(BF16)
        grad_active = dot_cols(grad_branch, weight_out[1])
        slope = cumulative + hidden * (bell * INV_ROOT_TWO_PI)
        grad_hidden = (grad_active * slope).astype(BF16)
        grad_lifted = dot_cols(grad_hidden, weight_in[1])
        grad_mixed = normalise_back(grad_lifted * param(norm_gain, 1), normed, inverse)
        grad_mixed = grad_mixed.reshape(second_step, second_width, channels)
        for index in range(second_step):
            result[row + index] = value[index]
            inner[row + pad + index] = grad_mixed[index]

        shape = (second_step, second_width, channels)
        row_of = lax.broadcasted_iota(jnp.int32, shape, 0) + (row - own_start)
        col_of = lax.broadcasted_iota(jnp.int32, shape, 1) - INNER_AT
        inside = (row_of >= 0) & (row_of < height) & (col_of >= 0) & (col_of < breadth)
        inside = jnp.where(inside, 1.0, 0.0).astype(F32).reshape(cells, channels)
        own_lifted = grad_lifted * inside
        own_branch = grad_branch.astype(F32) * inside
        sums[1, 0] += fold(masked * branch * inside)
        sums[1, 1] += fold(own_branch)
        sums[1, 2] += fold(own_lifted * normed)
        sums[1, 3] += fold(own_lifted)
        wide = jnp.concatenate([inside] * (hidden.shape[1] // channels), axis=1)
        hidden_sums[1] += fold(grad_hidden.astype(F32) * wide)
        spots = pl.ds(pl.multiple_of(step * cells, cells), cells)
        active_all[spots] = active
        hidden_all[spots] = grad_hidden
        lifted_all[spots] = (lifted * inside).astype(BF16)
        branch_grad_all[spots] = own_branch.astype(BF16)
        return carry

    lax.fori_loop(0, second_rows // second_step, both_second, 0)

    back_step = divisor(height, BACK_STEP)

    def backward_first(step, carry):
        row = own_start + step * back_step
        cells = back_step * breadth
        mark = rows_of(coded, row + pad, FIELD_AT, back_step, breadth)
        ocean = mark < LAND_BOUND
        masked_next = jnp.where(ocean, mark, 0.0)
        spread = conv_rows(inner, row, 0, back_step, breadth, kernels.at[1], True)
        masked = jnp.where(ocean, masked_next + spread, 0.0)
        grad_branch = (masked * param(layer_scale, 0)).astype(BF16)
        grad_active = dot_cols(grad_branch, weight_out[0])
        slope = slope_own[pl.ds(row, back_step)].reshape(cells, grad_active.shape[1])
        grad_hidden = (grad_active * slope).astype(BF16)
        grad_lifted = dot_cols(grad_hidden, weight_in[0])
        normed = normed_own[pl.ds(row, back_step)].reshape(cells, channels)
        inverse = inverse_own[pl.ds(row, back_step)].reshape(cells, channels)
        grad_mixed = normalise_back(grad_lifted * param(norm_gain, 0), normed, inverse)
        branch = branch_own[pl.ds(row, back_step)].reshape(cells, channels)
        sums[0, 0] += fold(masked * branch)
        sums[0, 1] += fold(grad_branch.astype(F32))
        sums[0, 2] += fold(grad_lifted * normed)
        sums[0, 3] += fold(grad_lifted)
        sums[0, 4] += fold(grad_mixed)
        hidden_sums[0] += fold(grad_hidden.astype(F32))
        inner_rows = rows_of(inner, row + pad, INNER_AT, back_step, breadth)
        sums[1, 4] += fold(inner_rows)
        tile = pl.ds(step * back_step, back_step)
        shape = (back_step, breadth, channels)
        grad_mixed = grad_mixed.reshape(shape)
        mixed_own[tile] = grad_mixed
        mixed_out[tile] = grad_mixed.astype(BF16)
        masked_out[tile] = masked.reshape(shape).astype(BF16)
        hidden_own[tile] = grad_hidden.reshape(back_step, breadth, grad_hidden.shape[1])
        branch_grad_own[tile] = grad_branch.reshape(shape)
        value = rows_of(result, row, INNER_AT, back_step, breadth)
        output[tile] = value.reshape(shape).astype(BF16)
        return carry

    lax.fori_loop(0, height // back_step, backward_first, 0)

    mixed_edges[...] = jnp.zeros_like(mixed_edges)
    lower = starts[3] == 0
    for row in range(height):
        first = mixed_own[row, pl.ds(0, MARGIN), :]
        last = mixed_own[row, pl.ds(breadth - MARGIN, MARGIN), :]
        spots = pl.ds(row * MARGIN, MARGIN)
        mixed_edges[0, spots] = jnp.where(lower, last, first)
        mixed_edges[1, spots] = jnp.where(lower, first, last)
    edges_out[...] = mixed_edges[...].astype(BF16)

    hidden_units = weight_in.shape[2]
    groups = hidden_units // channels
    tile = pl.ds(own_start, height)
    cells = height * breadth

    def flat(ref, spots):
        return ref[spots].reshape(cells, ref.shape[2])

    operands = (
        (
            flat(lifted_own, tile),
            flat(hidden_own, pl.ds(0, height)),
            flat(active_own, tile),
            flat(branch_grad_own, pl.ds(0, height)),
        ),
        (lifted_all[...], hidden_all[...], active_all[...], branch_grad_all[...]),
    )
    for layer, (lifted, grad_hidden, active, grad_branch) in enumerate(operands):
        at = layer * (grads_out.shape[0] // BLOCKS)
        grad_in = dot_rows(lifted, grad_hidden)
        for group in range(groups):
            grads_out[pl.ds(at + group * channels, channels), :] = grad_in[
                :, group * channels : (group + 1) * channels
            ].astype(BF16)
        grad_out = dot_rows(grad_branch, active)
        for group in range(groups):
            grads_out[pl.ds(at + hidden_units + group * channels, channels), :] = grad_out[
                :, group * channels : (group + 1) * channels
            ].T.astype(BF16)

    taps[...] = jnp.zeros_like(taps)
    for layer in range(BLOCKS):
        base = layer * (taps.shape[0] // BLOCKS)
        if layer:
            tap_sums(
                inner,
                own_start + pad,
                INNER_AT,
                field,
                own_start,
                FIELD_AT - MARGIN,
                height,
                breadth,
                taps.at[pl.ds(base, TAPS)],
            )
        else:
            tap_sums(
                mixed_own,
                0,
                0,
                state,
                own_start,
                STATE_AT - MARGIN,
                height,
                breadth,
                taps.at[pl.ds(base, TAPS)],
            )
        for member in range(5):
            taps[pl.ds(base + TAPS + member, 1), :] = jnp.sum(
                sums[layer, member], axis=0, keepdims=True
            )
        hidden_total = jnp.sum(hidden_sums[layer], axis=0, keepdims=True)
        for group in range(groups):
            taps[pl.ds(base + TAPS + 5 + group, 1), :] = hidden_total[
                :, group * channels : (group + 1) * channels
            ]
    small = taps.shape[0] // BLOCKS
    for layer in range(BLOCKS):
        at = layer * (grads_out.shape[0] // BLOCKS) + 2 * hidden_units
        grads_out[pl.ds(at, small), :] = taps[pl.ds(layer * small, small), :].astype(BF16)


def state_kernel(starts, mixed, within, across, lat_pieces, masked, dw_in, out, wide, kernels, edges):
    height, breadth, channels = masked.shape
    wide[...] = jnp.zeros_like(wide)
    kernels[...] = dw_in[...].astype(F32)
    wide[pl.ds(MARGIN, height), pl.ds(MARGIN, breadth), :] = mixed[...].astype(F32)
    sides = lat_pieces.shape[0]
    inner = MARGIN * breadth
    beside = MARGIN * MARGIN
    for side in range(sides):
        first = starts[1 + side]
        piece = lat_pieces[side].astype(F32)
        for row in range(MARGIN):
            spots = slice(row * breadth, (row + 1) * breadth)
            wide[first + row, pl.ds(MARGIN, breadth), :] = piece[spots]

    def fill_columns(source, place, west):
        column = 0 if west else MARGIN + breadth
        edges[...] = source[...].astype(F32)
        for row in range(height):
            wide[MARGIN + row, pl.ds(column, MARGIN), :] = edges[pl.ds(row * MARGIN, MARGIN), :]
        for side in range(sides):
            piece = lat_pieces[side].astype(F32)
            for row in range(MARGIN):
                at = inner + place * beside + row * MARGIN
                wide[starts[1 + side] + row, pl.ds(column, MARGIN), :] = piece[at : at + MARGIN]

    @pl.when(starts[0] == 0)
    def _():
        fill_columns(within, 0, False)
        fill_columns(across, 1, True)

    @pl.when(starts[0] != 0)
    def _():
        fill_columns(within, 0, True)
        fill_columns(across, 1, False)

    rows = divisor(height, BACK_STEP)

    def advance(step, carry):
        row = step * rows
        spread = conv_rows(wide, row, 0, rows, breadth, kernels, True)
        tile = pl.ds(row, rows)
        shape = (rows, breadth, channels)
        out[tile] = (masked[tile].astype(F32) + spread.reshape(shape)).astype(BF16)
        return carry

    lax.fori_loop(0, height // rows, advance, 0)


def gradient_kernel(grad_norm, held, own, other, *outs):
    kernel, conv_bias, gain, shift, first, first_bias, second, second_bias, scale = outs
    channels = own.shape[1]
    units = second.shape[1]
    groups = units // channels

    def unpack(rows, layer):
        for group in range(groups):
            spots = pl.ds(group * channels, channels)
            first[layer, :, spots] = rows[spots].astype(F32) * grad_norm
        second[layer] = rows[pl.ds(units, units)].astype(F32) * grad_norm
        small = rows[pl.ds(2 * units, rows.shape[0] - 2 * units)].astype(F32) * grad_norm
        for index in range(TAPS):
            kernel[index // KSIZE, index % KSIZE, layer : layer + 1] = small[index : index + 1]
        for member, out in enumerate((scale, second_bias, gain, shift, conv_bias)):
            out[layer : layer + 1] = small[TAPS + member : TAPS + member + 1]
        for group in range(groups):
            row = TAPS + 5 + group
            first_bias[layer : layer + 1, pl.ds(group * channels, channels)] = small[row : row + 1]

    @pl.when(held[0] == 0)
    def _():
        unpack(own, 0)
        unpack(other, 1)

    @pl.when(held[0] != 0)
    def _():
        unpack(own, 1)
        unpack(other, 0)


class Links:
    def __init__(self, mesh):
        self.lon = mesh.shape["lon"]
        self.lat = mesh.shape["lat"]
        self.axes = ("lon", "lat")

    def lon_neighbours(self, within, across):
        there = [place + 1 if place % 2 else place - 1 for place in range(self.lon)]
        pairs = [(place, other % self.lon) for place, other in enumerate(there)]
        across = lax.ppermute(across, "lon", pairs)
        return self.swap(within, 1, 0), across

    def shift_lat(self, values, by):
        pairs = [
            (place, place + by) for place in range(self.lat) if 0 <= place + by < self.lat
        ]
        return lax.ppermute(values, "lat", pairs)

    def lat_neighbours(self, last, first):
        if self.lat == 2:
            return self.swap(last, 0, 1)[None]
        return jnp.stack([self.shift_lat(last, 1), self.shift_lat(first, -1)])

    def swap(self, values, lon_bits, lat_bits):
        pairs = []
        for lon in range(self.lon):
            for lat in range(self.lat):
                there = (lon ^ lon_bits) * self.lat + (lat ^ lat_bits)
                pairs.append((lon * self.lat + lat, there))
        return lax.ppermute(values, self.axes, pairs)

    def sum_all(self, rows, edges, finish):
        lon = lax.axis_index("lon")
        lat = lax.axis_index("lat")
        bits = [(1 << bit, 0) for bit in range(self.lon.bit_length() - 1)]
        bits = bits[:1] + [(0, 1 << bit) for bit in range(self.lat.bit_length() - 1)] + bits[1:]

        def code(group):
            total = jnp.int32(0)
            for index, (lon_bit, lat_bit) in enumerate(group):
                held = (lon // lon_bit) % 2 if lon_bit else (lat // lat_bit) % 2
                total = total + held * (1 << index)
            return total

        def merged(group, choice):
            lon_bits = sum(bit[0] for index, bit in enumerate(group) if choice >> index & 1)
            lat_bits = sum(bit[1] for index, bit in enumerate(group) if choice >> index & 1)
            return lon_bits, lat_bits

        def scatter(values, group):
            count = 1 << len(group)
            pieces = values.reshape(count, -1, values.shape[1])
            here = code(group)
            total = lax.dynamic_index_in_dim(pieces, here, 0, False).astype(F32)
            arrived = []
            for choice in range(1, count):
                sent = lax.dynamic_index_in_dim(pieces, here ^ choice, 0, False)
                arrived.append(self.swap(sent, *merged(group, choice)))
            return total, arrived

        def summed(total, arrived):
            for values in arrived:
                total = total + values.astype(F32)
            return total.astype(BF16)

        def exchange(values, group):
            total = values.astype(F32)
            for choice in range(1, 1 << len(group)):
                total = total + self.swap(values, *merged(group, choice)).astype(F32)
            return total.astype(BF16)

        def gather(values, group):
            count = 1 << len(group)
            pieces = [values]
            for choice in range(1, count):
                pieces.append(self.swap(values, *merged(group, choice)))
            stack = jnp.stack(pieces)
            here = code(group)
            ordered = [
                lax.dynamic_index_in_dim(stack, here ^ place, 0, False) for place in range(count)
            ]
            return jnp.concatenate(ordered, axis=0)

        pair, quad, rest = bits[:1], bits[1:3], bits[3:]
        values = summed(*scatter(rows, pair))
        total, arrived = scatter(values, quad)
        arrived[0], edges = lax.optimization_barrier((arrived[0], edges))
        beside = finish(edges)
        values = summed(total, arrived)
        while rest:
            values = exchange(values, rest[:2])
            rest = rest[2:]
        values = gather(values, quad)
        values, beside = lax.optimization_barrier((values, beside))
        return code(pair), values, self.swap(values, *pair[0]), beside


def on_device(links, state, land_sea, cotangent, *params):
    dw_kernel, weight_in = params[0], params[4]
    height, breadth, channels = state.shape
    hidden_units = weight_in.shape[2]
    groups = hidden_units // channels
    grad_norm = 1.0 / math.sqrt(links.lat * height * links.lon * breadth)
    lat = lax.axis_index("lat")
    sides = 1 if links.lat == 2 else 2
    window_rows = height + sides * WIDE
    first_rows = height + sides * NARROW
    second_rows = height + sides * MARGIN

    def start(margin):
        skipped = WIDE - margin
        return lat * skipped if sides == 1 else jnp.int32(skipped)

    core = lax.axis_index("lon") % 2
    vmem = pl.BlockSpec(memory_space=pltpu.VMEM)
    smem = pl.BlockSpec(memory_space=pltpu.SMEM)
    tile = (height, breadth, channels)

    def flat(values):
        return values.reshape(-1, channels)

    def whole_rows(values, rows):
        return jnp.pad(values, ((0, rows - values.shape[0]), (0, channels - values.shape[1])))

    land = land_sea.T
    marks = (land != 0).astype(BF16)

    packed_rows = round_up((WIDE + MARGIN + 1) * breadth, 16)
    packed = (sides, packed_rows, channels)
    packed = pl.pallas_call(
        pack_kernel,
        out_shape=jax.ShapeDtypeStruct(packed, BF16),
        in_specs=[smem] + [vmem] * 3,
        out_specs=vmem,
        scratch_shapes=[pltpu.VMEM(packed, F32)],
        compiler_params=pltpu.CompilerParams(vmem_limit_bytes=8 * 1024 * 1024),
    )(lat.reshape(1), state, cotangent, land)
    pieces = links.lat_neighbours(packed[0], packed[-1])
    far, near = WIDE * breadth, MARGIN * breadth
    piece_states = pieces[:, :far].reshape(sides, WIDE, breadth, channels)
    piece_cotangents = pieces[:, far : far + near].reshape(sides, MARGIN, breadth, channels)
    piece_marks = pieces[:, far + near : far + near + breadth]

    def lon_columns(wide, narrow, margin):
        own = jnp.concatenate([state[:, wide], cotangent[:, margin]], axis=1)

        def ends(side, above):
            empty = ((NARROW, 0) if above else (0, NARROW), (0, 0), (0, 0))
            near_rows = jnp.pad(piece_cotangents[side][:, margin], empty)
            return jnp.concatenate([piece_states[side][:, wide], near_rows], axis=1)

        if sides == 1:
            rows = jnp.where(
                lat == 0,
                jnp.concatenate([own, ends(0, False)]),
                jnp.concatenate([ends(0, True), own]),
            )
        else:
            rows = jnp.concatenate([ends(0, True), own, ends(1, False)])
        kept = [whole_rows(marks[narrow], 8)]
        kept += [jnp.pad(piece_marks[side][narrow], ((0, 8 - NARROW), (0, 0))) for side in range(sides)]
        return jnp.concatenate([flat(rows), *kept])

    first_columns = lon_columns(slice(0, WIDE), slice(0, NARROW), slice(0, MARGIN))
    last_columns = lon_columns(
        slice(breadth - WIDE, breadth),
        slice(breadth - NARROW, breadth),
        slice(breadth - MARGIN, breadth),
    )
    within, across = links.lon_neighbours(
        jnp.where(core == 0, last_columns, first_columns),
        jnp.where(core == 0, first_columns, last_columns),
    )
    if sides == 1:
        places = [(1 - lat) * height]
        closest = [jnp.where(lat == 0, height, WIDE - MARGIN)]
    else:
        places = [0, WIDE + height]
        closest = [WIDE - MARGIN, WIDE + height]
    starts = [start(0), start(MARGIN), start(NARROW), core, *places, *closest]
    starts = jnp.stack([jnp.asarray(entry, jnp.int32) for entry in starts])
    state_pitch, field_pitch, inner_pitch = (
        round_up(breadth + size, 8) for size in (STATE_AT + WIDE, FIELD_AT + NARROW, NARROW)
    )

    padded_rows = window_rows + 2 * MARGIN + 1
    all_cells = second_rows * inner_pitch
    layer_rows = round_up(2 * hidden_units + TAPS + 5 + groups, 4 * 16)
    small_rows = BLOCKS * (layer_rows - 2 * hidden_units)
    grad_rows = BLOCKS * layer_rows
    own_rows = (window_rows, breadth)
    edge_rows = round_up(height * MARGIN, 8)
    scratch = [
        pltpu.VMEM((padded_rows, state_pitch, channels), F32),
        pltpu.VMEM((padded_rows, field_pitch, channels), F32),
        pltpu.VMEM((BLOCKS, TAPS, channels), F32),
        pltpu.VMEM((padded_rows, field_pitch, channels), F32),
        pltpu.VMEM((padded_rows, inner_pitch, channels), F32),
        pltpu.VMEM((window_rows, inner_pitch, channels), F32),
        pltpu.VMEM(own_rows + (channels,), F32),
        pltpu.VMEM(own_rows + (channels,), F32),
        pltpu.VMEM(own_rows + (channels,), F32),
        pltpu.VMEM(own_rows + (hidden_units,), F32),
        pltpu.VMEM(own_rows + (hidden_units,), BF16),
        pltpu.VMEM((height, breadth, hidden_units), BF16),
        pltpu.VMEM(own_rows + (channels,), BF16),
        pltpu.VMEM(tile, BF16),
        pltpu.VMEM(tile, F32),
        pltpu.VMEM((all_cells, hidden_units), BF16),
        pltpu.VMEM((all_cells, hidden_units), BF16),
        pltpu.VMEM((all_cells, channels), BF16),
        pltpu.VMEM((all_cells, channels), BF16),
        pltpu.VMEM((BLOCKS, 5, 8, channels), F32),
        pltpu.VMEM((BLOCKS, 8, hidden_units), F32),
        pltpu.VMEM((small_rows, channels), F32),
        pltpu.VMEM(within.shape, F32),
        pltpu.VMEM((2, edge_rows, channels), F32),
    ]
    sizes = (height, breadth, first_rows, second_rows, window_rows)
    taps_in = dw_kernel.reshape(BLOCKS, TAPS, channels)
    output, grad_mixed, masked, mixed_edges, grads = pl.pallas_call(
        functools.partial(tile_kernel, sizes),
        out_shape=(
            jax.ShapeDtypeStruct(tile, BF16),
            jax.ShapeDtypeStruct(tile, BF16),
            jax.ShapeDtypeStruct(tile, BF16),
            jax.ShapeDtypeStruct((2, edge_rows, channels), BF16),
            jax.ShapeDtypeStruct((grad_rows, channels), BF16),
        ),
        in_specs=[smem] + [vmem] * 15,
        out_specs=(vmem,) * 5,
        scratch_shapes=scratch,
        compiler_params=pltpu.CompilerParams(vmem_limit_bytes=48 * 1024 * 1024),
        cost_estimate=pl.CostEstimate(
            flops=20 * all_cells * channels * hidden_units,
            bytes_accessed=4 * height * breadth * channels * 4,
            transcendentals=0,
        ),
    )(starts, state, cotangent, land, pieces, within, across, taps_in, *params[1:])

    def finish(mixed_edges):
        within, across = links.lon_neighbours(mixed_edges[0], mixed_edges[1])
        corner = MARGIN * MARGIN

        def corner_rows(rows, first):
            beside = slice(first * MARGIN, first * MARGIN + corner)
            parts = jnp.concatenate([flat(grad_mixed[rows]), within[beside], across[beside]])
            return jnp.pad(parts, ((0, -parts.shape[0] % 16), (0, 0)))

        last = corner_rows(slice(height - MARGIN, height), height - MARGIN)
        first = corner_rows(slice(0, MARGIN), 0)
        if sides == 1:
            last = first = jnp.where(lat == 0, last, first)
        pieces = links.lat_neighbours(last, first)
        if sides == 1:
            places = [(1 - lat) * (MARGIN + height)]
        else:
            places = [0, MARGIN + height]
        starts = jnp.stack([jnp.asarray(entry, jnp.int32) for entry in (core, *places)])
        wide = (height + 2 * MARGIN + 1, round_up(breadth + 2 * MARGIN, 8), channels)
        return pl.pallas_call(
            state_kernel,
            out_shape=jax.ShapeDtypeStruct(tile, BF16),
            in_specs=[smem] + [vmem] * 6,
            out_specs=vmem,
            scratch_shapes=[
                pltpu.VMEM(wide, F32),
                pltpu.VMEM((TAPS, channels), F32),
                pltpu.VMEM((edge_rows, channels), F32),
            ],
            compiler_params=pltpu.CompilerParams(vmem_limit_bytes=16 * 1024 * 1024),
            cost_estimate=pl.CostEstimate(
                flops=4_000_000_000, bytes_accessed=8_000_000, transcendentals=0
            ),
        )(starts, grad_mixed, within, across, pieces, masked, taps_in[0])

    held, own, other, grad_state = links.sum_all(grads, mixed_edges, finish)
    shapes = [(KSIZE, KSIZE, BLOCKS, channels)] + [member.shape for member in params[1:]]
    grad_kernel, *gradients = pl.pallas_call(
        functools.partial(gradient_kernel, grad_norm),
        out_shape=tuple(jax.ShapeDtypeStruct(shape, F32) for shape in shapes),
        in_specs=[smem, vmem, vmem],
        out_specs=(vmem,) * 9,
        compiler_params=pltpu.CompilerParams(vmem_limit_bytes=8 * 1024 * 1024),
    )(held.reshape(1), own, other)
    return (output, grad_state, grad_kernel.transpose(2, 0, 1, 3), *gradients)


def solution(mesh):
    tile = P("lat", "lon", None)
    placed = (tile, P("lat", "lon"), tile) + (P(),) * 9
    return jax.shard_map(
        functools.partial(on_device, Links(mesh)),
        mesh=mesh,
        in_specs=placed,
        out_specs=(tile, tile) + (P(),) * 9,
        check_vma=False,
    )
```

```python
import functools
import math

import jax
import jax.numpy as jnp
from jax import lax
from jax.experimental import pallas as pl
from jax.experimental.pallas import tpu as pltpu
from jax.sharding import PartitionSpec as P

KSIZE = 7
MARGIN = KSIZE // 2
TAPS = KSIZE * KSIZE
BLOCKS = 2
EPS_NORM = 1e-06
INV_ROOT_TWO = 0.7071067811865476
INV_ROOT_TWO_PI = 0.3989422804014327
LAND = 1024.0
LAND_BOUND = 512.0
VMEM_LIMIT = 48 * 1024 * 1024
PACK_LIMIT = 62 * 1024 * 1024
F32 = jnp.float32
BF16 = jnp.bfloat16
FIRST_STEP = 19
SECOND_STEP = 17
BACK_STEP = 45
TAP_STEP = 9
STATE_AT = 11
FIELD_AT = 8
INNER_AT = 3
WIDE = 3 * MARGIN
NARROW = 2 * MARGIN


def divisor(size, most):
    return max(step for step in range(1, most + 1) if size % step == 0)


def round_up(size, unit):
    return (size + unit - 1) // unit * unit


def pack_rows(above, below):
    shape = (above.shape[0] // 8, 8, above.shape[1])
    return jnp.concatenate([above.reshape(shape), below.reshape(shape)], axis=1).astype(BF16)


def conv_rows(source, base, first, count, width, kernel_ref, flip):
    pairs = (count + 1) // 2
    sums = [[None, None] for _ in range(pairs)]
    channels = source.shape[2]
    for tap_col in range(KSIZE):
        parts = [None] * pairs
        taps = []
        for tap_row in range(KSIZE):
            index = tap_row * KSIZE + tap_col
            tap = kernel_ref[pl.ds(TAPS - 1 - index if flip else index, 1), :]
            taps.append(jnp.broadcast_to(tap, (16, channels)).astype(BF16)[None])
        above = source[base, pl.ds(first + tap_col, width), :]
        for row in range(2 * pairs + KSIZE - 2):
            below = source[base + row + 1, pl.ds(first + tap_col, width), :]
            both = pack_rows(above, below)
            above = below
            for tap_row in range(row % 2, KSIZE, 2):
                out = (row - tap_row) // 2
                if 0 <= out < pairs:
                    term = both * taps[tap_row]
                    parts[out] = term if parts[out] is None else parts[out] + term
        for out in range(pairs):
            for side in range(2):
                value = parts[out].astype(F32)[:, 8 * side : 8 * side + 8]
                old = sums[out][side]
                sums[out][side] = value if old is None else old + value
    rows = [sums[row // 2][row % 2].reshape(width, channels) for row in range(count)]
    return jnp.concatenate(rows, axis=0)


def normal_parts(hidden):
    cumulative = 0.5 + 0.5 * lax.erf(hidden * INV_ROOT_TWO)
    return cumulative, jnp.exp(-0.5 * hidden * hidden)


def fold(values):
    return jnp.sum(values.reshape(values.shape[0] // 8, 8, values.shape[1]), axis=0)


def normalise(mixed):
    center = mixed - jnp.mean(mixed, axis=-1, keepdims=True)
    inverse = lax.rsqrt(jnp.mean(center * center, axis=-1, keepdims=True) + EPS_NORM)
    return center * inverse, inverse


def normalise_back(grad, normed, inverse):
    return inverse * (
        grad
        - jnp.mean(grad, axis=-1, keepdims=True)
        - normed * jnp.mean(grad * normed, axis=-1, keepdims=True)
    )


def rows_of(ref, base, first, count, width):
    return jnp.concatenate(
        [ref[base + row, pl.ds(first, width), :] for row in range(count)], axis=0
    )


CONTRACT_COLS = (((1,), (1,)), ((), ()))
CONTRACT_ROWS = (((0,), (0,)), ((), ()))


def dot(left, right):
    return jnp.dot(left, right, preferred_element_type=F32)


def dot_cols(left, right):
    return lax.dot_general(left, right, CONTRACT_COLS, preferred_element_type=F32)


def dot_rows(left, right):
    return lax.dot_general(left, right, CONTRACT_ROWS, preferred_element_type=F32)


def tap_sums(grad_ref, grad_row, grad_col, field_ref, field_row, field_col, height, width, out):
    rows = divisor(height, TAP_STEP)
    pairs = (rows + 1) // 2
    for cols in ((0, 1, 2, 3), (4, 5, 6)):

        def advance(step, sums):
            sums = list(sums)
            at = step * rows
            grads = [grad_ref[grad_row + at + row, pl.ds(grad_col, width), :] for row in range(rows)]
            grads += [jnp.zeros_like(grads[0])] * (2 * pairs - rows)
            grads = [pack_rows(grads[2 * pair], grads[2 * pair + 1]) for pair in range(pairs)]
            for place, tap_col in enumerate(cols):
                spots = pl.ds(field_col + tap_col, width)
                parts = [None] * KSIZE
                above = field_ref[field_row + at, spots, :]
                for row in range(2 * pairs + KSIZE - 2):
                    below = field_ref[field_row + at + row + 1, spots, :]
                    both = pack_rows(above, below)
                    above = below
                    for tap_row in range(row % 2, KSIZE, 2):
                        pair = (row - tap_row) // 2
                        if 0 <= pair < pairs:
                            term = grads[pair] * both
                            old = parts[tap_row]
                            parts[tap_row] = term if old is None else old + term
                for tap_row in range(KSIZE):
                    part = parts[tap_row]
                    total = part[0]
                    for group in range(1, part.shape[0]):
                        total = total + part[group]
                    index = place * KSIZE + tap_row
                    sums[index] = sums[index] + fold(total.astype(F32))
            return tuple(sums)

        zeros = tuple(jnp.zeros((8, grad_ref.shape[2]), F32) for _ in range(KSIZE * len(cols)))
        sums = lax.fori_loop(0, height // rows, advance, zeros)
        for place, tap_col in enumerate(cols):
            for tap_row in range(KSIZE):
                total = jnp.sum(sums[place * KSIZE + tap_row], axis=0, keepdims=True)
                out[pl.ds(tap_row * KSIZE + tap_col, 1), :] = total


def pack_kernel(lat, state, cotangent, land_sea, out, rows, far_rows, near_rows, land, arrived):
    height, breadth = state.shape[:2]
    sides = out.shape[0]
    copies = [pltpu.make_async_copy(land_sea, land, arrived.at[0])]
    for side in range(sides):
        last = lat[0] == 0 if sides == 1 else side == 0
        first = jnp.where(last, height - WIDE, 0)
        closest = jnp.where(last, height - MARGIN, 0)
        source = state.at[pl.ds(first, WIDE)]
        copies.append(pltpu.make_async_copy(source, far_rows.at[side], arrived.at[1 + side]))
        source = cotangent.at[pl.ds(closest, MARGIN)]
        copies.append(
            pltpu.make_async_copy(source, near_rows.at[side], arrived.at[1 + sides + side])
        )
    for copy in copies:
        copy.start()
    rows[...] = jnp.zeros_like(rows)
    for copy in copies:
        copy.wait()
    ocean = jnp.where(land[...] != 0, 1.0, 0.0).astype(F32)
    far, near = WIDE * breadth, MARGIN * breadth
    for side in range(sides):
        last = lat[0] == 0 if sides == 1 else side == 0
        for row in range(WIDE):
            rows[side, pl.ds(row * breadth, breadth), :] = far_rows[side, row].astype(F32)
        for row in range(MARGIN):
            spots = pl.ds(far + row * breadth, breadth)
            rows[side, spots, :] = near_rows[side, row].astype(F32)
        marks = jnp.where(last, ocean[:, height - WIDE :], ocean[:, :WIDE])
        rows[side, pl.ds(far + near, breadth), pl.ds(0, WIDE)] = marks
    out[...] = rows[...].astype(BF16)


def fill_windows(sizes, starts, sources, state, coded, edges):
    height, breadth, window_rows = sizes
    state_tile, cotangent, land_sea, lat_pieces, within, across = sources
    channels = state.shape[2]
    pad = MARGIN
    own = pad + starts[0]
    lower = starts[3] == 0
    state[pl.ds(pad, window_rows)] = jnp.zeros((window_rows,) + state.shape[1:], F32)
    coded[pl.ds(pad, window_rows)] = jnp.zeros((window_rows,) + coded.shape[1:], F32)

    def spread(marks, column):
        return jnp.broadcast_to(marks[:, column : column + 1], (marks.shape[0], channels))

    state[pl.ds(own, height), pl.ds(STATE_AT, breadth), :] = state_tile[...].astype(F32)
    ocean = jnp.where(land_sea[...] != 0, 1.0, 0.0).astype(F32)
    for row in range(height):
        value = jnp.where(spread(ocean, row) > 0.5, cotangent[row].astype(F32), LAND)
        coded[own + row, pl.ds(FIELD_AT, breadth), :] = value

    sides = lat_pieces.shape[0]
    far, near = WIDE * breadth, MARGIN * breadth
    for side in range(sides):
        first = pad + starts[4 + side]
        closest = pad + starts[4 + sides + side]
        piece = lat_pieces[side].astype(F32)
        marks = piece[far + near : far + near + breadth]
        for row in range(WIDE):
            spots = pl.ds(row * breadth, breadth)
            state[first + row, pl.ds(STATE_AT, breadth), :] = lat_pieces[side, spots].astype(F32)
            value = jnp.where(spread(marks, row) > 0.5, 0.0, LAND)
            coded[first + row, pl.ds(FIELD_AT, breadth), :] = value
        for row in range(MARGIN):
            value = piece[far + row * breadth : far + (row + 1) * breadth]
            old = coded[closest + row, pl.ds(FIELD_AT, breadth), :]
            value = jnp.where(old > LAND_BOUND, LAND, value)
            coded[closest + row, pl.ds(FIELD_AT, breadth), :] = value

    group = WIDE + MARGIN

    def fill_columns(source, west):
        edges[...] = source[...].astype(F32)
        state_at = STATE_AT - WIDE if west else STATE_AT + breadth
        mark_at = FIELD_AT - NARROW if west else FIELD_AT + breadth
        value_at = FIELD_AT - MARGIN if west else FIELD_AT + breadth
        shown = slice(NARROW - MARGIN, NARROW) if west else slice(0, MARGIN)
        spans = [(own - pad, height, 0)] + [(starts[4 + side], WIDE, side + 1) for side in range(sides)]
        for first, count, place in spans:
            marks = edges[pl.ds(window_rows * group + place * 8, 8), :]
            for row in range(count):
                at = pad + first + row
                lines = (first + row) * group
                state[at, pl.ds(state_at, WIDE), :] = edges[pl.ds(lines, WIDE), :]
                mark = spread(marks, row)[:NARROW]
                coded[at, pl.ds(mark_at, NARROW), :] = jnp.where(mark > 0.5, 0.0, LAND)
                value = jnp.where(mark[shown] > 0.5, edges[pl.ds(lines + WIDE, MARGIN), :], LAND)
                coded[at, pl.ds(value_at, MARGIN), :] = value

    @pl.when(lower)
    def _():
        fill_columns(across, True)
        fill_columns(within, False)

    @pl.when(jnp.logical_not(lower))
    def _():
        fill_columns(within, True)
        fill_columns(across, False)


def tile_kernel(
    sizes,
    starts,
    state_tile,
    cotangent,
    land_sea,
    lat_pieces,
    within,
    across,
    dw_in,
    conv_bias,
    norm_gain,
    norm_bias,
    weight_in,
    bias_in,
    weight_out,
    bias_out,
    layer_scale,
    output,
    mixed_out,
    masked_out,
    edges_out,
    grads_out,
    state,
    coded,
    kernels,
    field,
    inner,
    result,
    normed_own,
    inverse_own,
    branch_own,
    slope_own,
    active_own,
    hidden_own,
    lifted_own,
    branch_grad_own,
    mixed_own,
    active_all,
    hidden_all,
    lifted_all,
    branch_grad_all,
    sums,
    hidden_sums,
    taps,
    edges,
    mixed_edges,
):
    height, breadth, first_rows, second_rows, window_rows = sizes
    channels = state.shape[2]
    own_start = starts[0]
    second_start = starts[1]
    first_start = starts[2]
    first_width = field.shape[1]
    second_width = inner.shape[1]
    pad = MARGIN

    for ref in (state, coded, field, inner):
        ref[pl.ds(0, pad)] = jnp.zeros((pad,) + ref.shape[1:], F32)
        below = ref.shape[0] - pad - window_rows
        ref[pl.ds(pad + window_rows, below)] = jnp.zeros((below,) + ref.shape[1:], F32)
    state[pl.ds(pad, window_rows)] = jnp.zeros((window_rows,) + state.shape[1:], F32)
    coded[pl.ds(pad, window_rows)] = jnp.zeros((window_rows,) + coded.shape[1:], F32)

    fill_windows(
        (height, breadth, window_rows),
        starts,
        (state_tile, cotangent, land_sea, lat_pieces, within, across),
        state,
        coded,
        edges,
    )
    kernels[...] = dw_in[...].astype(F32)
    sums[...] = jnp.zeros_like(sums)
    hidden_sums[...] = jnp.zeros_like(hidden_sums)

    def param(ref, layer):
        return ref[pl.ds(layer, 1), :]

    first_step = divisor(first_rows, FIRST_STEP)

    def forward_first(step, carry):
        row = first_start + step * first_step
        cells = first_step * first_width
        mixed = conv_rows(state, row, 0, first_step, first_width, kernels.at[0], False)
        normed, inverse = normalise(mixed + param(conv_bias, 0))
        lifted = (normed * param(norm_gain, 0) + param(norm_bias, 0)).astype(BF16)
        hidden = dot(lifted, weight_in[0]) + param(bias_in, 0)
        cumulative, bell = normal_parts(hidden)
        active = hidden * cumulative
        branch = dot(active.astype(BF16), weight_out[0]) + param(bias_out, 0)
        center = rows_of(state, row + pad, MARGIN, first_step, first_width)
        mark = rows_of(coded, row + pad, 0, first_step, first_width)
        value = jnp.where(mark < LAND_BOUND, center + param(layer_scale, 0) * branch, 0.0)
        value = value.reshape(first_step, first_width, channels)

        for index in range(first_step):
            field[row + pad + index] = value[index]

        def own(values):
            shape = (first_step, first_width, values.shape[1])
            return values.reshape(shape)[:, FIELD_AT : FIELD_AT + breadth]

        slope = own(cumulative) + own(hidden) * (own(bell) * INV_ROOT_TWO_PI)
        spots = pl.ds(row, first_step)
        slope_own[spots] = slope
        active_own[spots] = own(active).astype(BF16)
        normed_own[spots] = own(normed)
        inverse_own[spots] = own(jnp.broadcast_to(inverse, normed.shape))
        branch_own[spots] = own(branch)
        lifted_own[spots] = own(normed * param(norm_gain, 0) + param(norm_bias, 0)).astype(BF16)
        return carry

    lax.fori_loop(0, first_rows // first_step, forward_first, 0)

    second_step = divisor(second_rows, SECOND_STEP)

    def both_second(step, carry):
        row = second_start + step * second_step
        cells = second_step * second_width
        shift = FIELD_AT - INNER_AT
        mixed = conv_rows(
            field, row, shift - MARGIN, second_step, second_width, kernels.at[1], False
        )
        normed, inverse = normalise(mixed + param(conv_bias, 1))
        lifted = normed * param(norm_gain, 1) + param(norm_bias, 1)
        hidden = dot(lifted.astype(BF16), weight_in[1]) + param(bias_in, 1)
        cumulative, bell = normal_parts(hidden)
        active = (hidden * cumulative).astype(BF16)
        branch = dot(active, weight_out[1]) + param(bias_out, 1)
        center = rows_of(field, row + pad, shift, second_step, second_width)
        mark = rows_of(coded, row + pad, shift, second_step, second_width)
        ocean = mark < LAND_BOUND
        value = jnp.where(ocean, center + param(layer_scale, 1) * branch, 0.0)
        value = value.reshape(second_step, second_width, channels)
        masked = jnp.where(ocean, mark, 0.0)
        grad_branch = (masked * param(layer_scale, 1)).astype(BF16)
        grad_active = dot_cols(grad_branch, weight_out[1])
        slope = cumulative + hidden * (bell * INV_ROOT_TWO_PI)
        grad_hidden = (grad_active * slope).astype(BF16)
        grad_lifted = dot_cols(grad_hidden, weight_in[1])
        grad_mixed = normalise_back(grad_lifted * param(norm_gain, 1), normed, inverse)
        grad_mixed = grad_mixed.reshape(second_step, second_width, channels)
        for index in range(second_step):
            result[row + index] = value[index]
            inner[row + pad + index] = grad_mixed[index]

        shape = (second_step, second_width, channels)
        row_of = lax.broadcasted_iota(jnp.int32, shape, 0) + (row - own_start)
        col_of = lax.broadcasted_iota(jnp.int32, shape, 1) - INNER_AT
        inside = (row_of >= 0) & (row_of < height) & (col_of >= 0) & (col_of < breadth)
        inside = jnp.where(inside, 1.0, 0.0).astype(F32).reshape(cells, channels)
        own_lifted = grad_lifted * inside
        own_branch = grad_branch.astype(F32) * inside
        sums[1, 0] += fold(masked * branch * inside)
        sums[1, 1] += fold(own_branch)
        sums[1, 2] += fold(own_lifted * normed)
        sums[1, 3] += fold(own_lifted)
        wide = jnp.concatenate([inside] * (hidden.shape[1] // channels), axis=1)
        hidden_sums[1] += fold(grad_hidden.astype(F32) * wide)
        spots = pl.ds(pl.multiple_of(step * cells, cells), cells)
        active_all[spots] = active
        hidden_all[spots] = grad_hidden
        lifted_all[spots] = (lifted * inside).astype(BF16)
        branch_grad_all[spots] = own_branch.astype(BF16)
        return carry

    lax.fori_loop(0, second_rows // second_step, both_second, 0)

    back_step = divisor(height, BACK_STEP)

    def backward_first(step, carry):
        row = own_start + step * back_step
        cells = back_step * breadth
        mark = rows_of(coded, row + pad, FIELD_AT, back_step, breadth)
        ocean = mark < LAND_BOUND
        masked_next = jnp.where(ocean, mark, 0.0)
        spread = conv_rows(inner, row, 0, back_step, breadth, kernels.at[1], True)
        masked = jnp.where(ocean, masked_next + spread, 0.0)
        grad_branch = (masked * param(layer_scale, 0)).astype(BF16)
        grad_active = dot_cols(grad_branch, weight_out[0])
        slope = slope_own[pl.ds(row, back_step)].reshape(cells, grad_active.shape[1])
        grad_hidden = (grad_active * slope).astype(BF16)
        grad_lifted = dot_cols(grad_hidden, weight_in[0])
        normed = normed_own[pl.ds(row, back_step)].reshape(cells, channels)
        inverse = inverse_own[pl.ds(row, back_step)].reshape(cells, channels)
        grad_mixed = normalise_back(grad_lifted * param(norm_gain, 0), normed, inverse)
        branch = branch_own[pl.ds(row, back_step)].reshape(cells, channels)
        sums[0, 0] += fold(masked * branch)
        sums[0, 1] += fold(grad_branch.astype(F32))
        sums[0, 2] += fold(grad_lifted * normed)
        sums[0, 3] += fold(grad_lifted)
        sums[0, 4] += fold(grad_mixed)
        hidden_sums[0] += fold(grad_hidden.astype(F32))
        inner_rows = rows_of(inner, row + pad, INNER_AT, back_step, breadth)
        sums[1, 4] += fold(inner_rows)
        tile = pl.ds(step * back_step, back_step)
        shape = (back_step, breadth, channels)
        grad_mixed = grad_mixed.reshape(shape)
        mixed_own[tile] = grad_mixed
        mixed_out[tile] = grad_mixed.astype(BF16)
        masked_out[tile] = masked.reshape(shape).astype(BF16)
        hidden_own[tile] = grad_hidden.reshape(back_step, breadth, grad_hidden.shape[1])
        branch_grad_own[tile] = grad_branch.reshape(shape)
        value = rows_of(result, row, INNER_AT, back_step, breadth)
        output[tile] = value.reshape(shape).astype(BF16)
        return carry

    lax.fori_loop(0, height // back_step, backward_first, 0)

    mixed_edges[...] = jnp.zeros_like(mixed_edges)
    lower = starts[3] == 0
    for row in range(height):
        first = mixed_own[row, pl.ds(0, MARGIN), :]
        last = mixed_own[row, pl.ds(breadth - MARGIN, MARGIN), :]
        spots = pl.ds(row * MARGIN, MARGIN)
        mixed_edges[0, spots] = jnp.where(lower, last, first)
        mixed_edges[1, spots] = jnp.where(lower, first, last)
    edges_out[...] = mixed_edges[...].astype(BF16)

    hidden_units = weight_in.shape[2]
    groups = hidden_units // channels
    tile = pl.ds(own_start, height)
    cells = height * breadth

    def flat(ref, spots):
        return ref[spots].reshape(cells, ref.shape[2])

    operands = (
        (
            flat(lifted_own, tile),
            flat(hidden_own, pl.ds(0, height)),
            flat(active_own, tile),
            flat(branch_grad_own, pl.ds(0, height)),
        ),
        (lifted_all[...], hidden_all[...], active_all[...], branch_grad_all[...]),
    )
    for layer, (lifted, grad_hidden, active, grad_branch) in enumerate(operands):
        at = layer * (grads_out.shape[0] // BLOCKS)
        grad_in = dot_rows(lifted, grad_hidden)
        for group in range(groups):
            grads_out[pl.ds(at + group * channels, channels), :] = grad_in[
                :, group * channels : (group + 1) * channels
            ].astype(BF16)
        grad_out = dot_rows(grad_branch, active)
        for group in range(groups):
            grads_out[pl.ds(at + hidden_units + group * channels, channels), :] = grad_out[
                :, group * channels : (group + 1) * channels
            ].T.astype(BF16)

    taps[...] = jnp.zeros_like(taps)
    for layer in range(BLOCKS):
        base = layer * (taps.shape[0] // BLOCKS)
        if layer:
            tap_sums(
                inner,
                own_start + pad,
                INNER_AT,
                field,
                own_start,
                FIELD_AT - MARGIN,
                height,
                breadth,
                taps.at[pl.ds(base, TAPS)],
            )
        else:
            tap_sums(
                mixed_own,
                0,
                0,
                state,
                own_start,
                STATE_AT - MARGIN,
                height,
                breadth,
                taps.at[pl.ds(base, TAPS)],
            )
        for member in range(5):
            taps[pl.ds(base + TAPS + member, 1), :] = jnp.sum(
                sums[layer, member], axis=0, keepdims=True
            )
        hidden_total = jnp.sum(hidden_sums[layer], axis=0, keepdims=True)
        for group in range(groups):
            taps[pl.ds(base + TAPS + 5 + group, 1), :] = hidden_total[
                :, group * channels : (group + 1) * channels
            ]
    small = taps.shape[0] // BLOCKS
    for layer in range(BLOCKS):
        at = layer * (grads_out.shape[0] // BLOCKS) + 2 * hidden_units
        grads_out[pl.ds(at, small), :] = taps[pl.ds(layer * small, small), :].astype(BF16)


def state_kernel(starts, mixed, within, across, lat_pieces, masked, dw_in, out, wide, kernels, edges):
    height, breadth, channels = masked.shape
    wide[...] = jnp.zeros_like(wide)
    kernels[...] = dw_in[...].astype(F32)
    wide[pl.ds(MARGIN, height), pl.ds(MARGIN, breadth), :] = mixed[...].astype(F32)
    sides = lat_pieces.shape[0]
    inner = MARGIN * breadth
    beside = MARGIN * MARGIN
    for side in range(sides):
        first = starts[1 + side]
        piece = lat_pieces[side].astype(F32)
        for row in range(MARGIN):
            spots = slice(row * breadth, (row + 1) * breadth)
            wide[first + row, pl.ds(MARGIN, breadth), :] = piece[spots]

    def fill_columns(source, place, west):
        column = 0 if west else MARGIN + breadth
        edges[...] = source[...].astype(F32)
        for row in range(height):
            wide[MARGIN + row, pl.ds(column, MARGIN), :] = edges[pl.ds(row * MARGIN, MARGIN), :]
        for side in range(sides):
            piece = lat_pieces[side].astype(F32)
            for row in range(MARGIN):
                at = inner + place * beside + row * MARGIN
                wide[starts[1 + side] + row, pl.ds(column, MARGIN), :] = piece[at : at + MARGIN]

    @pl.when(starts[0] == 0)
    def _():
        fill_columns(within, 0, False)
        fill_columns(across, 1, True)

    @pl.when(starts[0] != 0)
    def _():
        fill_columns(within, 0, True)
        fill_columns(across, 1, False)

    rows = divisor(height, BACK_STEP)

    def advance(step, carry):
        row = step * rows
        spread = conv_rows(wide, row, 0, rows, breadth, kernels, True)
        tile = pl.ds(row, rows)
        shape = (rows, breadth, channels)
        out[tile] = (masked[tile].astype(F32) + spread.reshape(shape)).astype(BF16)
        return carry

    lax.fori_loop(0, height // rows, advance, 0)


def gradient_kernel(grad_norm, held, own, other, *outs):
    kernel, conv_bias, gain, shift, first, first_bias, second, second_bias, scale = outs
    channels = own.shape[1]
    units = second.shape[1]
    groups = units // channels

    def unpack(rows, layer):
        for group in range(groups):
            spots = pl.ds(group * channels, channels)
            first[layer, :, spots] = rows[spots].astype(F32) * grad_norm
        second[layer] = rows[pl.ds(units, units)].astype(F32) * grad_norm
        small = rows[pl.ds(2 * units, rows.shape[0] - 2 * units)].astype(F32) * grad_norm
        for index in range(TAPS):
            kernel[index // KSIZE, index % KSIZE, layer : layer + 1] = small[index : index + 1]
        for member, out in enumerate((scale, second_bias, gain, shift, conv_bias)):
            out[layer : layer + 1] = small[TAPS + member : TAPS + member + 1]
        for group in range(groups):
            row = TAPS + 5 + group
            first_bias[layer : layer + 1, pl.ds(group * channels, channels)] = small[row : row + 1]

    @pl.when(held[0] == 0)
    def _():
        unpack(own, 0)
        unpack(other, 1)

    @pl.when(held[0] != 0)
    def _():
        unpack(own, 1)
        unpack(other, 0)


class Links:
    def __init__(self, mesh):
        self.lon = mesh.shape["lon"]
        self.lat = mesh.shape["lat"]
        self.axes = ("lon", "lat")

    def lon_neighbours(self, within, across):
        there = [place + 1 if place % 2 else place - 1 for place in range(self.lon)]
        pairs = [(place, other % self.lon) for place, other in enumerate(there)]
        across = lax.ppermute(across, "lon", pairs)
        return self.swap(within, 1, 0), across

    def shift_lat(self, values, by):
        pairs = [
            (place, place + by) for place in range(self.lat) if 0 <= place + by < self.lat
        ]
        return lax.ppermute(values, "lat", pairs)

    def lat_neighbours(self, last, first):
        if self.lat == 2:
            return self.swap(last, 0, 1)[None]
        return jnp.stack([self.shift_lat(last, 1), self.shift_lat(first, -1)])

    def swap(self, values, lon_bits, lat_bits):
        pairs = []
        for lon in range(self.lon):
            for lat in range(self.lat):
                there = (lon ^ lon_bits) * self.lat + (lat ^ lat_bits)
                pairs.append((lon * self.lat + lat, there))
        return lax.ppermute(values, self.axes, pairs)

    def sum_all(self, rows, edges, finish):
        lon = lax.axis_index("lon")
        lat = lax.axis_index("lat")
        bits = [(1 << bit, 0) for bit in range(self.lon.bit_length() - 1)]
        bits = bits[:1] + [(0, 1 << bit) for bit in range(self.lat.bit_length() - 1)] + bits[1:]

        def code(group):
            total = jnp.int32(0)
            for index, (lon_bit, lat_bit) in enumerate(group):
                held = (lon // lon_bit) % 2 if lon_bit else (lat // lat_bit) % 2
                total = total + held * (1 << index)
            return total

        def merged(group, choice):
            lon_bits = sum(bit[0] for index, bit in enumerate(group) if choice >> index & 1)
            lat_bits = sum(bit[1] for index, bit in enumerate(group) if choice >> index & 1)
            return lon_bits, lat_bits

        def scatter(values, group):
            count = 1 << len(group)
            pieces = values.reshape(count, -1, values.shape[1])
            here = code(group)
            total = lax.dynamic_index_in_dim(pieces, here, 0, False).astype(F32)
            arrived = []
            for choice in range(1, count):
                sent = lax.dynamic_index_in_dim(pieces, here ^ choice, 0, False)
                arrived.append(self.swap(sent, *merged(group, choice)))
            return total, arrived

        def summed(total, arrived):
            for values in arrived:
                total = total + values.astype(F32)
            return total.astype(BF16)

        def exchange(values, group):
            total = values.astype(F32)
            for choice in range(1, 1 << len(group)):
                total = total + self.swap(values, *merged(group, choice)).astype(F32)
            return total.astype(BF16)

        def gather(values, group):
            count = 1 << len(group)
            pieces = [values]
            for choice in range(1, count):
                pieces.append(self.swap(values, *merged(group, choice)))
            stack = jnp.stack(pieces)
            here = code(group)
            ordered = [
                lax.dynamic_index_in_dim(stack, here ^ place, 0, False) for place in range(count)
            ]
            return jnp.concatenate(ordered, axis=0)

        pair, quad, rest = bits[:1], bits[1:3], bits[3:]
        values = summed(*scatter(rows, pair))
        total, arrived = scatter(values, quad)
        arrived[0], edges = lax.optimization_barrier((arrived[0], edges))
        beside = finish(edges)
        values = summed(total, arrived)
        while rest:
            values = exchange(values, rest[:2])
            rest = rest[2:]
        values = gather(values, quad)
        values, beside = lax.optimization_barrier((values, beside))
        return code(pair), values, self.swap(values, *pair[0]), beside


def on_device(links, state, land_sea, cotangent, *params):
    dw_kernel, weight_in = params[0], params[4]
    height, breadth, channels = state.shape
    hidden_units = weight_in.shape[2]
    groups = hidden_units // channels
    grad_norm = 1.0 / math.sqrt(links.lat * height * links.lon * breadth)
    lat = lax.axis_index("lat")
    sides = 1 if links.lat == 2 else 2
    window_rows = height + sides * WIDE
    first_rows = height + sides * NARROW
    second_rows = height + sides * MARGIN

    def start(margin):
        skipped = WIDE - margin
        return lat * skipped if sides == 1 else jnp.int32(skipped)

    core = lax.axis_index("lon") % 2
    vmem = pl.BlockSpec(memory_space=pltpu.VMEM)
    smem = pl.BlockSpec(memory_space=pltpu.SMEM)
    tile = (height, breadth, channels)

    def flat(values):
        return values.reshape(-1, channels)

    def whole_rows(values, rows):
        return jnp.pad(values, ((0, rows - values.shape[0]), (0, channels - values.shape[1])))

    land = land_sea.T
    marks = (land != 0).astype(BF16)

    packed_rows = round_up((WIDE + MARGIN + 1) * breadth, 16)
    packed = (sides, packed_rows, channels)
    packed = pl.pallas_call(
        pack_kernel,
        out_shape=jax.ShapeDtypeStruct(packed, BF16),
        in_specs=[smem] + [pl.BlockSpec(memory_space=pl.ANY)] * 3,
        out_specs=vmem,
        scratch_shapes=[
            pltpu.VMEM(packed, F32),
            pltpu.VMEM((sides, WIDE, breadth, channels), BF16),
            pltpu.VMEM((sides, MARGIN, breadth, channels), BF16),
            pltpu.VMEM((breadth, height), jnp.int32),
            pltpu.SemaphoreType.DMA((1 + 2 * sides,)),
        ],
        compiler_params=pltpu.CompilerParams(vmem_limit_bytes=PACK_LIMIT),
    )(lat.reshape(1), state, cotangent, land)
    pieces = links.lat_neighbours(packed[0], packed[-1])
    far, near = WIDE * breadth, MARGIN * breadth
    piece_states = pieces[:, :far].reshape(sides, WIDE, breadth, channels)
    piece_cotangents = pieces[:, far : far + near].reshape(sides, MARGIN, breadth, channels)
    piece_marks = pieces[:, far + near : far + near + breadth]

    def lon_columns(wide, narrow, margin):
        own = jnp.concatenate([state[:, wide], cotangent[:, margin]], axis=1)

        def ends(side, above):
            empty = ((NARROW, 0) if above else (0, NARROW), (0, 0), (0, 0))
            near_rows = jnp.pad(piece_cotangents[side][:, margin], empty)
            return jnp.concatenate([piece_states[side][:, wide], near_rows], axis=1)

        if sides == 1:
            rows = jnp.where(
                lat == 0,
                jnp.concatenate([own, ends(0, False)]),
                jnp.concatenate([ends(0, True), own]),
            )
        else:
            rows = jnp.concatenate([ends(0, True), own, ends(1, False)])
        kept = [whole_rows(marks[narrow], 8)]
        kept += [jnp.pad(piece_marks[side][narrow], ((0, 8 - NARROW), (0, 0))) for side in range(sides)]
        return jnp.concatenate([flat(rows), *kept])

    first_columns = lon_columns(slice(0, WIDE), slice(0, NARROW), slice(0, MARGIN))
    last_columns = lon_columns(
        slice(breadth - WIDE, breadth),
        slice(breadth - NARROW, breadth),
        slice(breadth - MARGIN, breadth),
    )
    within, across = links.lon_neighbours(
        jnp.where(core == 0, last_columns, first_columns),
        jnp.where(core == 0, first_columns, last_columns),
    )
    if sides == 1:
        places = [(1 - lat) * height]
        closest = [jnp.where(lat == 0, height, WIDE - MARGIN)]
    else:
        places = [0, WIDE + height]
        closest = [WIDE - MARGIN, WIDE + height]
    starts = [start(0), start(MARGIN), start(NARROW), core, *places, *closest]
    starts = jnp.stack([jnp.asarray(entry, jnp.int32) for entry in starts])
    state_pitch, field_pitch, inner_pitch = (
        round_up(breadth + size, 8) for size in (STATE_AT + WIDE, FIELD_AT + NARROW, NARROW)
    )

    padded_rows = window_rows + 2 * MARGIN + 1
    all_cells = second_rows * inner_pitch
    layer_rows = round_up(2 * hidden_units + TAPS + 5 + groups, 4 * 16)
    small_rows = BLOCKS * (layer_rows - 2 * hidden_units)
    grad_rows = BLOCKS * layer_rows
    own_rows = (window_rows, breadth)
    edge_rows = round_up(height * MARGIN, 8)
    scratch = [
        pltpu.VMEM((padded_rows, state_pitch, channels), F32),
        pltpu.VMEM((padded_rows, field_pitch, channels), F32),
        pltpu.VMEM((BLOCKS, TAPS, channels), F32),
        pltpu.VMEM((padded_rows, field_pitch, channels), F32),
        pltpu.VMEM((padded_rows, inner_pitch, channels), F32),
        pltpu.VMEM((window_rows, inner_pitch, channels), F32),
        pltpu.VMEM(own_rows + (channels,), F32),
        pltpu.VMEM(own_rows + (channels,), F32),
        pltpu.VMEM(own_rows + (channels,), F32),
        pltpu.VMEM(own_rows + (hidden_units,), F32),
        pltpu.VMEM(own_rows + (hidden_units,), BF16),
        pltpu.VMEM((height, breadth, hidden_units), BF16),
        pltpu.VMEM(own_rows + (channels,), BF16),
        pltpu.VMEM(tile, BF16),
        pltpu.VMEM(tile, F32),
        pltpu.VMEM((all_cells, hidden_units), BF16),
        pltpu.VMEM((all_cells, hidden_units), BF16),
        pltpu.VMEM((all_cells, channels), BF16),
        pltpu.VMEM((all_cells, channels), BF16),
        pltpu.VMEM((BLOCKS, 5, 8, channels), F32),
        pltpu.VMEM((BLOCKS, 8, hidden_units), F32),
        pltpu.VMEM((small_rows, channels), F32),
        pltpu.VMEM(within.shape, F32),
        pltpu.VMEM((2, edge_rows, channels), F32),
    ]
    sizes = (height, breadth, first_rows, second_rows, window_rows)
    taps_in = dw_kernel.reshape(BLOCKS, TAPS, channels)
    output, grad_mixed, masked, mixed_edges, grads = pl.pallas_call(
        functools.partial(tile_kernel, sizes),
        out_shape=(
            jax.ShapeDtypeStruct(tile, BF16),
            jax.ShapeDtypeStruct(tile, BF16),
            jax.ShapeDtypeStruct(tile, BF16),
            jax.ShapeDtypeStruct((2, edge_rows, channels), BF16),
            jax.ShapeDtypeStruct((grad_rows, channels), BF16),
        ),
        in_specs=[smem] + [vmem] * 15,
        out_specs=(vmem,) * 5,
        scratch_shapes=scratch,
        compiler_params=pltpu.CompilerParams(vmem_limit_bytes=VMEM_LIMIT),
        cost_estimate=pl.CostEstimate(
            flops=20 * all_cells * channels * hidden_units,
            bytes_accessed=4 * height * breadth * channels * 4,
            transcendentals=0,
        ),
    )(starts, state, cotangent, land, pieces, within, across, taps_in, *params[1:])

    def finish(mixed_edges):
        within, across = links.lon_neighbours(mixed_edges[0], mixed_edges[1])
        corner = MARGIN * MARGIN

        def corner_rows(rows, first):
            beside = slice(first * MARGIN, first * MARGIN + corner)
            parts = jnp.concatenate([flat(grad_mixed[rows]), within[beside], across[beside]])
            return jnp.pad(parts, ((0, -parts.shape[0] % 16), (0, 0)))

        last = corner_rows(slice(height - MARGIN, height), height - MARGIN)
        first = corner_rows(slice(0, MARGIN), 0)
        if sides == 1:
            last = first = jnp.where(lat == 0, last, first)
        pieces = links.lat_neighbours(last, first)
        if sides == 1:
            places = [(1 - lat) * (MARGIN + height)]
        else:
            places = [0, MARGIN + height]
        starts = jnp.stack([jnp.asarray(entry, jnp.int32) for entry in (core, *places)])
        wide = (height + 2 * MARGIN + 1, round_up(breadth + 2 * MARGIN, 8), channels)
        return pl.pallas_call(
            state_kernel,
            out_shape=jax.ShapeDtypeStruct(tile, BF16),
            in_specs=[smem] + [vmem] * 6,
            out_specs=vmem,
            scratch_shapes=[
                pltpu.VMEM(wide, F32),
                pltpu.VMEM((TAPS, channels), F32),
                pltpu.VMEM((edge_rows, channels), F32),
            ],
            compiler_params=pltpu.CompilerParams(vmem_limit_bytes=16 * 1024 * 1024),
            cost_estimate=pl.CostEstimate(
                flops=4_000_000_000, bytes_accessed=8_000_000, transcendentals=0
            ),
        )(starts, grad_mixed, within, across, pieces, masked, taps_in[0])

    held, own, other, grad_state = links.sum_all(grads, mixed_edges, finish)
    shapes = [(KSIZE, KSIZE, BLOCKS, channels)] + [member.shape for member in params[1:]]
    grad_kernel, *gradients = pl.pallas_call(
        functools.partial(gradient_kernel, grad_norm),
        out_shape=tuple(jax.ShapeDtypeStruct(shape, F32) for shape in shapes),
        in_specs=[smem, vmem, vmem],
        out_specs=(vmem,) * 9,
        compiler_params=pltpu.CompilerParams(vmem_limit_bytes=8 * 1024 * 1024),
    )(held.reshape(1), own, other)
    return (output, grad_state, grad_kernel.transpose(2, 0, 1, 3), *gradients)


def solution(mesh):
    tile = P("lat", "lon", None)
    placed = (tile, P("lat", "lon"), tile) + (P(),) * 9
    return jax.shard_map(
        functools.partial(on_device, Links(mesh)),
        mesh=mesh,
        in_specs=placed,
        out_specs=(tile, tile) + (P(),) * 9,
        check_vma=False,
    )
```

```python
import functools
import math

import jax
import jax.numpy as jnp
from jax import lax
from jax.experimental import pallas as pl
from jax.experimental.pallas import tpu as pltpu
from jax.sharding import PartitionSpec as P

KSIZE = 7
MARGIN = KSIZE // 2
TAPS = KSIZE * KSIZE
BLOCKS = 2
EPS_NORM = 1e-06
INV_ROOT_TWO = 0.7071067811865476
INV_ROOT_TWO_PI = 0.3989422804014327
LAND = 1024.0
LAND_BOUND = 512.0
VMEM_LIMIT = 48 * 1024 * 1024
PACK_LIMIT = 62 * 1024 * 1024
F32 = jnp.float32
BF16 = jnp.bfloat16
FIRST_STEP = 57
SECOND_STEP = 17
BACK_STEP = 45
TAP_STEP = 9
STATE_AT = 11
FIELD_AT = 8
INNER_AT = 3
WIDE = 3 * MARGIN
NARROW = 2 * MARGIN


def divisor(size, most):
    return max(step for step in range(1, most + 1) if size % step == 0)


def round_up(size, unit):
    return (size + unit - 1) // unit * unit


def pack_rows(above, below):
    shape = (above.shape[0] // 8, 8, above.shape[1])
    return jnp.concatenate([above.reshape(shape), below.reshape(shape)], axis=1).astype(BF16)


def conv_rows(source, base, first, count, width, kernel_ref, flip):
    pairs = (count + 1) // 2
    sums = [[None, None] for _ in range(pairs)]
    channels = source.shape[2]
    for tap_col in range(KSIZE):
        parts = [None] * pairs
        taps = []
        for tap_row in range(KSIZE):
            index = tap_row * KSIZE + tap_col
            tap = kernel_ref[pl.ds(TAPS - 1 - index if flip else index, 1), :]
            taps.append(jnp.broadcast_to(tap, (16, channels)).astype(BF16)[None])
        above = source[base, pl.ds(first + tap_col, width), :]
        for row in range(2 * pairs + KSIZE - 2):
            below = source[base + row + 1, pl.ds(first + tap_col, width), :]
            both = pack_rows(above, below)
            above = below
            for tap_row in range(row % 2, KSIZE, 2):
                out = (row - tap_row) // 2
                if 0 <= out < pairs:
                    term = both * taps[tap_row]
                    parts[out] = term if parts[out] is None else parts[out] + term
        for out in range(pairs):
            for side in range(2):
                value = parts[out].astype(F32)[:, 8 * side : 8 * side + 8]
                old = sums[out][side]
                sums[out][side] = value if old is None else old + value
    rows = [sums[row // 2][row % 2].reshape(width, channels) for row in range(count)]
    return jnp.concatenate(rows, axis=0)


def normal_parts(hidden):
    cumulative = 0.5 + 0.5 * lax.erf(hidden * INV_ROOT_TWO)
    return cumulative, jnp.exp(-0.5 * hidden * hidden)


def fold(values):
    return jnp.sum(values.reshape(values.shape[0] // 8, 8, values.shape[1]), axis=0)


def normalise(mixed):
    center = mixed - jnp.mean(mixed, axis=-1, keepdims=True)
    inverse = lax.rsqrt(jnp.mean(center * center, axis=-1, keepdims=True) + EPS_NORM)
    return center * inverse, inverse


def normalise_back(grad, normed, inverse):
    return inverse * (
        grad
        - jnp.mean(grad, axis=-1, keepdims=True)
        - normed * jnp.mean(grad * normed, axis=-1, keepdims=True)
    )


def rows_of(ref, base, first, count, width):
    return jnp.concatenate(
        [ref[base + row, pl.ds(first, width), :] for row in range(count)], axis=0
    )


CONTRACT_COLS = (((1,), (1,)), ((), ()))
CONTRACT_ROWS = (((0,), (0,)), ((), ()))


def dot(left, right):
    return jnp.dot(left, right, preferred_element_type=F32)


def dot_cols(left, right):
    return lax.dot_general(left, right, CONTRACT_COLS, preferred_element_type=F32)


def dot_rows(left, right):
    return lax.dot_general(left, right, CONTRACT_ROWS, preferred_element_type=F32)


def tap_sums(grad_ref, grad_row, grad_col, field_ref, field_row, field_col, height, width, out):
    rows = divisor(height, TAP_STEP)
    pairs = (rows + 1) // 2
    for cols in ((0, 1, 2, 3), (4, 5, 6)):

        def advance(step, sums):
            sums = list(sums)
            at = step * rows
            grads = [grad_ref[grad_row + at + row, pl.ds(grad_col, width), :] for row in range(rows)]
            grads += [jnp.zeros_like(grads[0])] * (2 * pairs - rows)
            grads = [pack_rows(grads[2 * pair], grads[2 * pair + 1]) for pair in range(pairs)]
            for place, tap_col in enumerate(cols):
                spots = pl.ds(field_col + tap_col, width)
                parts = [None] * KSIZE
                above = field_ref[field_row + at, spots, :]
                for row in range(2 * pairs + KSIZE - 2):
                    below = field_ref[field_row + at + row + 1, spots, :]
                    both = pack_rows(above, below)
                    above = below
                    for tap_row in range(row % 2, KSIZE, 2):
                        pair = (row - tap_row) // 2
                        if 0 <= pair < pairs:
                            term = grads[pair] * both
                            old = parts[tap_row]
                            parts[tap_row] = term if old is None else old + term
                for tap_row in range(KSIZE):
                    part = parts[tap_row]
                    total = part[0]
                    for group in range(1, part.shape[0]):
                        total = total + part[group]
                    index = place * KSIZE + tap_row
                    sums[index] = sums[index] + fold(total.astype(F32))
            return tuple(sums)

        zeros = tuple(jnp.zeros((8, grad_ref.shape[2]), F32) for _ in range(KSIZE * len(cols)))
        sums = lax.fori_loop(0, height // rows, advance, zeros)
        for place, tap_col in enumerate(cols):
            for tap_row in range(KSIZE):
                total = jnp.sum(sums[place * KSIZE + tap_row], axis=0, keepdims=True)
                out[pl.ds(tap_row * KSIZE + tap_col, 1), :] = total


def pack_kernel(lat, state, cotangent, land_sea, out, rows, far_rows, near_rows, land, arrived):
    height, breadth = state.shape[:2]
    sides = out.shape[0]
    copies = [pltpu.make_async_copy(land_sea, land, arrived.at[0])]
    for side in range(sides):
        last = lat[0] == 0 if sides == 1 else side == 0
        first = jnp.where(last, height - WIDE, 0)
        closest = jnp.where(last, height - MARGIN, 0)
        source = state.at[pl.ds(first, WIDE)]
        copies.append(pltpu.make_async_copy(source, far_rows.at[side], arrived.at[1 + side]))
        source = cotangent.at[pl.ds(closest, MARGIN)]
        copies.append(
            pltpu.make_async_copy(source, near_rows.at[side], arrived.at[1 + sides + side])
        )
    for copy in copies:
        copy.start()
    rows[...] = jnp.zeros_like(rows)
    for copy in copies:
        copy.wait()
    ocean = jnp.where(land[...] != 0, 1.0, 0.0).astype(F32)
    far, near = WIDE * breadth, MARGIN * breadth
    for side in range(sides):
        last = lat[0] == 0 if sides == 1 else side == 0
        for row in range(WIDE):
            rows[side, pl.ds(row * breadth, breadth), :] = far_rows[side, row].astype(F32)
        for row in range(MARGIN):
            spots = pl.ds(far + row * breadth, breadth)
            rows[side, spots, :] = near_rows[side, row].astype(F32)
        marks = jnp.where(last, ocean[:, height - WIDE :], ocean[:, :WIDE])
        rows[side, pl.ds(far + near, breadth), pl.ds(0, WIDE)] = marks
    out[...] = rows[...].astype(BF16)


def fill_windows(sizes, starts, sources, state, coded, edges):
    height, breadth, window_rows = sizes
    state_tile, cotangent, land_sea, lat_pieces, within, across = sources
    channels = state.shape[2]
    pad = MARGIN
    own = pad + starts[0]
    lower = starts[3] == 0
    state[pl.ds(pad, window_rows)] = jnp.zeros((window_rows,) + state.shape[1:], F32)
    coded[pl.ds(pad, window_rows)] = jnp.zeros((window_rows,) + coded.shape[1:], F32)

    def spread(marks, column):
        return jnp.broadcast_to(marks[:, column : column + 1], (marks.shape[0], channels))

    state[pl.ds(own, height), pl.ds(STATE_AT, breadth), :] = state_tile[...].astype(F32)
    ocean = jnp.where(land_sea[...] != 0, 1.0, 0.0).astype(F32)
    for row in range(height):
        value = jnp.where(spread(ocean, row) > 0.5, cotangent[row].astype(F32), LAND)
        coded[own + row, pl.ds(FIELD_AT, breadth), :] = value

    sides = lat_pieces.shape[0]
    far, near = WIDE * breadth, MARGIN * breadth
    for side in range(sides):
        first = pad + starts[4 + side]
        closest = pad + starts[4 + sides + side]
        piece = lat_pieces[side].astype(F32)
        marks = piece[far + near : far + near + breadth]
        for row in range(WIDE):
            spots = pl.ds(row * breadth, breadth)
            state[first + row, pl.ds(STATE_AT, breadth), :] = lat_pieces[side, spots].astype(F32)
            value = jnp.where(spread(marks, row) > 0.5, 0.0, LAND)
            coded[first + row, pl.ds(FIELD_AT, breadth), :] = value
        for row in range(MARGIN):
            value = piece[far + row * breadth : far + (row + 1) * breadth]
            old = coded[closest + row, pl.ds(FIELD_AT, breadth), :]
            value = jnp.where(old > LAND_BOUND, LAND, value)
            coded[closest + row, pl.ds(FIELD_AT, breadth), :] = value

    group = WIDE + MARGIN

    def fill_columns(source, west):
        edges[...] = source[...].astype(F32)
        state_at = STATE_AT - WIDE if west else STATE_AT + breadth
        mark_at = FIELD_AT - NARROW if west else FIELD_AT + breadth
        value_at = FIELD_AT - MARGIN if west else FIELD_AT + breadth
        shown = slice(NARROW - MARGIN, NARROW) if west else slice(0, MARGIN)
        spans = [(own - pad, height, 0)] + [(starts[4 + side], WIDE, side + 1) for side in range(sides)]
        for first, count, place in spans:
            marks = edges[pl.ds(window_rows * group + place * 8, 8), :]
            for row in range(count):
                at = pad + first + row
                lines = (first + row) * group
                state[at, pl.ds(state_at, WIDE), :] = edges[pl.ds(lines, WIDE), :]
                mark = spread(marks, row)[:NARROW]
                coded[at, pl.ds(mark_at, NARROW), :] = jnp.where(mark > 0.5, 0.0, LAND)
                value = jnp.where(mark[shown] > 0.5, edges[pl.ds(lines + WIDE, MARGIN), :], LAND)
                coded[at, pl.ds(value_at, MARGIN), :] = value

    @pl.when(lower)
    def _():
        fill_columns(across, True)
        fill_columns(within, False)

    @pl.when(jnp.logical_not(lower))
    def _():
        fill_columns(within, True)
        fill_columns(across, False)


def tile_kernel(
    sizes,
    starts,
    state_tile,
    cotangent,
    land_sea,
    lat_pieces,
    within,
    across,
    dw_in,
    conv_bias,
    norm_gain,
    norm_bias,
    weight_in,
    bias_in,
    weight_out,
    bias_out,
    layer_scale,
    output,
    mixed_out,
    masked_out,
    edges_out,
    grads_out,
    state,
    coded,
    kernels,
    field,
    inner,
    result,
    normed_own,
    inverse_own,
    branch_own,
    slope_own,
    active_own,
    hidden_own,
    lifted_own,
    branch_grad_own,
    mixed_own,
    active_all,
    hidden_all,
    lifted_all,
    branch_grad_all,
    sums,
    hidden_sums,
    taps,
    edges,
    mixed_edges,
):
    height, breadth, first_rows, second_rows, window_rows = sizes
    channels = state.shape[2]
    own_start = starts[0]
    second_start = starts[1]
    first_start = starts[2]
    first_width = field.shape[1]
    second_width = inner.shape[1]
    pad = MARGIN

    for ref in (state, coded, field, inner):
        ref[pl.ds(0, pad)] = jnp.zeros((pad,) + ref.shape[1:], F32)
        below = ref.shape[0] - pad - window_rows
        ref[pl.ds(pad + window_rows, below)] = jnp.zeros((below,) + ref.shape[1:], F32)
    state[pl.ds(pad, window_rows)] = jnp.zeros((window_rows,) + state.shape[1:], F32)
    coded[pl.ds(pad, window_rows)] = jnp.zeros((window_rows,) + coded.shape[1:], F32)

    fill_windows(
        (height, breadth, window_rows),
        starts,
        (state_tile, cotangent, land_sea, lat_pieces, within, across),
        state,
        coded,
        edges,
    )
    kernels[...] = dw_in[...].astype(F32)
    sums[...] = jnp.zeros_like(sums)
    hidden_sums[...] = jnp.zeros_like(hidden_sums)

    def param(ref, layer):
        return ref[pl.ds(layer, 1), :]

    first_step = divisor(first_rows, FIRST_STEP)

    def forward_first(step, carry):
        row = first_start + step * first_step
        cells = first_step * first_width
        mixed = conv_rows(state, row, 0, first_step, first_width, kernels.at[0], False)
        normed, inverse = normalise(mixed + param(conv_bias, 0))
        lifted = (normed * param(norm_gain, 0) + param(norm_bias, 0)).astype(BF16)
        hidden = dot(lifted, weight_in[0]) + param(bias_in, 0)
        cumulative, bell = normal_parts(hidden)
        active = hidden * cumulative
        branch = dot(active.astype(BF16), weight_out[0]) + param(bias_out, 0)
        center = rows_of(state, row + pad, MARGIN, first_step, first_width)
        mark = rows_of(coded, row + pad, 0, first_step, first_width)
        value = jnp.where(mark < LAND_BOUND, center + param(layer_scale, 0) * branch, 0.0)
        value = value.reshape(first_step, first_width, channels)

        for index in range(first_step):
            field[row + pad + index] = value[index]

        def own(values):
            shape = (first_step, first_width, values.shape[1])
            return values.reshape(shape)[:, FIELD_AT : FIELD_AT + breadth]

        slope = own(cumulative) + own(hidden) * (own(bell) * INV_ROOT_TWO_PI)
        spots = pl.ds(row, first_step)
        slope_own[spots] = slope
        active_own[spots] = own(active).astype(BF16)
        normed_own[spots] = own(normed)
        inverse_own[spots] = own(jnp.broadcast_to(inverse, normed.shape))
        branch_own[spots] = own(branch)
        lifted_own[spots] = own(normed * param(norm_gain, 0) + param(norm_bias, 0)).astype(BF16)
        return carry

    lax.fori_loop(0, first_rows // first_step, forward_first, 0)

    second_step = divisor(second_rows, SECOND_STEP)

    def both_second(step, carry):
        row = second_start + step * second_step
        cells = second_step * second_width
        shift = FIELD_AT - INNER_AT
        mixed = conv_rows(
            field, row, shift - MARGIN, second_step, second_width, kernels.at[1], False
        )
        normed, inverse = normalise(mixed + param(conv_bias, 1))
        lifted = normed * param(norm_gain, 1) + param(norm_bias, 1)
        hidden = dot(lifted.astype(BF16), weight_in[1]) + param(bias_in, 1)
        cumulative, bell = normal_parts(hidden)
        active = (hidden * cumulative).astype(BF16)
        branch = dot(active, weight_out[1]) + param(bias_out, 1)
        center = rows_of(field, row + pad, shift, second_step, second_width)
        mark = rows_of(coded, row + pad, shift, second_step, second_width)
        ocean = mark < LAND_BOUND
        value = jnp.where(ocean, center + param(layer_scale, 1) * branch, 0.0)
        value = value.reshape(second_step, second_width, channels)
        masked = jnp.where(ocean, mark, 0.0)
        grad_branch = (masked * param(layer_scale, 1)).astype(BF16)
        grad_active = dot_cols(grad_branch, weight_out[1])
        slope = cumulative + hidden * (bell * INV_ROOT_TWO_PI)
        grad_hidden = (grad_active * slope).astype(BF16)
        grad_lifted = dot_cols(grad_hidden, weight_in[1])
        grad_mixed = normalise_back(grad_lifted * param(norm_gain, 1), normed, inverse)
        grad_mixed = grad_mixed.reshape(second_step, second_width, channels)
        for index in range(second_step):
            result[row + index] = value[index]
            inner[row + pad + index] = grad_mixed[index]

        shape = (second_step, second_width, channels)
        row_of = lax.broadcasted_iota(jnp.int32, shape, 0) + (row - own_start)
        col_of = lax.broadcasted_iota(jnp.int32, shape, 1) - INNER_AT
        inside = (row_of >= 0) & (row_of < height) & (col_of >= 0) & (col_of < breadth)
        inside = jnp.where(inside, 1.0, 0.0).astype(F32).reshape(cells, channels)
        own_lifted = grad_lifted * inside
        own_branch = grad_branch.astype(F32) * inside
        sums[1, 0] += fold(masked * branch * inside)
        sums[1, 1] += fold(own_branch)
        sums[1, 2] += fold(own_lifted * normed)
        sums[1, 3] += fold(own_lifted)
        wide = jnp.concatenate([inside] * (hidden.shape[1] // channels), axis=1)
        hidden_sums[1] += fold(grad_hidden.astype(F32) * wide)
        spots = pl.ds(pl.multiple_of(step * cells, cells), cells)
        active_all[spots] = active
        hidden_all[spots] = grad_hidden
        lifted_all[spots] = (lifted * inside).astype(BF16)
        branch_grad_all[spots] = own_branch.astype(BF16)
        return carry

    lax.fori_loop(0, second_rows // second_step, both_second, 0)

    back_step = divisor(height, BACK_STEP)

    def backward_first(step, carry):
        row = own_start + step * back_step
        cells = back_step * breadth
        mark = rows_of(coded, row + pad, FIELD_AT, back_step, breadth)
        ocean = mark < LAND_BOUND
        masked_next = jnp.where(ocean, mark, 0.0)
        spread = conv_rows(inner, row, 0, back_step, breadth, kernels.at[1], True)
        masked = jnp.where(ocean, masked_next + spread, 0.0)
        grad_branch = (masked * param(layer_scale, 0)).astype(BF16)
        grad_active = dot_cols(grad_branch, weight_out[0])
        slope = slope_own[pl.ds(row, back_step)].reshape(cells, grad_active.shape[1])
        grad_hidden = (grad_active * slope).astype(BF16)
        grad_lifted = dot_cols(grad_hidden, weight_in[0])
        normed = normed_own[pl.ds(row, back_step)].reshape(cells, channels)
        inverse = inverse_own[pl.ds(row, back_step)].reshape(cells, channels)
        grad_mixed = normalise_back(grad_lifted * param(norm_gain, 0), normed, inverse)
        branch = branch_own[pl.ds(row, back_step)].reshape(cells, channels)
        sums[0, 0] += fold(masked * branch)
        sums[0, 1] += fold(grad_branch.astype(F32))
        sums[0, 2] += fold(grad_lifted * normed)
        sums[0, 3] += fold(grad_lifted)
        sums[0, 4] += fold(grad_mixed)
        hidden_sums[0] += fold(grad_hidden.astype(F32))
        inner_rows = rows_of(inner, row + pad, INNER_AT, back_step, breadth)
        sums[1, 4] += fold(inner_rows)
        tile = pl.ds(step * back_step, back_step)
        shape = (back_step, breadth, channels)
        grad_mixed = grad_mixed.reshape(shape)
        mixed_own[tile] = grad_mixed
        mixed_out[tile] = grad_mixed.astype(BF16)
        masked_out[tile] = masked.reshape(shape).astype(BF16)
        hidden_own[tile] = grad_hidden.reshape(back_step, breadth, grad_hidden.shape[1])
        branch_grad_own[tile] = grad_branch.reshape(shape)
        value = rows_of(result, row, INNER_AT, back_step, breadth)
        output[tile] = value.reshape(shape).astype(BF16)
        return carry

    lax.fori_loop(0, height // back_step, backward_first, 0)

    mixed_edges[...] = jnp.zeros_like(mixed_edges)
    lower = starts[3] == 0
    for row in range(height):
        first = mixed_own[row, pl.ds(0, MARGIN), :]
        last = mixed_own[row, pl.ds(breadth - MARGIN, MARGIN), :]
        spots = pl.ds(row * MARGIN, MARGIN)
        mixed_edges[0, spots] = jnp.where(lower, last, first)
        mixed_edges[1, spots] = jnp.where(lower, first, last)
    edges_out[...] = mixed_edges[...].astype(BF16)

    hidden_units = weight_in.shape[2]
    groups = hidden_units // channels
    tile = pl.ds(own_start, height)
    cells = height * breadth

    def flat(ref, spots):
        return ref[spots].reshape(cells, ref.shape[2])

    operands = (
        (
            flat(lifted_own, tile),
            flat(hidden_own, pl.ds(0, height)),
            flat(active_own, tile),
            flat(branch_grad_own, pl.ds(0, height)),
        ),
        (lifted_all[...], hidden_all[...], active_all[...], branch_grad_all[...]),
    )
    for layer, (lifted, grad_hidden, active, grad_branch) in enumerate(operands):
        at = layer * (grads_out.shape[0] // BLOCKS)
        grad_in = dot_rows(lifted, grad_hidden)
        for group in range(groups):
            grads_out[pl.ds(at + group * channels, channels), :] = grad_in[
                :, group * channels : (group + 1) * channels
            ].astype(BF16)
        grad_out = dot_rows(grad_branch, active)
        for group in range(groups):
            grads_out[pl.ds(at + hidden_units + group * channels, channels), :] = grad_out[
                :, group * channels : (group + 1) * channels
            ].T.astype(BF16)

    taps[...] = jnp.zeros_like(taps)
    for layer in range(BLOCKS):
        base = layer * (taps.shape[0] // BLOCKS)
        if layer:
            tap_sums(
                inner,
                own_start + pad,
                INNER_AT,
                field,
                own_start,
                FIELD_AT - MARGIN,
                height,
                breadth,
                taps.at[pl.ds(base, TAPS)],
            )
        else:
            tap_sums(
                mixed_own,
                0,
                0,
                state,
                own_start,
                STATE_AT - MARGIN,
                height,
                breadth,
                taps.at[pl.ds(base, TAPS)],
            )
        for member in range(5):
            taps[pl.ds(base + TAPS + member, 1), :] = jnp.sum(
                sums[layer, member], axis=0, keepdims=True
            )
        hidden_total = jnp.sum(hidden_sums[layer], axis=0, keepdims=True)
        for group in range(groups):
            taps[pl.ds(base + TAPS + 5 + group, 1), :] = hidden_total[
                :, group * channels : (group + 1) * channels
            ]
    small = taps.shape[0] // BLOCKS
    for layer in range(BLOCKS):
        at = layer * (grads_out.shape[0] // BLOCKS) + 2 * hidden_units
        grads_out[pl.ds(at, small), :] = taps[pl.ds(layer * small, small), :].astype(BF16)


def state_kernel(starts, mixed, within, across, lat_pieces, masked, dw_in, out, wide, kernels, edges):
    height, breadth, channels = masked.shape
    wide[...] = jnp.zeros_like(wide)
    kernels[...] = dw_in[...].astype(F32)
    wide[pl.ds(MARGIN, height), pl.ds(MARGIN, breadth), :] = mixed[...].astype(F32)
    sides = lat_pieces.shape[0]
    inner = MARGIN * breadth
    beside = MARGIN * MARGIN
    for side in range(sides):
        first = starts[1 + side]
        piece = lat_pieces[side].astype(F32)
        for row in range(MARGIN):
            spots = slice(row * breadth, (row + 1) * breadth)
            wide[first + row, pl.ds(MARGIN, breadth), :] = piece[spots]

    def fill_columns(source, place, west):
        column = 0 if west else MARGIN + breadth
        edges[...] = source[...].astype(F32)
        for row in range(height):
            wide[MARGIN + row, pl.ds(column, MARGIN), :] = edges[pl.ds(row * MARGIN, MARGIN), :]
        for side in range(sides):
            piece = lat_pieces[side].astype(F32)
            for row in range(MARGIN):
                at = inner + place * beside + row * MARGIN
                wide[starts[1 + side] + row, pl.ds(column, MARGIN), :] = piece[at : at + MARGIN]

    @pl.when(starts[0] == 0)
    def _():
        fill_columns(within, 0, False)
        fill_columns(across, 1, True)

    @pl.when(starts[0] != 0)
    def _():
        fill_columns(within, 0, True)
        fill_columns(across, 1, False)

    rows = divisor(height, BACK_STEP)

    def advance(step, carry):
        row = step * rows
        spread = conv_rows(wide, row, 0, rows, breadth, kernels, True)
        tile = pl.ds(row, rows)
        shape = (rows, breadth, channels)
        out[tile] = (masked[tile].astype(F32) + spread.reshape(shape)).astype(BF16)
        return carry

    lax.fori_loop(0, height // rows, advance, 0)


def gradient_kernel(grad_norm, held, own, other, *outs):
    kernel, conv_bias, gain, shift, first, first_bias, second, second_bias, scale = outs
    channels = own.shape[1]
    units = second.shape[1]
    groups = units // channels

    def unpack(rows, layer):
        for group in range(groups):
            spots = pl.ds(group * channels, channels)
            first[layer, :, spots] = rows[spots].astype(F32) * grad_norm
        second[layer] = rows[pl.ds(units, units)].astype(F32) * grad_norm
        small = rows[pl.ds(2 * units, rows.shape[0] - 2 * units)].astype(F32) * grad_norm
        for index in range(TAPS):
            kernel[index // KSIZE, index % KSIZE, layer : layer + 1] = small[index : index + 1]
        for member, out in enumerate((scale, second_bias, gain, shift, conv_bias)):
            out[layer : layer + 1] = small[TAPS + member : TAPS + member + 1]
        for group in range(groups):
            row = TAPS + 5 + group
            first_bias[layer : layer + 1, pl.ds(group * channels, channels)] = small[row : row + 1]

    @pl.when(held[0] == 0)
    def _():
        unpack(own, 0)
        unpack(other, 1)

    @pl.when(held[0] != 0)
    def _():
        unpack(own, 1)
        unpack(other, 0)


class Links:
    def __init__(self, mesh):
        self.lon = mesh.shape["lon"]
        self.lat = mesh.shape["lat"]
        self.axes = ("lon", "lat")

    def lon_neighbours(self, within, across):
        there = [place + 1 if place % 2 else place - 1 for place in range(self.lon)]
        pairs = [(place, other % self.lon) for place, other in enumerate(there)]
        across = lax.ppermute(across, "lon", pairs)
        return self.swap(within, 1, 0), across

    def shift_lat(self, values, by):
        pairs = [
            (place, place + by) for place in range(self.lat) if 0 <= place + by < self.lat
        ]
        return lax.ppermute(values, "lat", pairs)

    def lat_neighbours(self, last, first):
        if self.lat == 2:
            return self.swap(last, 0, 1)[None]
        return jnp.stack([self.shift_lat(last, 1), self.shift_lat(first, -1)])

    def swap(self, values, lon_bits, lat_bits):
        pairs = []
        for lon in range(self.lon):
            for lat in range(self.lat):
                there = (lon ^ lon_bits) * self.lat + (lat ^ lat_bits)
                pairs.append((lon * self.lat + lat, there))
        return lax.ppermute(values, self.axes, pairs)

    def sum_all(self, rows, edges, finish):
        lon = lax.axis_index("lon")
        lat = lax.axis_index("lat")
        bits = [(1 << bit, 0) for bit in range(self.lon.bit_length() - 1)]
        bits = bits[:1] + [(0, 1 << bit) for bit in range(self.lat.bit_length() - 1)] + bits[1:]

        def code(group):
            total = jnp.int32(0)
            for index, (lon_bit, lat_bit) in enumerate(group):
                held = (lon // lon_bit) % 2 if lon_bit else (lat // lat_bit) % 2
                total = total + held * (1 << index)
            return total

        def merged(group, choice):
            lon_bits = sum(bit[0] for index, bit in enumerate(group) if choice >> index & 1)
            lat_bits = sum(bit[1] for index, bit in enumerate(group) if choice >> index & 1)
            return lon_bits, lat_bits

        def scatter(values, group):
            count = 1 << len(group)
            pieces = values.reshape(count, -1, values.shape[1])
            here = code(group)
            total = lax.dynamic_index_in_dim(pieces, here, 0, False).astype(F32)
            arrived = []
            for choice in range(1, count):
                sent = lax.dynamic_index_in_dim(pieces, here ^ choice, 0, False)
                arrived.append(self.swap(sent, *merged(group, choice)))
            return total, arrived

        def summed(total, arrived):
            for values in arrived:
                total = total + values.astype(F32)
            return total.astype(BF16)

        def exchange(values, group):
            total = values.astype(F32)
            for choice in range(1, 1 << len(group)):
                total = total + self.swap(values, *merged(group, choice)).astype(F32)
            return total.astype(BF16)

        def gather(values, group):
            count = 1 << len(group)
            pieces = [values]
            for choice in range(1, count):
                pieces.append(self.swap(values, *merged(group, choice)))
            stack = jnp.stack(pieces)
            here = code(group)
            ordered = [
                lax.dynamic_index_in_dim(stack, here ^ place, 0, False) for place in range(count)
            ]
            return jnp.concatenate(ordered, axis=0)

        pair, quad, rest = bits[:1], bits[1:3], bits[3:]
        values = summed(*scatter(rows, pair))
        total, arrived = scatter(values, quad)
        arrived[0], edges = lax.optimization_barrier((arrived[0], edges))
        beside = finish(edges)
        values = summed(total, arrived)
        while rest:
            values = exchange(values, rest[:2])
            rest = rest[2:]
        values = gather(values, quad)
        values, beside = lax.optimization_barrier((values, beside))
        return code(pair), values, self.swap(values, *pair[0]), beside


def on_device(links, state, land_sea, cotangent, *params):
    dw_kernel, weight_in = params[0], params[4]
    height, breadth, channels = state.shape
    hidden_units = weight_in.shape[2]
    groups = hidden_units // channels
    grad_norm = 1.0 / math.sqrt(links.lat * height * links.lon * breadth)
    lat = lax.axis_index("lat")
    sides = 1 if links.lat == 2 else 2
    window_rows = height + sides * WIDE
    first_rows = height + sides * NARROW
    second_rows = height + sides * MARGIN

    def start(margin):
        skipped = WIDE - margin
        return lat * skipped if sides == 1 else jnp.int32(skipped)

    core = lax.axis_index("lon") % 2
    vmem = pl.BlockSpec(memory_space=pltpu.VMEM)
    smem = pl.BlockSpec(memory_space=pltpu.SMEM)
    tile = (height, breadth, channels)

    def flat(values):
        return values.reshape(-1, channels)

    def whole_rows(values, rows):
        return jnp.pad(values, ((0, rows - values.shape[0]), (0, channels - values.shape[1])))

    land = land_sea.T
    marks = (land != 0).astype(BF16)

    packed_rows = round_up((WIDE + MARGIN + 1) * breadth, 16)
    packed = (sides, packed_rows, channels)
    packed = pl.pallas_call(
        pack_kernel,
        out_shape=jax.ShapeDtypeStruct(packed, BF16),
        in_specs=[smem] + [pl.BlockSpec(memory_space=pl.ANY)] * 3,
        out_specs=vmem,
        scratch_shapes=[
            pltpu.VMEM(packed, F32),
            pltpu.VMEM((sides, WIDE, breadth, channels), BF16),
            pltpu.VMEM((sides, MARGIN, breadth, channels), BF16),
            pltpu.VMEM((breadth, height), jnp.int32),
            pltpu.SemaphoreType.DMA((1 + 2 * sides,)),
        ],
        compiler_params=pltpu.CompilerParams(vmem_limit_bytes=PACK_LIMIT),
    )(lat.reshape(1), state, cotangent, land)
    pieces = links.lat_neighbours(packed[0], packed[-1])
    far, near = WIDE * breadth, MARGIN * breadth
    piece_states = pieces[:, :far].reshape(sides, WIDE, breadth, channels)
    piece_cotangents = pieces[:, far : far + near].reshape(sides, MARGIN, breadth, channels)
    piece_marks = pieces[:, far + near : far + near + breadth]

    def lon_columns(wide, narrow, margin):
        own = jnp.concatenate([state[:, wide], cotangent[:, margin]], axis=1)

        def ends(side, above):
            empty = ((NARROW, 0) if above else (0, NARROW), (0, 0), (0, 0))
            near_rows = jnp.pad(piece_cotangents[side][:, margin], empty)
            return jnp.concatenate([piece_states[side][:, wide], near_rows], axis=1)

        if sides == 1:
            rows = jnp.where(
                lat == 0,
                jnp.concatenate([own, ends(0, False)]),
                jnp.concatenate([ends(0, True), own]),
            )
        else:
            rows = jnp.concatenate([ends(0, True), own, ends(1, False)])
        kept = [whole_rows(marks[narrow], 8)]
        kept += [jnp.pad(piece_marks[side][narrow], ((0, 8 - NARROW), (0, 0))) for side in range(sides)]
        return jnp.concatenate([flat(rows), *kept])

    first_columns = lon_columns(slice(0, WIDE), slice(0, NARROW), slice(0, MARGIN))
    last_columns = lon_columns(
        slice(breadth - WIDE, breadth),
        slice(breadth - NARROW, breadth),
        slice(breadth - MARGIN, breadth),
    )
    within, across = links.lon_neighbours(
        jnp.where(core == 0, last_columns, first_columns),
        jnp.where(core == 0, first_columns, last_columns),
    )
    if sides == 1:
        places = [(1 - lat) * height]
        closest = [jnp.where(lat == 0, height, WIDE - MARGIN)]
    else:
        places = [0, WIDE + height]
        closest = [WIDE - MARGIN, WIDE + height]
    starts = [start(0), start(MARGIN), start(NARROW), core, *places, *closest]
    starts = jnp.stack([jnp.asarray(entry, jnp.int32) for entry in starts])
    state_pitch, field_pitch, inner_pitch = (
        round_up(breadth + size, 8) for size in (STATE_AT + WIDE, FIELD_AT + NARROW, NARROW)
    )

    padded_rows = window_rows + 2 * MARGIN + 1
    all_cells = second_rows * inner_pitch
    layer_rows = round_up(2 * hidden_units + TAPS + 5 + groups, 4 * 16)
    small_rows = BLOCKS * (layer_rows - 2 * hidden_units)
    grad_rows = BLOCKS * layer_rows
    own_rows = (window_rows, breadth)
    edge_rows = round_up(height * MARGIN, 8)
    scratch = [
        pltpu.VMEM((padded_rows, state_pitch, channels), F32),
        pltpu.VMEM((padded_rows, field_pitch, channels), F32),
        pltpu.VMEM((BLOCKS, TAPS, channels), F32),
        pltpu.VMEM((padded_rows, field_pitch, channels), F32),
        pltpu.VMEM((padded_rows, inner_pitch, channels), F32),
        pltpu.VMEM((window_rows, inner_pitch, channels), F32),
        pltpu.VMEM(own_rows + (channels,), F32),
        pltpu.VMEM(own_rows + (channels,), F32),
        pltpu.VMEM(own_rows + (channels,), F32),
        pltpu.VMEM(own_rows + (hidden_units,), F32),
        pltpu.VMEM(own_rows + (hidden_units,), BF16),
        pltpu.VMEM((height, breadth, hidden_units), BF16),
        pltpu.VMEM(own_rows + (channels,), BF16),
        pltpu.VMEM(tile, BF16),
        pltpu.VMEM(tile, F32),
        pltpu.VMEM((all_cells, hidden_units), BF16),
        pltpu.VMEM((all_cells, hidden_units), BF16),
        pltpu.VMEM((all_cells, channels), BF16),
        pltpu.VMEM((all_cells, channels), BF16),
        pltpu.VMEM((BLOCKS, 5, 8, channels), F32),
        pltpu.VMEM((BLOCKS, 8, hidden_units), F32),
        pltpu.VMEM((small_rows, channels), F32),
        pltpu.VMEM(within.shape, F32),
        pltpu.VMEM((2, edge_rows, channels), F32),
    ]
    sizes = (height, breadth, first_rows, second_rows, window_rows)
    taps_in = dw_kernel.reshape(BLOCKS, TAPS, channels)
    output, grad_mixed, masked, mixed_edges, grads = pl.pallas_call(
        functools.partial(tile_kernel, sizes),
        out_shape=(
            jax.ShapeDtypeStruct(tile, BF16),
            jax.ShapeDtypeStruct(tile, BF16),
            jax.ShapeDtypeStruct(tile, BF16),
            jax.ShapeDtypeStruct((2, edge_rows, channels), BF16),
            jax.ShapeDtypeStruct((grad_rows, channels), BF16),
        ),
        in_specs=[smem] + [vmem] * 15,
        out_specs=(vmem,) * 5,
        scratch_shapes=scratch,
        compiler_params=pltpu.CompilerParams(vmem_limit_bytes=VMEM_LIMIT),
        cost_estimate=pl.CostEstimate(
            flops=20 * all_cells * channels * hidden_units,
            bytes_accessed=4 * height * breadth * channels * 4,
            transcendentals=0,
        ),
    )(starts, state, cotangent, land, pieces, within, across, taps_in, *params[1:])

    def finish(mixed_edges):
        within, across = links.lon_neighbours(mixed_edges[0], mixed_edges[1])
        corner = MARGIN * MARGIN

        def corner_rows(rows, first):
            beside = slice(first * MARGIN, first * MARGIN + corner)
            parts = jnp.concatenate([flat(grad_mixed[rows]), within[beside], across[beside]])
            return jnp.pad(parts, ((0, -parts.shape[0] % 16), (0, 0)))

        last = corner_rows(slice(height - MARGIN, height), height - MARGIN)
        first = corner_rows(slice(0, MARGIN), 0)
        if sides == 1:
            last = first = jnp.where(lat == 0, last, first)
        pieces = links.lat_neighbours(last, first)
        if sides == 1:
            places = [(1 - lat) * (MARGIN + height)]
        else:
            places = [0, MARGIN + height]
        starts = jnp.stack([jnp.asarray(entry, jnp.int32) for entry in (core, *places)])
        wide = (height + 2 * MARGIN + 1, round_up(breadth + 2 * MARGIN, 8), channels)
        return pl.pallas_call(
            state_kernel,
            out_shape=jax.ShapeDtypeStruct(tile, BF16),
            in_specs=[smem] + [vmem] * 6,
            out_specs=vmem,
            scratch_shapes=[
                pltpu.VMEM(wide, F32),
                pltpu.VMEM((TAPS, channels), F32),
                pltpu.VMEM((edge_rows, channels), F32),
            ],
            compiler_params=pltpu.CompilerParams(vmem_limit_bytes=16 * 1024 * 1024),
            cost_estimate=pl.CostEstimate(
                flops=4_000_000_000, bytes_accessed=8_000_000, transcendentals=0
            ),
        )(starts, grad_mixed, within, across, pieces, masked, taps_in[0])

    held, own, other, grad_state = links.sum_all(grads, mixed_edges, finish)
    shapes = [(KSIZE, KSIZE, BLOCKS, channels)] + [member.shape for member in params[1:]]
    grad_kernel, *gradients = pl.pallas_call(
        functools.partial(gradient_kernel, grad_norm),
        out_shape=tuple(jax.ShapeDtypeStruct(shape, F32) for shape in shapes),
        in_specs=[smem, vmem, vmem],
        out_specs=(vmem,) * 9,
        compiler_params=pltpu.CompilerParams(vmem_limit_bytes=8 * 1024 * 1024),
    )(held.reshape(1), own, other)
    return (output, grad_state, grad_kernel.transpose(2, 0, 1, 3), *gradients)


def solution(mesh):
    tile = P("lat", "lon", None)
    placed = (tile, P("lat", "lon"), tile) + (P(),) * 9
    return jax.shard_map(
        functools.partial(on_device, Links(mesh)),
        mesh=mesh,
        in_specs=placed,
        out_specs=(tile, tile) + (P(),) * 9,
        check_vma=False,
    )
```

```python
import functools
import math

import jax
import jax.numpy as jnp
from jax import lax
from jax.experimental import pallas as pl
from jax.experimental.pallas import tpu as pltpu
from jax.sharding import PartitionSpec as P

KSIZE = 7
MARGIN = KSIZE // 2
TAPS = KSIZE * KSIZE
BLOCKS = 2
EPS_NORM = 1e-06
INV_ROOT_TWO = 0.7071067811865476
INV_ROOT_TWO_PI = 0.3989422804014327
LAND = 1024.0
LAND_BOUND = 512.0
VMEM_LIMIT = 48 * 1024 * 1024
PACK_LIMIT = 62 * 1024 * 1024
F32 = jnp.float32
BF16 = jnp.bfloat16
FIRST_STEP = 57
SECOND_STEP = 17
BACK_STEP = 45
TAP_STEP = 15
STATE_AT = 11
FIELD_AT = 8
INNER_AT = 3
WIDE = 3 * MARGIN
NARROW = 2 * MARGIN


def divisor(size, most):
    return max(step for step in range(1, most + 1) if size % step == 0)


def round_up(size, unit):
    return (size + unit - 1) // unit * unit


def pack_rows(above, below):
    shape = (above.shape[0] // 8, 8, above.shape[1])
    return jnp.concatenate([above.reshape(shape), below.reshape(shape)], axis=1).astype(BF16)


def conv_rows(source, base, first, count, width, kernel_ref, flip):
    pairs = (count + 1) // 2
    sums = [[None, None] for _ in range(pairs)]
    channels = source.shape[2]
    for tap_col in range(KSIZE):
        parts = [None] * pairs
        taps = []
        for tap_row in range(KSIZE):
            index = tap_row * KSIZE + tap_col
            tap = kernel_ref[pl.ds(TAPS - 1 - index if flip else index, 1), :]
            taps.append(jnp.broadcast_to(tap, (16, channels)).astype(BF16)[None])
        above = source[base, pl.ds(first + tap_col, width), :]
        for row in range(2 * pairs + KSIZE - 2):
            below = source[base + row + 1, pl.ds(first + tap_col, width), :]
            both = pack_rows(above, below)
            above = below
            for tap_row in range(row % 2, KSIZE, 2):
                out = (row - tap_row) // 2
                if 0 <= out < pairs:
                    term = both * taps[tap_row]
                    parts[out] = term if parts[out] is None else parts[out] + term
        for out in range(pairs):
            for side in range(2):
                value = parts[out].astype(F32)[:, 8 * side : 8 * side + 8]
                old = sums[out][side]
                sums[out][side] = value if old is None else old + value
    rows = [sums[row // 2][row % 2].reshape(width, channels) for row in range(count)]
    return jnp.concatenate(rows, axis=0)


def normal_parts(hidden):
    cumulative = 0.5 + 0.5 * lax.erf(hidden * INV_ROOT_TWO)
    return cumulative, jnp.exp(-0.5 * hidden * hidden)


def fold(values):
    return jnp.sum(values.reshape(values.shape[0] // 8, 8, values.shape[1]), axis=0)


def normalise(mixed):
    center = mixed - jnp.mean(mixed, axis=-1, keepdims=True)
    inverse = lax.rsqrt(jnp.mean(center * center, axis=-1, keepdims=True) + EPS_NORM)
    return center * inverse, inverse


def normalise_back(grad, normed, inverse):
    return inverse * (
        grad
        - jnp.mean(grad, axis=-1, keepdims=True)
        - normed * jnp.mean(grad * normed, axis=-1, keepdims=True)
    )


def rows_of(ref, base, first, count, width):
    return jnp.concatenate(
        [ref[base + row, pl.ds(first, width), :] for row in range(count)], axis=0
    )


CONTRACT_COLS = (((1,), (1,)), ((), ()))
CONTRACT_ROWS = (((0,), (0,)), ((), ()))


def dot(left, right):
    return jnp.dot(left, right, preferred_element_type=F32)


def dot_cols(left, right):
    return lax.dot_general(left, right, CONTRACT_COLS, preferred_element_type=F32)


def dot_rows(left, right):
    return lax.dot_general(left, right, CONTRACT_ROWS, preferred_element_type=F32)


def tap_sums(grad_ref, grad_row, grad_col, field_ref, field_row, field_col, height, width, out):
    rows = divisor(height, TAP_STEP)
    pairs = (rows + 1) // 2
    for cols in ((0, 1, 2, 3), (4, 5, 6)):

        def advance(step, sums):
            sums = list(sums)
            at = step * rows
            grads = [grad_ref[grad_row + at + row, pl.ds(grad_col, width), :] for row in range(rows)]
            grads += [jnp.zeros_like(grads[0])] * (2 * pairs - rows)
            grads = [pack_rows(grads[2 * pair], grads[2 * pair + 1]) for pair in range(pairs)]
            for place, tap_col in enumerate(cols):
                spots = pl.ds(field_col + tap_col, width)
                parts = [None] * KSIZE
                above = field_ref[field_row + at, spots, :]
                for row in range(2 * pairs + KSIZE - 2):
                    below = field_ref[field_row + at + row + 1, spots, :]
                    both = pack_rows(above, below)
                    above = below
                    for tap_row in range(row % 2, KSIZE, 2):
                        pair = (row - tap_row) // 2
                        if 0 <= pair < pairs:
                            term = grads[pair] * both
                            old = parts[tap_row]
                            parts[tap_row] = term if old is None else old + term
                for tap_row in range(KSIZE):
                    part = parts[tap_row]
                    total = part[0]
                    for group in range(1, part.shape[0]):
                        total = total + part[group]
                    index = place * KSIZE + tap_row
                    sums[index] = sums[index] + fold(total.astype(F32))
            return tuple(sums)

        zeros = tuple(jnp.zeros((8, grad_ref.shape[2]), F32) for _ in range(KSIZE * len(cols)))
        sums = lax.fori_loop(0, height // rows, advance, zeros)
        for place, tap_col in enumerate(cols):
            for tap_row in range(KSIZE):
                total = jnp.sum(sums[place * KSIZE + tap_row], axis=0, keepdims=True)
                out[pl.ds(tap_row * KSIZE + tap_col, 1), :] = total


def pack_kernel(lat, state, cotangent, land_sea, out, rows, far_rows, near_rows, land, arrived):
    height, breadth = state.shape[:2]
    sides = out.shape[0]
    copies = [pltpu.make_async_copy(land_sea, land, arrived.at[0])]
    for side in range(sides):
        last = lat[0] == 0 if sides == 1 else side == 0
        first = jnp.where(last, height - WIDE, 0)
        closest = jnp.where(last, height - MARGIN, 0)
        source = state.at[pl.ds(first, WIDE)]
        copies.append(pltpu.make_async_copy(source, far_rows.at[side], arrived.at[1 + side]))
        source = cotangent.at[pl.ds(closest, MARGIN)]
        copies.append(
            pltpu.make_async_copy(source, near_rows.at[side], arrived.at[1 + sides + side])
        )
    for copy in copies:
        copy.start()
    rows[...] = jnp.zeros_like(rows)
    for copy in copies:
        copy.wait()
    ocean = jnp.where(land[...] != 0, 1.0, 0.0).astype(F32)
    far, near = WIDE * breadth, MARGIN * breadth
    for side in range(sides):
        last = lat[0] == 0 if sides == 1 else side == 0
        for row in range(WIDE):
            rows[side, pl.ds(row * breadth, breadth), :] = far_rows[side, row].astype(F32)
        for row in range(MARGIN):
            spots = pl.ds(far + row * breadth, breadth)
            rows[side, spots, :] = near_rows[side, row].astype(F32)
        marks = jnp.where(last, ocean[:, height - WIDE :], ocean[:, :WIDE])
        rows[side, pl.ds(far + near, breadth), pl.ds(0, WIDE)] = marks
    out[...] = rows[...].astype(BF16)


def fill_windows(sizes, starts, sources, state, coded, edges):
    height, breadth, window_rows = sizes
    state_tile, cotangent, land_sea, lat_pieces, within, across = sources
    channels = state.shape[2]
    pad = MARGIN
    own = pad + starts[0]
    lower = starts[3] == 0
    state[pl.ds(pad, window_rows)] = jnp.zeros((window_rows,) + state.shape[1:], F32)
    coded[pl.ds(pad, window_rows)] = jnp.zeros((window_rows,) + coded.shape[1:], F32)

    def spread(marks, column):
        return jnp.broadcast_to(marks[:, column : column + 1], (marks.shape[0], channels))

    state[pl.ds(own, height), pl.ds(STATE_AT, breadth), :] = state_tile[...].astype(F32)
    ocean = jnp.where(land_sea[...] != 0, 1.0, 0.0).astype(F32)
    for row in range(height):
        value = jnp.where(spread(ocean, row) > 0.5, cotangent[row].astype(F32), LAND)
        coded[own + row, pl.ds(FIELD_AT, breadth), :] = value

    sides = lat_pieces.shape[0]
    far, near = WIDE * breadth, MARGIN * breadth
    for side in range(sides):
        first = pad + starts[4 + side]
        closest = pad + starts[4 + sides + side]
        piece = lat_pieces[side].astype(F32)
        marks = piece[far + near : far + near + breadth]
        for row in range(WIDE):
            spots = pl.ds(row * breadth, breadth)
            state[first + row, pl.ds(STATE_AT, breadth), :] = lat_pieces[side, spots].astype(F32)
            value = jnp.where(spread(marks, row) > 0.5, 0.0, LAND)
            coded[first + row, pl.ds(FIELD_AT, breadth), :] = value
        for row in range(MARGIN):
            value = piece[far + row * breadth : far + (row + 1) * breadth]
            old = coded[closest + row, pl.ds(FIELD_AT, breadth), :]
            value = jnp.where(old > LAND_BOUND, LAND, value)
            coded[closest + row, pl.ds(FIELD_AT, breadth), :] = value

    group = WIDE + MARGIN

    def fill_columns(source, west):
        edges[...] = source[...].astype(F32)
        state_at = STATE_AT - WIDE if west else STATE_AT + breadth
        mark_at = FIELD_AT - NARROW if west else FIELD_AT + breadth
        value_at = FIELD_AT - MARGIN if west else FIELD_AT + breadth
        shown = slice(NARROW - MARGIN, NARROW) if west else slice(0, MARGIN)
        spans = [(own - pad, height, 0)] + [(starts[4 + side], WIDE, side + 1) for side in range(sides)]
        for first, count, place in spans:
            marks = edges[pl.ds(window_rows * group + place * 8, 8), :]
            for row in range(count):
                at = pad + first + row
                lines = (first + row) * group
                state[at, pl.ds(state_at, WIDE), :] = edges[pl.ds(lines, WIDE), :]
                mark = spread(marks, row)[:NARROW]
                coded[at, pl.ds(mark_at, NARROW), :] = jnp.where(mark > 0.5, 0.0, LAND)
                value = jnp.where(mark[shown] > 0.5, edges[pl.ds(lines + WIDE, MARGIN), :], LAND)
                coded[at, pl.ds(value_at, MARGIN), :] = value

    @pl.when(lower)
    def _():
        fill_columns(across, True)
        fill_columns(within, False)

    @pl.when(jnp.logical_not(lower))
    def _():
        fill_columns(within, True)
        fill_columns(across, False)


def tile_kernel(
    sizes,
    starts,
    state_tile,
    cotangent,
    land_sea,
    lat_pieces,
    within,
    across,
    dw_in,
    conv_bias,
    norm_gain,
    norm_bias,
    weight_in,
    bias_in,
    weight_out,
    bias_out,
    layer_scale,
    output,
    mixed_out,
    masked_out,
    edges_out,
    grads_out,
    state,
    coded,
    kernels,
    field,
    inner,
    result,
    normed_own,
    inverse_own,
    branch_own,
    slope_own,
    active_own,
    hidden_own,
    lifted_own,
    branch_grad_own,
    mixed_own,
    active_all,
    hidden_all,
    lifted_all,
    branch_grad_all,
    sums,
    hidden_sums,
    taps,
    edges,
    mixed_edges,
):
    height, breadth, first_rows, second_rows, window_rows = sizes
    channels = state.shape[2]
    own_start = starts[0]
    second_start = starts[1]
    first_start = starts[2]
    first_width = field.shape[1]
    second_width = inner.shape[1]
    pad = MARGIN

    for ref in (state, coded, field, inner):
        ref[pl.ds(0, pad)] = jnp.zeros((pad,) + ref.shape[1:], F32)
        below = ref.shape[0] - pad - window_rows
        ref[pl.ds(pad + window_rows, below)] = jnp.zeros((below,) + ref.shape[1:], F32)
    state[pl.ds(pad, window_rows)] = jnp.zeros((window_rows,) + state.shape[1:], F32)
    coded[pl.ds(pad, window_rows)] = jnp.zeros((window_rows,) + coded.shape[1:], F32)

    fill_windows(
        (height, breadth, window_rows),
        starts,
        (state_tile, cotangent, land_sea, lat_pieces, within, across),
        state,
        coded,
        edges,
    )
    kernels[...] = dw_in[...].astype(F32)
    sums[...] = jnp.zeros_like(sums)
    hidden_sums[...] = jnp.zeros_like(hidden_sums)

    def param(ref, layer):
        return ref[pl.ds(layer, 1), :]

    first_step = divisor(first_rows, FIRST_STEP)

    def forward_first(step, carry):
        row = first_start + step * first_step
        cells = first_step * first_width
        mixed = conv_rows(state, row, 0, first_step, first_width, kernels.at[0], False)
        normed, inverse = normalise(mixed + param(conv_bias, 0))
        lifted = (normed * param(norm_gain, 0) + param(norm_bias, 0)).astype(BF16)
        hidden = dot(lifted, weight_in[0]) + param(bias_in, 0)
        cumulative, bell = normal_parts(hidden)
        active = hidden * cumulative
        branch = dot(active.astype(BF16), weight_out[0]) + param(bias_out, 0)
        center = rows_of(state, row + pad, MARGIN, first_step, first_width)
        mark = rows_of(coded, row + pad, 0, first_step, first_width)
        value = jnp.where(mark < LAND_BOUND, center + param(layer_scale, 0) * branch, 0.0)
        value = value.reshape(first_step, first_width, channels)

        for index in range(first_step):
            field[row + pad + index] = value[index]

        def own(values):
            shape = (first_step, first_width, values.shape[1])
            return values.reshape(shape)[:, FIELD_AT : FIELD_AT + breadth]

        slope = own(cumulative) + own(hidden) * (own(bell) * INV_ROOT_TWO_PI)
        spots = pl.ds(row, first_step)
        slope_own[spots] = slope
        active_own[spots] = own(active).astype(BF16)
        normed_own[spots] = own(normed)
        inverse_own[spots] = own(jnp.broadcast_to(inverse, normed.shape))
        branch_own[spots] = own(branch)
        lifted_own[spots] = own(normed * param(norm_gain, 0) + param(norm_bias, 0)).astype(BF16)
        return carry

    lax.fori_loop(0, first_rows // first_step, forward_first, 0)

    second_step = divisor(second_rows, SECOND_STEP)

    def both_second(step, carry):
        row = second_start + step * second_step
        cells = second_step * second_width
        shift = FIELD_AT - INNER_AT
        mixed = conv_rows(
            field, row, shift - MARGIN, second_step, second_width, kernels.at[1], False
        )
        normed, inverse = normalise(mixed + param(conv_bias, 1))
        lifted = normed * param(norm_gain, 1) + param(norm_bias, 1)
        hidden = dot(lifted.astype(BF16), weight_in[1]) + param(bias_in, 1)
        cumulative, bell = normal_parts(hidden)
        active = (hidden * cumulative).astype(BF16)
        branch = dot(active, weight_out[1]) + param(bias_out, 1)
        center = rows_of(field, row + pad, shift, second_step, second_width)
        mark = rows_of(coded, row + pad, shift, second_step, second_width)
        ocean = mark < LAND_BOUND
        value = jnp.where(ocean, center + param(layer_scale, 1) * branch, 0.0)
        value = value.reshape(second_step, second_width, channels)
        masked = jnp.where(ocean, mark, 0.0)
        grad_branch = (masked * param(layer_scale, 1)).astype(BF16)
        grad_active = dot_cols(grad_branch, weight_out[1])
        slope = cumulative + hidden * (bell * INV_ROOT_TWO_PI)
        grad_hidden = (grad_active * slope).astype(BF16)
        grad_lifted = dot_cols(grad_hidden, weight_in[1])
        grad_mixed = normalise_back(grad_lifted * param(norm_gain, 1), normed, inverse)
        grad_mixed = grad_mixed.reshape(second_step, second_width, channels)
        for index in range(second_step):
            result[row + index] = value[index]
            inner[row + pad + index] = grad_mixed[index]

        shape = (second_step, second_width, channels)
        row_of = lax.broadcasted_iota(jnp.int32, shape, 0) + (row - own_start)
        col_of = lax.broadcasted_iota(jnp.int32, shape, 1) - INNER_AT
        inside = (row_of >= 0) & (row_of < height) & (col_of >= 0) & (col_of < breadth)
        inside = jnp.where(inside, 1.0, 0.0).astype(F32).reshape(cells, channels)
        own_lifted = grad_lifted * inside
        own_branch = grad_branch.astype(F32) * inside
        sums[1, 0] += fold(masked * branch * inside)
        sums[1, 1] += fold(own_branch)
        sums[1, 2] += fold(own_lifted * normed)
        sums[1, 3] += fold(own_lifted)
        spots = pl.ds(pl.multiple_of(step * cells, cells), cells)
        active_all[spots] = active
        hidden_all[spots] = grad_hidden
        lifted_all[spots] = jnp.concatenate([lifted * inside, inside], axis=1).astype(BF16)
        branch_grad_all[spots] = own_branch.astype(BF16)
        return carry

    lax.fori_loop(0, second_rows // second_step, both_second, 0)

    back_step = divisor(height, BACK_STEP)

    def backward_first(step, carry):
        row = own_start + step * back_step
        cells = back_step * breadth
        mark = rows_of(coded, row + pad, FIELD_AT, back_step, breadth)
        ocean = mark < LAND_BOUND
        masked_next = jnp.where(ocean, mark, 0.0)
        spread = conv_rows(inner, row, 0, back_step, breadth, kernels.at[1], True)
        masked = jnp.where(ocean, masked_next + spread, 0.0)
        grad_branch = (masked * param(layer_scale, 0)).astype(BF16)
        grad_active = dot_cols(grad_branch, weight_out[0])
        slope = slope_own[pl.ds(row, back_step)].reshape(cells, grad_active.shape[1])
        grad_hidden = (grad_active * slope).astype(BF16)
        grad_lifted = dot_cols(grad_hidden, weight_in[0])
        normed = normed_own[pl.ds(row, back_step)].reshape(cells, channels)
        inverse = inverse_own[pl.ds(row, back_step)].reshape(cells, channels)
        grad_mixed = normalise_back(grad_lifted * param(norm_gain, 0), normed, inverse)
        branch = branch_own[pl.ds(row, back_step)].reshape(cells, channels)
        sums[0, 0] += fold(masked * branch)
        sums[0, 1] += fold(grad_branch.astype(F32))
        sums[0, 2] += fold(grad_lifted * normed)
        sums[0, 3] += fold(grad_lifted)
        sums[0, 4] += fold(grad_mixed)
        hidden_sums[0] += fold(grad_hidden.astype(F32))
        inner_rows = rows_of(inner, row + pad, INNER_AT, back_step, breadth)
        sums[1, 4] += fold(inner_rows)
        tile = pl.ds(step * back_step, back_step)
        shape = (back_step, breadth, channels)
        grad_mixed = grad_mixed.reshape(shape)
        mixed_own[tile] = grad_mixed
        mixed_out[tile] = grad_mixed.astype(BF16)
        masked_out[tile] = masked.reshape(shape).astype(BF16)
        hidden_own[tile] = grad_hidden.reshape(back_step, breadth, grad_hidden.shape[1])
        branch_grad_own[tile] = grad_branch.reshape(shape)
        value = rows_of(result, row, INNER_AT, back_step, breadth)
        output[tile] = value.reshape(shape).astype(BF16)
        return carry

    lax.fori_loop(0, height // back_step, backward_first, 0)

    mixed_edges[...] = jnp.zeros_like(mixed_edges)
    lower = starts[3] == 0
    for row in range(height):
        first = mixed_own[row, pl.ds(0, MARGIN), :]
        last = mixed_own[row, pl.ds(breadth - MARGIN, MARGIN), :]
        spots = pl.ds(row * MARGIN, MARGIN)
        mixed_edges[0, spots] = jnp.where(lower, last, first)
        mixed_edges[1, spots] = jnp.where(lower, first, last)
    edges_out[...] = mixed_edges[...].astype(BF16)

    hidden_units = weight_in.shape[2]
    groups = hidden_units // channels
    tile = pl.ds(own_start, height)
    cells = height * breadth

    def flat(ref, spots):
        return ref[spots].reshape(cells, ref.shape[2])

    operands = (
        (
            flat(lifted_own, tile),
            flat(hidden_own, pl.ds(0, height)),
            flat(active_own, tile),
            flat(branch_grad_own, pl.ds(0, height)),
        ),
        (lifted_all[...], hidden_all[...], active_all[...], branch_grad_all[...]),
    )
    for layer, (lifted, grad_hidden, active, grad_branch) in enumerate(operands):
        at = layer * (grads_out.shape[0] // BLOCKS)
        grad_in = dot_rows(lifted, grad_hidden)
        if layer:
            hidden_sums[1, 0:1] = grad_in[channels : channels + 1]
            grad_in = grad_in[:channels]
        for group in range(groups):
            grads_out[pl.ds(at + group * channels, channels), :] = grad_in[
                :, group * channels : (group + 1) * channels
            ].astype(BF16)
        grad_out = dot_rows(grad_branch, active)
        for group in range(groups):
            grads_out[pl.ds(at + hidden_units + group * channels, channels), :] = grad_out[
                :, group * channels : (group + 1) * channels
            ].T.astype(BF16)

    taps[...] = jnp.zeros_like(taps)
    for layer in range(BLOCKS):
        base = layer * (taps.shape[0] // BLOCKS)
        if layer:
            tap_sums(
                inner,
                own_start + pad,
                INNER_AT,
                field,
                own_start,
                FIELD_AT - MARGIN,
                height,
                breadth,
                taps.at[pl.ds(base, TAPS)],
            )
        else:
            tap_sums(
                mixed_own,
                0,
                0,
                state,
                own_start,
                STATE_AT - MARGIN,
                height,
                breadth,
                taps.at[pl.ds(base, TAPS)],
            )
        for member in range(5):
            taps[pl.ds(base + TAPS + member, 1), :] = jnp.sum(
                sums[layer, member], axis=0, keepdims=True
            )
        hidden_total = jnp.sum(hidden_sums[layer], axis=0, keepdims=True)
        for group in range(groups):
            taps[pl.ds(base + TAPS + 5 + group, 1), :] = hidden_total[
                :, group * channels : (group + 1) * channels
            ]
    small = taps.shape[0] // BLOCKS
    for layer in range(BLOCKS):
        at = layer * (grads_out.shape[0] // BLOCKS) + 2 * hidden_units
        grads_out[pl.ds(at, small), :] = taps[pl.ds(layer * small, small), :].astype(BF16)


def state_kernel(starts, mixed, within, across, lat_pieces, masked, dw_in, out, wide, kernels, edges):
    height, breadth, channels = masked.shape
    wide[...] = jnp.zeros_like(wide)
    kernels[...] = dw_in[...].astype(F32)
    wide[pl.ds(MARGIN, height), pl.ds(MARGIN, breadth), :] = mixed[...].astype(F32)
    sides = lat_pieces.shape[0]
    inner = MARGIN * breadth
    beside = MARGIN * MARGIN
    for side in range(sides):
        first = starts[1 + side]
        piece = lat_pieces[side].astype(F32)
        for row in range(MARGIN):
            spots = slice(row * breadth, (row + 1) * breadth)
            wide[first + row, pl.ds(MARGIN, breadth), :] = piece[spots]

    def fill_columns(source, place, west):
        column = 0 if west else MARGIN + breadth
        edges[...] = source[...].astype(F32)
        for row in range(height):
            wide[MARGIN + row, pl.ds(column, MARGIN), :] = edges[pl.ds(row * MARGIN, MARGIN), :]
        for side in range(sides):
            piece = lat_pieces[side].astype(F32)
            for row in range(MARGIN):
                at = inner + place * beside + row * MARGIN
                wide[starts[1 + side] + row, pl.ds(column, MARGIN), :] = piece[at : at + MARGIN]

    @pl.when(starts[0] == 0)
    def _():
        fill_columns(within, 0, False)
        fill_columns(across, 1, True)

    @pl.when(starts[0] != 0)
    def _():
        fill_columns(within, 0, True)
        fill_columns(across, 1, False)

    rows = divisor(height, BACK_STEP)

    def advance(step, carry):
        row = step * rows
        spread = conv_rows(wide, row, 0, rows, breadth, kernels, True)
        tile = pl.ds(row, rows)
        shape = (rows, breadth, channels)
        out[tile] = (masked[tile].astype(F32) + spread.reshape(shape)).astype(BF16)
        return carry

    lax.fori_loop(0, height // rows, advance, 0)


def gradient_kernel(grad_norm, held, own, other, *outs):
    kernel, conv_bias, gain, shift, first, first_bias, second, second_bias, scale = outs
    channels = own.shape[1]
    units = second.shape[1]
    groups = units // channels

    def unpack(rows, layer):
        for group in range(groups):
            spots = pl.ds(group * channels, channels)
            first[layer, :, spots] = rows[spots].astype(F32) * grad_norm
        second[layer] = rows[pl.ds(units, units)].astype(F32) * grad_norm
        small = rows[pl.ds(2 * units, rows.shape[0] - 2 * units)].astype(F32) * grad_norm
        for index in range(TAPS):
            kernel[index // KSIZE, index % KSIZE, layer : layer + 1] = small[index : index + 1]
        for member, out in enumerate((scale, second_bias, gain, shift, conv_bias)):
            out[layer : layer + 1] = small[TAPS + member : TAPS + member + 1]
        for group in range(groups):
            row = TAPS + 5 + group
            first_bias[layer : layer + 1, pl.ds(group * channels, channels)] = small[row : row + 1]

    @pl.when(held[0] == 0)
    def _():
        unpack(own, 0)
        unpack(other, 1)

    @pl.when(held[0] != 0)
    def _():
        unpack(own, 1)
        unpack(other, 0)


class Links:
    def __init__(self, mesh):
        self.lon = mesh.shape["lon"]
        self.lat = mesh.shape["lat"]
        self.axes = ("lon", "lat")

    def lon_neighbours(self, within, across):
        there = [place + 1 if place % 2 else place - 1 for place in range(self.lon)]
        pairs = [(place, other % self.lon) for place, other in enumerate(there)]
        across = lax.ppermute(across, "lon", pairs)
        return self.swap(within, 1, 0), across

    def shift_lat(self, values, by):
        pairs = [
            (place, place + by) for place in range(self.lat) if 0 <= place + by < self.lat
        ]
        return lax.ppermute(values, "lat", pairs)

    def lat_neighbours(self, last, first):
        if self.lat == 2:
            return self.swap(last, 0, 1)[None]
        return jnp.stack([self.shift_lat(last, 1), self.shift_lat(first, -1)])

    def swap(self, values, lon_bits, lat_bits):
        pairs = []
        for lon in range(self.lon):
            for lat in range(self.lat):
                there = (lon ^ lon_bits) * self.lat + (lat ^ lat_bits)
                pairs.append((lon * self.lat + lat, there))
        return lax.ppermute(values, self.axes, pairs)

    def sum_all(self, rows, edges, finish):
        lon = lax.axis_index("lon")
        lat = lax.axis_index("lat")
        bits = [(1 << bit, 0) for bit in range(self.lon.bit_length() - 1)]
        bits = bits[:1] + [(0, 1 << bit) for bit in range(self.lat.bit_length() - 1)] + bits[1:]

        def code(group):
            total = jnp.int32(0)
            for index, (lon_bit, lat_bit) in enumerate(group):
                held = (lon // lon_bit) % 2 if lon_bit else (lat // lat_bit) % 2
                total = total + held * (1 << index)
            return total

        def merged(group, choice):
            lon_bits = sum(bit[0] for index, bit in enumerate(group) if choice >> index & 1)
            lat_bits = sum(bit[1] for index, bit in enumerate(group) if choice >> index & 1)
            return lon_bits, lat_bits

        def scatter(values, group):
            count = 1 << len(group)
            pieces = values.reshape(count, -1, values.shape[1])
            here = code(group)
            total = lax.dynamic_index_in_dim(pieces, here, 0, False).astype(F32)
            arrived = []
            for choice in range(1, count):
                sent = lax.dynamic_index_in_dim(pieces, here ^ choice, 0, False)
                arrived.append(self.swap(sent, *merged(group, choice)))
            return total, arrived

        def summed(total, arrived):
            for values in arrived:
                total = total + values.astype(F32)
            return total.astype(BF16)

        def exchange(values, group):
            total = values.astype(F32)
            for choice in range(1, 1 << len(group)):
                total = total + self.swap(values, *merged(group, choice)).astype(F32)
            return total.astype(BF16)

        def gather(values, group):
            count = 1 << len(group)
            pieces = [values]
            for choice in range(1, count):
                pieces.append(self.swap(values, *merged(group, choice)))
            stack = jnp.stack(pieces)
            here = code(group)
            ordered = [
                lax.dynamic_index_in_dim(stack, here ^ place, 0, False) for place in range(count)
            ]
            return jnp.concatenate(ordered, axis=0)

        pair, quad, rest = bits[:1], bits[1:3], bits[3:]
        values = summed(*scatter(rows, pair))
        total, arrived = scatter(values, quad)
        arrived[0], edges = lax.optimization_barrier((arrived[0], edges))
        beside = finish(edges)
        values = summed(total, arrived)
        while rest:
            values = exchange(values, rest[:2])
            rest = rest[2:]
        values = gather(values, quad)
        values, beside = lax.optimization_barrier((values, beside))
        return code(pair), values, self.swap(values, *pair[0]), beside


def on_device(links, state, land_sea, cotangent, *params):
    dw_kernel, weight_in = params[0], params[4]
    height, breadth, channels = state.shape
    hidden_units = weight_in.shape[2]
    groups = hidden_units // channels
    grad_norm = 1.0 / math.sqrt(links.lat * height * links.lon * breadth)
    lat = lax.axis_index("lat")
    sides = 1 if links.lat == 2 else 2
    window_rows = height + sides * WIDE
    first_rows = height + sides * NARROW
    second_rows = height + sides * MARGIN

    def start(margin):
        skipped = WIDE - margin
        return lat * skipped if sides == 1 else jnp.int32(skipped)

    core = lax.axis_index("lon") % 2
    vmem = pl.BlockSpec(memory_space=pltpu.VMEM)
    smem = pl.BlockSpec(memory_space=pltpu.SMEM)
    tile = (height, breadth, channels)

    def flat(values):
        return values.reshape(-1, channels)

    def whole_rows(values, rows):
        return jnp.pad(values, ((0, rows - values.shape[0]), (0, channels - values.shape[1])))

    land = land_sea.T
    marks = (land != 0).astype(BF16)

    packed_rows = round_up((WIDE + MARGIN + 1) * breadth, 16)
    packed = (sides, packed_rows, channels)
    packed = pl.pallas_call(
        pack_kernel,
        out_shape=jax.ShapeDtypeStruct(packed, BF16),
        in_specs=[smem] + [pl.BlockSpec(memory_space=pl.ANY)] * 3,
        out_specs=vmem,
        scratch_shapes=[
            pltpu.VMEM(packed, F32),
            pltpu.VMEM((sides, WIDE, breadth, channels), BF16),
            pltpu.VMEM((sides, MARGIN, breadth, channels), BF16),
            pltpu.VMEM((breadth, height), jnp.int32),
            pltpu.SemaphoreType.DMA((1 + 2 * sides,)),
        ],
        compiler_params=pltpu.CompilerParams(vmem_limit_bytes=PACK_LIMIT),
    )(lat.reshape(1), state, cotangent, land)
    pieces = links.lat_neighbours(packed[0], packed[-1])
    far, near = WIDE * breadth, MARGIN * breadth
    piece_states = pieces[:, :far].reshape(sides, WIDE, breadth, channels)
    piece_cotangents = pieces[:, far : far + near].reshape(sides, MARGIN, breadth, channels)
    piece_marks = pieces[:, far + near : far + near + breadth]

    def lon_columns(wide, narrow, margin):
        own = jnp.concatenate([state[:, wide], cotangent[:, margin]], axis=1)

        def ends(side, above):
            empty = ((NARROW, 0) if above else (0, NARROW), (0, 0), (0, 0))
            near_rows = jnp.pad(piece_cotangents[side][:, margin], empty)
            return jnp.concatenate([piece_states[side][:, wide], near_rows], axis=1)

        if sides == 1:
            rows = jnp.where(
                lat == 0,
                jnp.concatenate([own, ends(0, False)]),
                jnp.concatenate([ends(0, True), own]),
            )
        else:
            rows = jnp.concatenate([ends(0, True), own, ends(1, False)])
        kept = [whole_rows(marks[narrow], 8)]
        kept += [jnp.pad(piece_marks[side][narrow], ((0, 8 - NARROW), (0, 0))) for side in range(sides)]
        return jnp.concatenate([flat(rows), *kept])

    first_columns = lon_columns(slice(0, WIDE), slice(0, NARROW), slice(0, MARGIN))
    last_columns = lon_columns(
        slice(breadth - WIDE, breadth),
        slice(breadth - NARROW, breadth),
        slice(breadth - MARGIN, breadth),
    )
    within, across = links.lon_neighbours(
        jnp.where(core == 0, last_columns, first_columns),
        jnp.where(core == 0, first_columns, last_columns),
    )
    if sides == 1:
        places = [(1 - lat) * height]
        closest = [jnp.where(lat == 0, height, WIDE - MARGIN)]
    else:
        places = [0, WIDE + height]
        closest = [WIDE - MARGIN, WIDE + height]
    starts = [start(0), start(MARGIN), start(NARROW), core, *places, *closest]
    starts = jnp.stack([jnp.asarray(entry, jnp.int32) for entry in starts])
    state_pitch, field_pitch, inner_pitch = (
        round_up(breadth + size, 8) for size in (STATE_AT + WIDE, FIELD_AT + NARROW, NARROW)
    )

    padded_rows = window_rows + 2 * MARGIN + 1
    all_cells = second_rows * inner_pitch
    layer_rows = round_up(2 * hidden_units + TAPS + 5 + groups, 4 * 16)
    small_rows = BLOCKS * (layer_rows - 2 * hidden_units)
    grad_rows = BLOCKS * layer_rows
    own_rows = (window_rows, breadth)
    edge_rows = round_up(height * MARGIN, 8)
    scratch = [
        pltpu.VMEM((padded_rows, state_pitch, channels), F32),
        pltpu.VMEM((padded_rows, field_pitch, channels), F32),
        pltpu.VMEM((BLOCKS, TAPS, channels), F32),
        pltpu.VMEM((padded_rows, field_pitch, channels), F32),
        pltpu.VMEM((padded_rows, inner_pitch, channels), F32),
        pltpu.VMEM((window_rows, inner_pitch, channels), F32),
        pltpu.VMEM(own_rows + (channels,), F32),
        pltpu.VMEM(own_rows + (channels,), F32),
        pltpu.VMEM(own_rows + (channels,), F32),
        pltpu.VMEM(own_rows + (hidden_units,), F32),
        pltpu.VMEM(own_rows + (hidden_units,), BF16),
        pltpu.VMEM((height, breadth, hidden_units), BF16),
        pltpu.VMEM(own_rows + (channels,), BF16),
        pltpu.VMEM(tile, BF16),
        pltpu.VMEM(tile, F32),
        pltpu.VMEM((all_cells, hidden_units), BF16),
        pltpu.VMEM((all_cells, hidden_units), BF16),
        pltpu.VMEM((all_cells, 2 * channels), BF16),
        pltpu.VMEM((all_cells, channels), BF16),
        pltpu.VMEM((BLOCKS, 5, 8, channels), F32),
        pltpu.VMEM((BLOCKS, 8, hidden_units), F32),
        pltpu.VMEM((small_rows, channels), F32),
        pltpu.VMEM(within.shape, F32),
        pltpu.VMEM((2, edge_rows, channels), F32),
    ]
    sizes = (height, breadth, first_rows, second_rows, window_rows)
    taps_in = dw_kernel.reshape(BLOCKS, TAPS, channels)
    output, grad_mixed, masked, mixed_edges, grads = pl.pallas_call(
        functools.partial(tile_kernel, sizes),
        out_shape=(
            jax.ShapeDtypeStruct(tile, BF16),
            jax.ShapeDtypeStruct(tile, BF16),
            jax.ShapeDtypeStruct(tile, BF16),
            jax.ShapeDtypeStruct((2, edge_rows, channels), BF16),
            jax.ShapeDtypeStruct((grad_rows, channels), BF16),
        ),
        in_specs=[smem] + [vmem] * 15,
        out_specs=(vmem,) * 5,
        scratch_shapes=scratch,
        compiler_params=pltpu.CompilerParams(vmem_limit_bytes=VMEM_LIMIT),
        cost_estimate=pl.CostEstimate(
            flops=20 * all_cells * channels * hidden_units,
            bytes_accessed=4 * height * breadth * channels * 4,
            transcendentals=0,
        ),
    )(starts, state, cotangent, land, pieces, within, across, taps_in, *params[1:])

    def finish(mixed_edges):
        within, across = links.lon_neighbours(mixed_edges[0], mixed_edges[1])
        corner = MARGIN * MARGIN

        def corner_rows(rows, first):
            beside = slice(first * MARGIN, first * MARGIN + corner)
            parts = jnp.concatenate([flat(grad_mixed[rows]), within[beside], across[beside]])
            return jnp.pad(parts, ((0, -parts.shape[0] % 16), (0, 0)))

        last = corner_rows(slice(height - MARGIN, height), height - MARGIN)
        first = corner_rows(slice(0, MARGIN), 0)
        if sides == 1:
            last = first = jnp.where(lat == 0, last, first)
        pieces = links.lat_neighbours(last, first)
        if sides == 1:
            places = [(1 - lat) * (MARGIN + height)]
        else:
            places = [0, MARGIN + height]
        starts = jnp.stack([jnp.asarray(entry, jnp.int32) for entry in (core, *places)])
        wide = (height + 2 * MARGIN + 1, round_up(breadth + 2 * MARGIN, 8), channels)
        return pl.pallas_call(
            state_kernel,
            out_shape=jax.ShapeDtypeStruct(tile, BF16),
            in_specs=[smem] + [vmem] * 6,
            out_specs=vmem,
            scratch_shapes=[
                pltpu.VMEM(wide, F32),
                pltpu.VMEM((TAPS, channels), F32),
                pltpu.VMEM((edge_rows, channels), F32),
            ],
            compiler_params=pltpu.CompilerParams(vmem_limit_bytes=16 * 1024 * 1024),
            cost_estimate=pl.CostEstimate(
                flops=4_000_000_000, bytes_accessed=8_000_000, transcendentals=0
            ),
        )(starts, grad_mixed, within, across, pieces, masked, taps_in[0])

    held, own, other, grad_state = links.sum_all(grads, mixed_edges, finish)
    shapes = [(KSIZE, KSIZE, BLOCKS, channels)] + [member.shape for member in params[1:]]
    grad_kernel, *gradients = pl.pallas_call(
        functools.partial(gradient_kernel, grad_norm),
        out_shape=tuple(jax.ShapeDtypeStruct(shape, F32) for shape in shapes),
        in_specs=[smem, vmem, vmem],
        out_specs=(vmem,) * 9,
        compiler_params=pltpu.CompilerParams(vmem_limit_bytes=8 * 1024 * 1024),
    )(held.reshape(1), own, other)
    return (output, grad_state, grad_kernel.transpose(2, 0, 1, 3), *gradients)


def solution(mesh):
    tile = P("lat", "lon", None)
    placed = (tile, P("lat", "lon"), tile) + (P(),) * 9
    return jax.shard_map(
        functools.partial(on_device, Links(mesh)),
        mesh=mesh,
        in_specs=placed,
        out_specs=(tile, tile) + (P(),) * 9,
        check_vma=False,
    )
```
